256 devices in a mesh: tm: 16 (over z_hi, y, core), tile: 16 (over z_lo, x).
Axes of the slice: x: 4, y: 4, z: 8 (z_hi: 2, z_lo: 4; z = z_hi * 4 + z_lo), core: 2. Of those that a mesh axis runs over, the one named last changes fastest.
Arguments:
- clip_tokens: bfloat16 [128, 16, 7, 7, 128], P('tm', 'tile'), may hold values from -6 to 6
- target: bfloat16 [128, 16, 7, 7, 128], P('tm', 'tile'), may hold values from -6 to 6
- norm1_gain: float32 [128], replicated, may hold values from 0.1 to 1.9
- norm1_bias: float32 [128], replicated, may hold values from -3 to 3
- qkv_weight: bfloat16 [128, 384], replicated, may hold values from -0.5 to 0.5
- qkv_bias: float32 [384], replicated, may hold values from -3 to 3
- bias_table: float32 [2535, 4], replicated, may hold values from -250 to 250
- proj_weight: bfloat16 [128, 128], replicated, may hold values from -0.5 to 0.5
- proj_bias: float32 [128], replicated, may hold values from -3 to 3
- norm2_gain: float32 [128], replicated, may hold values from 0.1 to 1.9
- norm2_bias: float32 [128], replicated, may hold values from -3 to 3
- fc1_weight: bfloat16 [128, 512], replicated, may hold values from -0.5 to 0.5
- fc1_bias: float32 [512], replicated, may hold values from -3 to 3
- fc2_weight: bfloat16 [512, 128], replicated, may hold values from -0.25 to 0.25
- fc2_bias: float32 [128], replicated, may hold values from -3 to 3
Outputs:
- grad_clip: bfloat16 [128, 16, 7, 7, 128], P('tm', 'tile')
The draws below stay inside these ranges and needn't reach their ends.
All inputs are finite; a program needn't handle non-finite values.
Results may differ from the reference program's by a relative error of at most 0.0085.
Values may be sent and summed in bfloat16 or wider, within the bound.
A program may use at most 192 MiB of HBM per device.

```python
import jax
import jax.numpy as jnp
import numpy as np
from jax import lax

C = 128
HEADS = 4
FF = 512
WT = 8
WH = 7
WW = 7
ST = 4
SH = 3
SW = 3
TCOLS = 4
H_DEV = 7
W_DEV = 7
NT = 128
N_TILE = 16


def draw_bias_table(key, part):
    key = jax.random.fold_in(key, 11)
    key_base = jax.random.fold_in(key, 0)
    rows_count = (2 * WT - 1) * (2 * WH - 1) * (2 * WW - 1)
    bias_values = jnp.clip(jax.random.normal(key_base, (rows_count, HEADS), jnp.float32), -4.0, 4.0)
    return bias_values.astype(jnp.float32)


def steps_of(key, dims, cuts, smallest, top_value):
    level = 1.0
    for position, shards_of in cuts:
        heights = jax.random.uniform(jax.random.fold_in(jax.random.fold_in(key, 6), position), (shards_of,), jnp.float32, smallest / len(cuts), top_value / len(cuts))
        level = level * jnp.repeat(jnp.exp(heights), dims[position] // shards_of).reshape((-1,) + (1,) * (len(dims) - 1 - position))
    return level


def scatter_about(key, dims, scale, limit, shards=(), kind=jnp.bfloat16):
    gain = steps_of(key, dims, shards, -0.22, 0.18) if shards else 1.0
    values = jax.random.normal(key, dims, jnp.float32) * scale * gain
    return jnp.minimum(jnp.maximum(values, -limit), limit).astype(kind)


def setup_inputs(seed: int = 0) -> dict:
    arg_keys = jax.random.split(jax.random.key(seed), 16)
    clip_tokens = scatter_about(arg_keys[0], (NT, N_TILE, H_DEV, W_DEV, C), 1.0, 6.0, ((0, 16), (1, 16)))
    target = scatter_about(arg_keys[1], (NT, N_TILE, H_DEV, W_DEV, C), 1.0, 6.0, ((0, 16), (1, 16)))
    norm1_gain = jnp.clip(1.0 + 0.18 * jax.random.normal(arg_keys[2], (C,), jnp.float32), 0.1, 1.9)
    norm1_bias = scatter_about(arg_keys[3], (C,), 0.5, 3.0, (), jnp.float32)
    qkv_weight = scatter_about(arg_keys[4], (C, 3 * C), C ** -0.5, 0.5)
    qkv_bias = scatter_about(arg_keys[5], (3 * C,), 0.5, 3.0, (), jnp.float32)
    bias_table = draw_bias_table(jax.random.fold_in(arg_keys[15], 71), 0)
    proj_weight = scatter_about(arg_keys[7], (C, C), C ** -0.5, 0.5)
    proj_bias = scatter_about(arg_keys[8], (C,), 0.5, 3.0, (), jnp.float32)
    norm2_gain = jnp.clip(1.0 + 0.18 * jax.random.normal(arg_keys[9], (C,), jnp.float32), 0.1, 1.9)
    norm2_bias = scatter_about(arg_keys[10], (C,), 0.5, 3.0, (), jnp.float32)
    fc1_weight = scatter_about(arg_keys[11], (C, FF), C ** -0.5, 0.5)
    fc1_bias = scatter_about(arg_keys[12], (FF,), 0.5, 3.0, (), jnp.float32)
    fc2_weight = scatter_about(arg_keys[13], (FF, C), FF ** -0.5, 0.25)
    fc2_bias = scatter_about(arg_keys[14], (C,), 0.5, 3.0, (), jnp.float32)
    return {"clip_tokens": clip_tokens, "target": target, "norm1_gain": norm1_gain, "norm1_bias": norm1_bias, "qkv_weight": qkv_weight, "qkv_bias": qkv_bias, "bias_table": bias_table, "proj_weight": proj_weight, "proj_bias": proj_bias, "norm2_gain": norm2_gain, "norm2_bias": norm2_bias, "fc1_weight": fc1_weight, "fc1_bias": fc1_bias, "fc2_weight": fc2_weight, "fc2_bias": fc2_bias}


EPSILON = 1e-05
MASKED = -1000000000.0
ROOT_HALF = 0.7071067811865476
INV_ROOT_TAU = 0.3989422804014327

def widen(tensor):
    return lax.optimization_barrier(tensor).astype(jnp.float32)

def norm_forward(values, norm_gain, norm_bias):
    center = values - lax.optimization_barrier(jnp.mean(values, -1, keepdims=True))
    inv_std = lax.rsqrt(lax.optimization_barrier(jnp.mean(center * center, -1, keepdims=True)) + EPSILON)
    normal = center * inv_std
    return (normal, inv_std, normal * norm_gain + norm_bias)

def norm_backward(grad_out, normal, inv_std, norm_gain):
    scaled = grad_out * norm_gain
    return inv_std * (scaled - lax.optimization_barrier(jnp.mean(scaled, -1, keepdims=True)) - normal * lax.optimization_barrier(jnp.mean(scaled * normal, -1, keepdims=True)))

def gelu_exact(values):
    return values * 0.5 * (1.0 + jax.scipy.special.erf(values * ROOT_HALF))

def gelu_slope(values):
    return 0.5 * (1.0 + jax.scipy.special.erf(values * ROOT_HALF)) + values * INV_ROOT_TAU * jnp.exp(-0.5 * values * values)

def to_frame(tokens):
    time_len, tile_count, row_len, col_len, chan_len = tokens.shape
    tile_rows = tile_count // TCOLS
    grid = tokens.reshape(time_len, tile_rows, TCOLS, row_len, col_len, chan_len)
    return grid.transpose(0, 1, 3, 2, 4, 5).reshape(time_len, tile_rows * row_len, TCOLS * col_len, chan_len)

def from_frame(frames, row_len, col_len):
    time_len, full_rows, full_cols, chan_len = frames.shape
    tile_rows = full_rows // row_len
    grid = frames.reshape(time_len, tile_rows, row_len, TCOLS, col_len, chan_len)
    return grid.transpose(0, 1, 3, 2, 4, 5).reshape(time_len, tile_rows * TCOLS, row_len, col_len, chan_len)

def split_windows(volume):
    time_len, row_len, col_len, chan_len = volume.shape
    blocks = volume.reshape(time_len // WT, WT, row_len // WH, WH, col_len // WW, WW, chan_len)
    return blocks.transpose(0, 2, 4, 1, 3, 5, 6).reshape(-1, WT * WH * WW, chan_len)

def join_windows(windows, time_len, row_len, col_len):
    chan_len = windows.shape[-1]
    blocks = windows.reshape(time_len // WT, row_len // WH, col_len // WW, WT, WH, WW, chan_len)
    return blocks.transpose(0, 3, 1, 4, 2, 5, 6).reshape(time_len, row_len, col_len, chan_len)

def region_code(coords, extent, window, shift_len):
    return jnp.where(coords < extent - window, 0, jnp.where(coords < extent - shift_len, 1, 2)).astype(jnp.int32)

def window_labels(time_pos, row_pos, col_pos, totals):
    grid_codes = region_code(time_pos, totals[0], WT, ST)[:, None, None] * 9 + region_code(row_pos, totals[1], WH, SH)[None, :, None] * 3 + region_code(col_pos, totals[2], WW, SW)[None, None, :]
    return split_windows(grid_codes[..., None])[..., 0]

def expand_bias(bias_table):
    coords = np.stack(np.meshgrid(np.arange(WT), np.arange(WH), np.arange(WW), indexing='ij')).reshape(3, -1)
    offsets = coords[:, :, None] - coords[:, None, :]
    flat_index = (offsets[0] + WT - 1) * ((2 * WH - 1) * (2 * WW - 1)) + (offsets[1] + WH - 1) * (2 * WW - 1) + offsets[2] + WW - 1
    window_size = WT * WH * WW
    by_head = jnp.transpose(bias_table)
    spread = jnp.take(by_head, jnp.asarray(flat_index.reshape(-1), dtype=jnp.int32), axis=1)
    return spread.reshape(-1, window_size, window_size)

def project_qkv(windows, qkv_weight, qkv_bias):
    win_count, win_len, chan_len = windows.shape
    head_size = chan_len // HEADS
    projected = jnp.dot(windows.reshape(-1, chan_len), qkv_weight, preferred_element_type=jnp.float32) + qkv_bias
    shape_heads = (win_count, win_len, HEADS, head_size)
    queries = (projected[:, :chan_len] * head_size ** (-0.5)).astype(jnp.bfloat16).reshape(shape_heads)
    keys_low = projected[:, chan_len:2 * chan_len].astype(jnp.bfloat16).reshape(shape_heads)
    values_low = projected[:, 2 * chan_len:].astype(jnp.bfloat16).reshape(shape_heads)
    return (queries, keys_low, values_low)

def attend(queries, keys_low, bias_full, allowed):
    scores = jnp.einsum('bihd,bjhd->bhij', widen(queries), widen(keys_low)) + bias_full[None]
    scores = jnp.where(allowed[:, None], scores, MASKED)
    row_max = lax.optimization_barrier(jnp.max(scores, -1, keepdims=True))
    exponent = jnp.exp(scores - row_max)
    return exponent / lax.optimization_barrier(jnp.sum(exponent, -1, keepdims=True))

def window_forward(windows, labels, weights, bias_full):
    qkv_weight, qkv_bias, proj_weight, proj_bias = weights
    win_count, win_len, chan_len = windows.shape
    allowed = labels[:, :, None] == labels[:, None, :]
    queries, keys_low, values_low = project_qkv(windows, qkv_weight, qkv_bias)
    attn_probs = attend(queries, keys_low, bias_full, allowed)
    mixed_heads = jnp.einsum('bhij,bjhd->bihd', widen(attn_probs.astype(jnp.bfloat16)), widen(values_low)).astype(jnp.bfloat16)
    branch = jnp.dot(mixed_heads.reshape(-1, chan_len), proj_weight, preferred_element_type=jnp.float32) + proj_bias
    return branch.astype(jnp.bfloat16).reshape(win_count, win_len, chan_len)

def window_backward(windows, labels, grad_branch, weights, bias_full):
    qkv_weight, qkv_bias, proj_weight, proj_bias = weights
    win_count, win_len, chan_len = windows.shape
    head_size = chan_len // HEADS
    allowed = labels[:, :, None] == labels[:, None, :]
    queries, keys_low, values_low = project_qkv(windows, qkv_weight, qkv_bias)
    attn_probs = attend(queries, keys_low, bias_full, allowed)
    probs_low = attn_probs.astype(jnp.bfloat16)
    grad_mixed = jnp.dot(grad_branch.reshape(-1, chan_len), proj_weight.T, preferred_element_type=jnp.float32)
    grad_mixed = grad_mixed.astype(jnp.bfloat16).reshape(win_count, win_len, HEADS, head_size)
    grad_values = jnp.einsum('bhij,bihd->bjhd', widen(probs_low), widen(grad_mixed))
    grad_probs = jnp.einsum('bihd,bjhd->bhij', widen(grad_mixed), widen(values_low))
    delta_rows = lax.optimization_barrier(jnp.sum(grad_probs * attn_probs, -1, keepdims=True))
    grad_scores = (attn_probs * (grad_probs - delta_rows)).astype(jnp.bfloat16)
    grad_queries = jnp.einsum('bhij,bjhd->bihd', widen(grad_scores), widen(keys_low)) * head_size ** (-0.5)
    grad_keys = jnp.einsum('bhij,bihd->bjhd', widen(grad_scores), widen(queries))
    grad_qkv = jnp.concatenate([grad_queries.reshape(-1, chan_len), grad_keys.reshape(-1, chan_len), grad_values.reshape(-1, chan_len)], axis=1).astype(jnp.bfloat16)
    grad_normed = jnp.dot(grad_qkv, qkv_weight.T, preferred_element_type=jnp.float32).astype(jnp.bfloat16)
    return grad_normed.reshape(win_count, win_len, chan_len)

def over_windows(step_fn, volumes, labels, group_size):
    time_len, row_len, col_len, chan_len = volumes[0].shape
    win_len = WT * WH * WW
    pieces = tuple((split_windows(volume).reshape(-1, group_size, win_len, chan_len) for volume in volumes))
    label_groups = labels.reshape(-1, group_size, win_len)
    results = lax.map(step_fn, (pieces, label_groups))
    return join_windows(results.reshape(-1, win_len, chan_len), time_len, row_len, col_len)

def mlp_gradient(ys, goal_rows, mlp_params):
    norm2_gain, norm2_bias, fc1_weight, fc1_bias, fc2_weight, fc2_bias = mlp_params
    normal2, inv_std2, affine2 = norm_forward(ys, norm2_gain, norm2_bias)
    normed2 = affine2.astype(jnp.bfloat16)
    pre_act = jnp.dot(normed2, fc1_weight, preferred_element_type=jnp.float32) + fc1_bias
    hidden = gelu_exact(pre_act).astype(jnp.bfloat16)
    outputs = ys + jnp.dot(hidden, fc2_weight, preferred_element_type=jnp.float32) + fc2_bias
    grad_out = outputs - goal_rows.astype(jnp.float32)
    grad_low = grad_out.astype(jnp.bfloat16)
    grad_hidden = jnp.dot(grad_low, fc2_weight.T, preferred_element_type=jnp.float32)
    grad_pre = (grad_hidden * gelu_slope(pre_act)).astype(jnp.bfloat16)
    grad_norm2 = jnp.dot(grad_pre, fc1_weight.T, preferred_element_type=jnp.float32)
    return grad_out + norm_backward(grad_norm2, normal2, inv_std2, norm2_gain)

def reference(clip_tokens, target, norm1_gain, norm1_bias, qkv_weight, qkv_bias, bias_table, proj_weight, proj_bias, norm2_gain, norm2_bias, fc1_weight, fc1_bias, fc2_weight, fc2_bias):
    frames = to_frame(clip_tokens)
    goal_frames = to_frame(target)
    time_len, row_len, col_len, chan_len = frames.shape
    inputs = frames.astype(jnp.float32)
    normal1, inv_std1, affine1 = norm_forward(inputs, norm1_gain, norm1_bias)
    normed1 = affine1.astype(jnp.bfloat16)
    rolled = jnp.roll(normed1, (-ST, -SH, -SW), (0, 1, 2))
    labels = window_labels(jnp.arange(time_len, dtype=jnp.int32), jnp.arange(row_len, dtype=jnp.int32), jnp.arange(col_len, dtype=jnp.int32), (time_len, row_len, col_len))
    bias_full = expand_bias(bias_table)
    weights = (qkv_weight, qkv_bias, proj_weight, proj_bias)
    group_size = col_len // WW

    def forward_step(packed):
        return window_forward(packed[0][0], packed[1], weights, bias_full)

    def backward_step(packed):
        return window_backward(packed[0][0], packed[1], packed[0][1], weights, bias_full)
    branch = over_windows(forward_step, (rolled,), labels, group_size)
    branch = jnp.roll(branch, (ST, SH, SW), (0, 1, 2))
    ys = inputs + branch.astype(jnp.float32)
    mlp_params = (norm2_gain, norm2_bias, fc1_weight, fc1_bias, fc2_weight, fc2_bias)

    def mlp_step(packed):
        return mlp_gradient(packed[0], packed[1], mlp_params)
    grad_ys = lax.map(mlp_step, (ys.reshape(time_len, -1, chan_len), goal_frames.reshape(time_len, -1, chan_len)))
    grad_ys = grad_ys.reshape(time_len, row_len, col_len, chan_len)
    grad_rolled = jnp.roll(grad_ys.astype(jnp.bfloat16), (-ST, -SH, -SW), (0, 1, 2))
    grad_normed = over_windows(backward_step, (rolled, grad_rolled), labels, group_size)
    grad_home = jnp.roll(grad_normed, (ST, SH, SW), (0, 1, 2))
    result = (grad_ys + norm_backward(grad_home.astype(jnp.float32), normal1, inv_std1, norm1_gain)).astype(jnp.bfloat16)
    return from_frame(result, clip_tokens.shape[2], clip_tokens.shape[3])
```

```python
import itertools

import jax
import jax.numpy as jnp
import numpy as np
from jax import lax
from jax.experimental import pallas as pl
from jax.experimental.pallas import tpu as pltpu
from jax.sharding import PartitionSpec as P

HEADS = 4
HEAD = 32
CHAN = 128
FF = 512
WT = 8
WH = 7
WW = 7
ST = 4
SH = 3
SW = 3
TCOLS = 4
TROWS = 4
TM = 16
TOK = WT * WH * WW
KEYS = 512
SLAB = WW * WT

EPSILON = 1e-05
MASKED = -1000000000.0
ROOT_HALF = 0.7071067811865476
INV_ROOT_TAU = 0.3989422804014327
SCALE = HEAD ** (-0.5)

F32 = jnp.float32
BF16 = jnp.bfloat16
MESH = pl.DeviceIdType.MESH


def message_plan():
    parts_time = (range(ST, WT), range(0, ST))
    parts_rows = (range(SH, WH), range(0, SH))
    parts_cols = (range(SW, WW), range(0, SW))
    plan = []
    offset = 0
    for et, er, ec in itertools.product(range(2), range(2), range(2)):
        tile_rows = []
        window_rows = []
        for h, w, t in itertools.product(parts_rows[er], parts_cols[ec], parts_time[et]):
            tile_rows.append((h * WW + w) * WT + t)
            a, b, c = (t - ST) % WT, (h - SH) % WH, (w - SW) % WW
            window_rows.append((b * WW + c) * WT + a)
        size = -(-len(tile_rows) // 16) * 16
        plan.append(((et, er, ec), offset, size, tile_rows, window_rows))
        offset += size
    return plan, offset


PLAN, PACKED = message_plan()
AWAY = [cut for cut in PLAN if any(cut[0])]


def selectors():
    from_tile = np.zeros((PACKED, TOK), np.float32)
    from_window = np.zeros((PACKED, TOK), np.float32)
    for _, offset, _, tile_rows, window_rows in PLAN:
        for i, (tile_row, window_row) in enumerate(zip(tile_rows, window_rows)):
            from_tile[offset + i, tile_row] = 1.0
            from_window[offset + i, window_row] = 1.0
    return from_tile, from_window


def dot(a, b, dims=((1,), (0,))):
    return lax.dot_general(a, b, (dims, ((), ())), preferred_element_type=F32)


NT = ((1,), (1,))


def row_mean(values):
    return jnp.sum(values, -1, keepdims=True) * (1.0 / CHAN)


def norm_stats(values):
    center = values - row_mean(values)
    inv_std = lax.rsqrt(row_mean(center * center) + EPSILON)
    return center * inv_std, inv_std


def norm_backward(grad_out, normal, inv_std, gain):
    scaled = grad_out * gain
    return inv_std * (scaled - row_mean(scaled) - normal * row_mean(scaled * normal))


def iota(shape, dim):
    return lax.broadcasted_iota(jnp.int32, shape, dim)


def neighbour(sign, cut):
    time_pos = lax.axis_index("tm")
    tile_pos = lax.axis_index("tile")
    row, col = tile_pos // TCOLS, tile_pos % TCOLS
    et, er, ec = cut
    to_time = (time_pos + TM + sign * et) % TM
    to_row = (row + TROWS + sign * er) % TROWS
    to_col = (col + TCOLS + sign * ec) % TCOLS
    return {"tm": to_time, "tile": to_row * TCOLS + to_col}


def copies(src, dst, send_sems, recv_sems, sign):
    return [
        pltpu.make_async_remote_copy(
            src_ref=src.at[pl.ds(offset, size), :],
            dst_ref=dst.at[pl.ds(offset, size), :],
            send_sem=send_sems.at[i],
            recv_sem=recv_sems.at[i],
            device_id=neighbour(sign, cut),
            device_id_type=MESH,
        )
        for i, (cut, offset, size, _, _) in enumerate(AWAY)
    ]


def fill_bias(table, slab_ref, spread_ref, skew_ref, bias_ref):
    time_span, row_span, col_span = 2 * WT - 1, 2 * WH - 1, 2 * WW - 1
    plane = row_span * col_span
    for d in range(time_span):
        slab_ref[HEADS * d : HEADS * (d + 1), :] = table[:, d * plane : (d + 1) * plane]
    slabs = slab_ref[...]
    high = slabs.astype(BF16)
    rest = slabs - high.astype(F32)
    middle = rest.astype(BF16)
    low = (rest - middle.astype(F32)).astype(BF16)
    lanes = iota((1, row_span * 128), 1)
    slot = lanes % 128 // WT
    wanted = jnp.where(slot < col_span, lanes // 128 * col_span + (col_span - 1) - slot, -1)
    pick = (iota((plane, row_span * 128), 0) == wanted).astype(F32).astype(BF16)
    spread = (dot(low, pick) + dot(middle, pick)) + dot(high, pick)
    for p in range(row_span):
        spread_ref[p] = spread[:, p * 128 : (p + 1) * 128]
    lane_time = iota((WT, 128), 1) % WT
    for h in range(HEADS):
        for p in range(row_span):
            skewed = None
            for a in range(WT):
                rows = spread_ref[p, pl.ds((WT - 1 - a) * HEADS + h, WT, stride=HEADS), :]
                skewed = rows if skewed is None else jnp.where(lane_time == a, rows, skewed)
            skew_ref[h, p] = skewed
    first = iota((WT, 128), 1) < 64
    for h in range(HEADS):
        for d in range(row_span):
            one, two = skew_ref[h, d], skew_ref[h, max(d - 1, 0)]
            for c in range(WW):
                shift = WT * (WW - 1 - c)
                bias_ref[h, d, c] = jnp.where(
                    first,
                    one if shift == 0 else pltpu.roll(one, 128 - shift, 1),
                    pltpu.roll(two, 64 - shift, 1),
                )


def region_classes(shape, row, col, time):
    last_time = lax.axis_index("tm") == TM - 1
    last_row = lax.axis_index("tile") // TCOLS == TROWS - 1
    last_col = lax.axis_index("tile") % TCOLS == TCOLS - 1
    return (
        jnp.where(time >= ST, jnp.where(last_time, 4, 0), 0)
        + jnp.where(row >= WH - SH, jnp.where(last_row, 2, 0), 0)
        + jnp.where(col >= WW - SW, jnp.where(last_col, 1, 0), 0)
    )


def pad_keys(values):
    blocks = values.reshape(WH, WW, WT, CHAN)
    blocks = jnp.concatenate([blocks, jnp.zeros((WH, 1, WT, CHAN), values.dtype)], axis=1)
    blocks = jnp.concatenate([blocks, jnp.zeros((1, 8, WT, CHAN), values.dtype)], axis=0)
    return blocks.reshape(KEYS, CHAN)


def unpad_keys(values):
    return values.reshape(8, 8, WT, CHAN)[:WH, :WW].reshape(TOK, CHAN)


def kernel(
    clip_ref,
    goal_ref,
    from_tile_ref,
    from_window_ref,
    to_tile_ref,
    to_window_ref,
    gain1_ref,
    shift1_ref,
    qkv_weight_ref,
    qkv_bias_ref,
    table_ref,
    proj_weight_ref,
    proj_bias_ref,
    gain2_ref,
    shift2_ref,
    fc1_weight_ref,
    fc1_bias_ref,
    fc2_weight_ref,
    fc2_bias_ref,
    out_ref,
    clip_out,
    clip_in,
    goal_out,
    goal_in,
    back_out,
    back_in,
    slab_ref,
    spread_ref,
    skew_ref,
    bias_ref,
    probs_ref,
    work_ref,
    send_sems,
    recv_sems,
):
    barrier = pltpu.get_barrier_semaphore()
    for cut, _, _, _, _ in AWAY:
        pl.semaphore_signal(barrier, inc=1, device_id=neighbour(1, cut), device_id_type=MESH)

    from_tile = from_tile_ref[...]
    clip_packed = dot(from_tile, clip_ref[...].reshape(TOK, CHAN)).astype(BF16)
    goal_packed = dot(from_tile, goal_ref[...].reshape(TOK, CHAN)).astype(BF16)
    clip_out[...] = clip_packed
    goal_out[...] = goal_packed
    pl.semaphore_wait(barrier, len(AWAY))
    clip_copies = copies(clip_out, clip_in, send_sems.at[0], recv_sems.at[0], -1)
    goal_copies = copies(goal_out, goal_in, send_sems.at[1], recv_sems.at[1], -1)
    for copy in clip_copies:
        copy.start()
    for copy in goal_copies:
        copy.start()
    kept = PLAN[0][2]
    clip_in[0:kept, :] = clip_packed[0:kept]
    goal_in[0:kept, :] = goal_packed[0:kept]

    fill_bias(table_ref[...], slab_ref, spread_ref, skew_ref, bias_ref)

    lane = iota((1, CHAN), 1)
    heads = [(lane // HEAD == h) for h in range(HEADS)]
    heads_low = [mask.astype(F32).astype(BF16) for mask in heads]
    places = [lane - (h + 1) % HEADS * HEAD for h in range(HEADS)]
    token = iota((TOK, 1), 0)
    query_class = region_classes(
        (TOK, 1), token // SLAB, token % SLAB // WT, token % WT
    )
    key = iota((KEYS, 1), 0)
    key_row, key_col = key // 64, key % 64 // WT
    key_class = region_classes((KEYS, 1), key_row, key_col, key % WT)
    key_class = jnp.where((key_row < WH) & (key_col < WW), key_class, 8)

    for copy in clip_copies:
        copy.wait_recv()
    to_window = to_window_ref[...]
    frames = dot(to_window, clip_in[...])
    normal1, inv_std1 = norm_stats(frames)
    normed1 = (normal1 * gain1_ref[...] + shift1_ref[...]).astype(BF16)
    projected = dot(normed1, qkv_weight_ref[...]) + qkv_bias_ref[...]
    queries = projected[:, :CHAN] * SCALE
    keys = pad_keys(projected[:, CHAN : 2 * CHAN])
    values = pad_keys(projected[:, 2 * CHAN :]).astype(BF16)
    queries_low = queries.astype(BF16)
    keys_low = keys.astype(BF16)

    mixed = None
    for h in range(HEADS):
        query_extra = ((query_class == places[h]) & (places[h] >= 0)).astype(F32)
        key_extra = jnp.where(
            (key_class != places[h]) & (places[h] >= 0) & (places[h] < 8), MASKED, 0.0
        )
        head_queries = jnp.where(heads[h], queries, query_extra).astype(BF16)
        head_keys = jnp.where(heads[h], keys, key_extra).astype(BF16)
        work_ref[h] = dot(head_queries, head_keys, NT)
        for b in range(WH):
            span = pl.ds(b * SLAB, SLAB)
            scores = work_ref[h, span, :]
            bias = jnp.concatenate(
                [bias_ref[h, b - 2 * m + 6].reshape(SLAB, 128) for m in range(4)], axis=1
            )
            scores = scores + bias
            exponent = jnp.exp(scores - jnp.max(scores, -1, keepdims=True))
            probs_ref[h, span, :] = exponent * (1.0 / jnp.sum(exponent, -1, keepdims=True))
        part = dot(probs_ref[h].astype(BF16), values * heads_low[h])
        mixed = part if mixed is None else mixed + part
    mixed = mixed.astype(BF16)
    branch = (dot(mixed, proj_weight_ref[...]) + proj_bias_ref[...]).astype(BF16)
    ys = frames + branch.astype(F32)

    normal2, inv_std2 = norm_stats(ys)
    normed2 = (normal2 * gain2_ref[...] + shift2_ref[...]).astype(BF16)
    work_ref[0] = dot(normed2, fc1_weight_ref[...]) + fc1_bias_ref[...]
    for b in range(WH):
        span = pl.ds(b * SLAB, SLAB)
        pre_act = work_ref[0, span, :]
        half = 0.5 * (1.0 + lax.erf(pre_act * ROOT_HALF))
        work_ref[1, span, :] = pre_act * half
        work_ref[2, span, :] = half + pre_act * INV_ROOT_TAU * jnp.exp(-0.5 * pre_act * pre_act)
    outputs = ys + dot(work_ref[1].astype(BF16), fc2_weight_ref[...]) + fc2_bias_ref[...]
    for copy in goal_copies:
        copy.wait_recv()
    goal = dot(to_window, goal_in[...])
    grad_out = outputs - goal
    grad_pre = (dot(grad_out.astype(BF16), fc2_weight_ref[...], NT) * work_ref[2]).astype(BF16)
    grad_norm2 = dot(grad_pre, fc1_weight_ref[...], NT)
    grad_ys = grad_out + norm_backward(grad_norm2, normal2, inv_std2, gain2_ref[...])

    grad_mixed = dot(grad_ys.astype(BF16), proj_weight_ref[...], NT)
    grad_mixed_low = grad_mixed.astype(BF16)
    queries_across = queries.T.astype(BF16)
    grad_mixed_across = grad_mixed.T.astype(BF16)
    grad_queries = None
    grad_keys = []
    grad_values = []
    for h in range(HEADS):
        rows = slice(h * HEAD, (h + 1) * HEAD)
        work_ref[h] = dot(grad_mixed_low * heads_low[h], values, NT)
        for b in range(WH):
            span = pl.ds(b * SLAB, SLAB)
            probs = probs_ref[h, span, :]
            grad_probs = work_ref[h, span, :]
            delta = jnp.sum(probs * grad_probs, -1, keepdims=True)
            work_ref[h, span, :] = probs * (grad_probs - delta)
        grad_scores = work_ref[h].astype(BF16)
        part = dot(grad_scores, keys_low * heads_low[h])
        grad_queries = part if grad_queries is None else grad_queries + part
        grad_keys.append(dot(queries_across[rows], grad_scores))
        grad_values.append(dot(grad_mixed_across[rows], probs_ref[h].astype(BF16)))
    grad_queries = (grad_queries * SCALE).astype(BF16)
    grad_keys = unpad_keys(jnp.concatenate(grad_keys, axis=0).T).astype(BF16)
    grad_values = unpad_keys(jnp.concatenate(grad_values, axis=0).T).astype(BF16)
    grad_qkv = jnp.concatenate([grad_queries, grad_keys, grad_values], axis=1)
    grad_normed = dot(grad_qkv, qkv_weight_ref[...], NT).astype(BF16).astype(F32)
    result = grad_ys + norm_backward(grad_normed, normal1, inv_std1, gain1_ref[...])

    back_packed = dot(from_window_ref[...], result.astype(BF16)).astype(BF16)
    back_out[...] = back_packed
    back_copies = copies(back_out, back_in, send_sems.at[2], recv_sems.at[2], 1)
    for copy in back_copies:
        copy.start()
    back_in[0:kept, :] = back_packed[0:kept]
    for copy in back_copies:
        copy.wait_recv()
    out_ref[...] = dot(to_tile_ref[...], back_in[...]).astype(BF16).reshape(WH * WW, WT, CHAN)
    for copy in clip_copies + goal_copies + back_copies:
        copy.wait_send()


def shards(
    clip_tokens,
    target,
    norm1_gain,
    norm1_bias,
    qkv_weight,
    qkv_bias,
    bias_table,
    proj_weight,
    proj_bias,
    norm2_gain,
    norm2_bias,
    fc1_weight,
    fc1_bias,
    fc2_weight,
    fc2_bias,
):
    def by_place(tokens):
        return jnp.transpose(tokens, (1, 2, 3, 0, 4)).reshape(WH * WW, WT, CHAN)

    from_tile, from_window = selectors()
    operands = [
        by_place(clip_tokens),
        by_place(target),
        jnp.asarray(from_tile, BF16),
        jnp.asarray(from_window, BF16),
        jnp.asarray(from_tile.T, BF16),
        jnp.asarray(from_window.T, BF16),
        norm1_gain.reshape(1, -1),
        norm1_bias.reshape(1, -1),
        qkv_weight,
        qkv_bias.reshape(1, -1),
        bias_table.T,
        proj_weight,
        proj_bias.reshape(1, -1),
        norm2_gain.reshape(1, -1),
        norm2_bias.reshape(1, -1),
        fc1_weight,
        fc1_bias.reshape(1, -1),
        fc2_weight,
        fc2_bias.reshape(1, -1),
    ]
    vmem = pl.BlockSpec(memory_space=pltpu.VMEM)
    plane = (2 * WH - 1) * (2 * WW - 1)
    out = pl.pallas_call(
        kernel,
        out_shape=jax.ShapeDtypeStruct((WH * WW, WT, CHAN), BF16),
        in_specs=[vmem] * len(operands),
        out_specs=vmem,
        scratch_shapes=[pltpu.VMEM((PACKED, CHAN), BF16)] * 6
        + [
            pltpu.VMEM((HEADS * (2 * WT - 1), plane), F32),
            pltpu.VMEM((2 * WH - 1, HEADS * (2 * WT - 1), 128), F32),
            pltpu.VMEM((HEADS, 2 * WH - 1, WT, 128), F32),
            pltpu.VMEM((HEADS, 2 * WH - 1, WW, WT, 128), F32),
            pltpu.VMEM((HEADS, TOK, KEYS), F32),
            pltpu.VMEM((HEADS, TOK, KEYS), F32),
            pltpu.SemaphoreType.DMA((3, len(AWAY))),
            pltpu.SemaphoreType.DMA((3, len(AWAY))),
        ],
        compiler_params=pltpu.CompilerParams(
            collective_id=0, has_side_effects=True, vmem_limit_bytes=48 * 1024 * 1024
        ),
        name="window_block",
    )(*operands)
    return jnp.transpose(out.reshape(1, WH, WW, WT, CHAN), (3, 0, 1, 2, 4))


def solution(mesh):
    return jax.shard_map(
        shards,
        mesh=mesh,
        in_specs=(P("tm", "tile", None, None, None),) * 2 + (P(),) * 13,
        out_specs=P("tm", "tile", None, None, None),
        check_vma=False,
    )
```

```python
import itertools

import jax
import jax.numpy as jnp
import numpy as np
from jax import lax
from jax.experimental import pallas as pl
from jax.experimental.pallas import tpu as pltpu
from jax.sharding import PartitionSpec as P

HEADS = 4
HEAD = 32
CHAN = 128
FF = 512
WT = 8
WH = 7
WW = 7
ST = 4
SH = 3
SW = 3
TCOLS = 4
TROWS = 4
TM = 16
TOK = WT * WH * WW
KEYS = 512
SLAB = WW * WT

EPSILON = 1e-05
MASKED = -1000000000.0
ROOT_HALF = 0.7071067811865476
INV_ROOT_TAU = 0.3989422804014327
SCALE = HEAD ** (-0.5)

F32 = jnp.float32
BF16 = jnp.bfloat16
MESH = pl.DeviceIdType.MESH


def message_plan():
    parts_time = (range(ST, WT), range(0, ST))
    parts_rows = (range(SH, WH), range(0, SH))
    parts_cols = (range(SW, WW), range(0, SW))
    plan = []
    offset = 0
    for et, er, ec in itertools.product(range(2), range(2), range(2)):
        tile_rows = []
        window_rows = []
        for h, w, t in itertools.product(parts_rows[er], parts_cols[ec], parts_time[et]):
            tile_rows.append((h * WW + w) * WT + t)
            a, b, c = (t - ST) % WT, (h - SH) % WH, (w - SW) % WW
            window_rows.append((b * WW + c) * WT + a)
        size = -(-len(tile_rows) // 16) * 16
        plan.append(((et, er, ec), offset, size, tile_rows, window_rows))
        offset += size
    return plan, offset


PLAN, PACKED = message_plan()
AWAY = [cut for cut in PLAN if any(cut[0])]


def selectors():
    from_tile = np.zeros((PACKED, TOK), np.float32)
    from_window = np.zeros((PACKED, TOK), np.float32)
    for _, offset, _, tile_rows, window_rows in PLAN:
        for i, (tile_row, window_row) in enumerate(zip(tile_rows, window_rows)):
            from_tile[offset + i, tile_row] = 1.0
            from_window[offset + i, window_row] = 1.0
    return from_tile, from_window


def dot(a, b, dims=((1,), (0,))):
    return lax.dot_general(a, b, (dims, ((), ())), preferred_element_type=F32)


NT = ((1,), (1,))


def row_mean(values):
    return jnp.sum(values, -1, keepdims=True) * (1.0 / CHAN)


def norm_stats(values):
    center = values - row_mean(values)
    inv_std = lax.rsqrt(row_mean(center * center) + EPSILON)
    return center * inv_std, inv_std


def norm_backward(grad_out, normal, inv_std, gain):
    scaled = grad_out * gain
    return inv_std * (scaled - row_mean(scaled) - normal * row_mean(scaled * normal))


def iota(shape, dim):
    return lax.broadcasted_iota(jnp.int32, shape, dim)


def neighbour(sign, cut):
    time_pos = lax.axis_index("tm")
    tile_pos = lax.axis_index("tile")
    row, col = tile_pos // TCOLS, tile_pos % TCOLS
    et, er, ec = cut
    to_time = (time_pos + TM + sign * et) % TM
    to_row = (row + TROWS + sign * er) % TROWS
    to_col = (col + TCOLS + sign * ec) % TCOLS
    return {"tm": to_time, "tile": to_row * TCOLS + to_col}


def copies(src, dst, send_sems, recv_sems, sign):
    return [
        pltpu.make_async_remote_copy(
            src_ref=src.at[pl.ds(offset, size), :],
            dst_ref=dst.at[pl.ds(offset, size), :],
            send_sem=send_sems.at[i],
            recv_sem=recv_sems.at[i],
            device_id=neighbour(sign, cut),
            device_id_type=MESH,
        )
        for i, (cut, offset, size, _, _) in enumerate(AWAY)
    ]


def fill_bias(table, slab_ref, spread_ref, skew_ref, bias_ref):
    time_span, row_span, col_span = 2 * WT - 1, 2 * WH - 1, 2 * WW - 1
    plane = row_span * col_span
    for d in range(time_span):
        slab_ref[HEADS * d : HEADS * (d + 1), :] = table[:, d * plane : (d + 1) * plane]
    slabs = slab_ref[...]
    high = slabs.astype(BF16)
    rest = slabs - high.astype(F32)
    middle = rest.astype(BF16)
    low = (rest - middle.astype(F32)).astype(BF16)
    lanes = iota((1, row_span * 128), 1)
    slot = lanes % 128 // WT
    wanted = jnp.where(slot < col_span, lanes // 128 * col_span + (col_span - 1) - slot, -1)
    pick = (iota((plane, row_span * 128), 0) == wanted).astype(F32).astype(BF16)
    spread = (dot(low, pick) + dot(middle, pick)) + dot(high, pick)
    for p in range(row_span):
        spread_ref[p] = spread[:, p * 128 : (p + 1) * 128]
    lane_time = iota((WT, 128), 1) % WT
    for h in range(HEADS):
        for p in range(row_span):
            skewed = None
            for a in range(WT):
                rows = spread_ref[p, pl.ds((WT - 1 - a) * HEADS + h, WT, stride=HEADS), :]
                skewed = rows if skewed is None else jnp.where(lane_time == a, rows, skewed)
            skew_ref[h, p] = skewed
    first = iota((WT, 128), 1) < 64
    for h in range(HEADS):
        for d in range(row_span):
            one, two = skew_ref[h, d], skew_ref[h, max(d - 1, 0)]
            for c in range(WW):
                shift = WT * (WW - 1 - c)
                bias_ref[h, d, c] = jnp.where(
                    first,
                    one if shift == 0 else pltpu.roll(one, 128 - shift, 1),
                    pltpu.roll(two, 64 - shift, 1),
                )


def region_classes(row, col, time):
    last_time = lax.axis_index("tm") == TM - 1
    last_row = lax.axis_index("tile") // TCOLS == TROWS - 1
    last_col = lax.axis_index("tile") % TCOLS == TCOLS - 1
    return (
        jnp.where(time >= ST, jnp.where(last_time, 4, 0), 0)
        + jnp.where(row >= WH - SH, jnp.where(last_row, 2, 0), 0)
        + jnp.where(col >= WW - SW, jnp.where(last_col, 1, 0), 0)
    )


def pad_keys(values):
    blocks = values.reshape(WH, WW, WT, CHAN)
    blocks = jnp.concatenate([blocks, jnp.zeros((WH, 1, WT, CHAN), values.dtype)], axis=1)
    blocks = jnp.concatenate([blocks, jnp.zeros((1, 8, WT, CHAN), values.dtype)], axis=0)
    return blocks.reshape(KEYS, CHAN)


def unpad_keys(values):
    return values.reshape(8, 8, WT, CHAN)[:WH, :WW].reshape(TOK, CHAN)


OPERANDS = (
    "clip",
    "from_tile",
    "table",
    "to_window",
    "gain1",
    "shift1",
    "qkv_weight",
    "qkv_bias",
    "goal",
    "proj_weight",
    "proj_bias",
    "gain2",
    "shift2",
    "fc1_weight",
    "fc1_bias",
    "fc2_weight",
    "fc2_bias",
    "from_window",
    "to_tile",
)


def kernel(*refs):
    count = len(OPERANDS)
    sources, out_ref, held = refs[:count], refs[count], refs[count + 1 : 2 * count + 1]
    (
        load_sems,
        clip_out,
        clip_in,
        goal_out,
        goal_in,
        back_out,
        back_in,
        slab_ref,
        spread_ref,
        skew_ref,
        bias_ref,
        scores_ref,
        probs_ref,
        grad_ref,
        send_sems,
        recv_sems,
    ) = refs[2 * count + 1 :]

    loads = {}
    for i, name in enumerate(OPERANDS):
        loads[name] = (pltpu.make_async_copy(sources[i], held[i], load_sems.at[i]), held[i])
        loads[name][0].start()
    barrier = pltpu.get_barrier_semaphore()
    for cut, _, _, _, _ in AWAY:
        pl.semaphore_signal(barrier, inc=1, device_id=neighbour(1, cut), device_id_type=MESH)

    def operand(name):
        copy, ref = loads[name]
        copy.wait()
        return ref[...]

    clip = operand("clip").reshape(TOK, CHAN)
    from_tile = operand("from_tile")[:PACKED]
    clip_packed = dot(from_tile, clip).astype(BF16)
    clip_out[...] = clip_packed
    pl.semaphore_wait(barrier, len(AWAY))
    clip_copies = copies(clip_out, clip_in, send_sems.at[0], recv_sems.at[0], -1)
    for copy in clip_copies:
        copy.start()
    kept = PLAN[0][2]
    clip_in[0:kept, :] = clip_packed[0:kept]

    goal_packed = dot(from_tile, operand("goal").reshape(TOK, CHAN)).astype(BF16)
    goal_out[...] = goal_packed
    goal_copies = copies(goal_out, goal_in, send_sems.at[1], recv_sems.at[1], -1)
    for copy in goal_copies:
        copy.start()
    goal_in[0:kept, :] = goal_packed[0:kept]

    fill_bias(operand("table"), slab_ref, spread_ref, skew_ref, bias_ref)

    lane = iota((1, CHAN), 1)
    heads = [(lane // HEAD == h) for h in range(HEADS)]
    heads_low = [mask.astype(F32).astype(BF16) for mask in heads]
    places = [lane - (h + 1) % HEADS * HEAD for h in range(HEADS)]
    token = iota((TOK, 1), 0)
    query_class = region_classes(token // SLAB, token % SLAB // WT, token % WT)
    key = iota((KEYS, 1), 0)
    key_row, key_col = key // 64, key % 64 // WT
    key_class = region_classes(key_row, key_col, key % WT)
    key_class = jnp.where((key_row < WH) & (key_col < WW), key_class, 8)

    to_window = operand("to_window")
    gain1 = operand("gain1")
    shift1 = operand("shift1")
    qkv_weight = operand("qkv_weight")
    qkv_bias = operand("qkv_bias")
    for copy in clip_copies:
        copy.wait_recv()
    frames = dot(to_window, clip_in[...])
    normal1, inv_std1 = norm_stats(frames)
    normed1 = (normal1 * gain1 + shift1).astype(BF16)
    projected = dot(normed1, qkv_weight)
    queries = (projected[:, :CHAN] + qkv_bias[0:1]) * SCALE
    keys = pad_keys(projected[:, CHAN : 2 * CHAN] + qkv_bias[1:2])
    values = pad_keys(projected[:, 2 * CHAN :] + qkv_bias[2:3]).astype(BF16)
    keys_low = keys.astype(BF16)

    mixed = None
    for h in range(HEADS):
        query_extra = ((query_class == places[h]) & (places[h] >= 0)).astype(F32)
        key_extra = jnp.where(
            (key_class != places[h]) & (places[h] >= 0) & (places[h] < 8), MASKED, 0.0
        )
        head_queries = jnp.where(heads[h], queries, query_extra).astype(BF16)
        head_keys = jnp.where(heads[h], keys, key_extra).astype(BF16)
        scores_ref[h] = dot(head_queries, head_keys, NT)
        for first in range(0, WH, 2):
            slabs = range(first, min(first + 2, WH))
            span = pl.ds(first * SLAB, len(slabs) * SLAB)
            bias = jnp.concatenate(
                [
                    jnp.concatenate(
                        [bias_ref[h, b - 2 * m + 6].reshape(SLAB, 128) for m in range(4)], axis=1
                    )
                    for b in slabs
                ],
                axis=0,
            )
            scores = scores_ref[h, span, :] + bias
            exponent = jnp.exp(scores - jnp.max(scores, -1, keepdims=True))
            probs_ref[h, span, :] = exponent.astype(BF16)
        ones = jnp.broadcast_to(heads_low[h], (KEYS, CHAN))
        part = dot(probs_ref[h], jnp.concatenate([values * heads_low[h], ones], axis=1))
        mixed = part if mixed is None else mixed + part
    inv_total = 1.0 / mixed[:, CHAN:]
    mixed = mixed[:, :CHAN] * inv_total
    proj_weight = operand("proj_weight")
    branch = (dot(mixed.astype(BF16), proj_weight) + operand("proj_bias")).astype(BF16)
    ys = frames + branch.astype(F32)

    gain2 = operand("gain2")
    fc1_weight = operand("fc1_weight")
    fc2_weight = operand("fc2_weight")
    normal2, inv_std2 = norm_stats(ys)
    normed2 = (normal2 * gain2 + operand("shift2")).astype(BF16)
    scores_ref[0] = dot(normed2, fc1_weight) + operand("fc1_bias")
    for b in range(WH):
        span = pl.ds(b * SLAB, SLAB)
        pre_act = scores_ref[0, span, :]
        half = 0.5 * (1.0 + lax.erf(pre_act * ROOT_HALF))
        scores_ref[1, span, :] = pre_act * half
        scores_ref[2, span, :] = half + pre_act * INV_ROOT_TAU * jnp.exp(-0.5 * pre_act * pre_act)
    outputs = ys + dot(scores_ref[1].astype(BF16), fc2_weight) + operand("fc2_bias")
    for copy in goal_copies:
        copy.wait_recv()
    goal = dot(to_window, goal_in[...])
    grad_out = outputs - goal
    grad_pre = (dot(grad_out.astype(BF16), fc2_weight, NT) * scores_ref[2]).astype(BF16)
    grad_norm2 = dot(grad_pre, fc1_weight, NT)
    grad_ys = grad_out + norm_backward(grad_norm2, normal2, inv_std2, gain2)

    grad_mixed = dot(grad_ys.astype(BF16), proj_weight, NT) * inv_total
    grad_mixed_low = grad_mixed.astype(BF16)
    toward = grad_mixed_low.astype(F32) * mixed
    queries_across = queries.T.astype(BF16)
    grad_mixed_across = grad_mixed.T.astype(BF16)
    grad_queries = None
    grad_keys = []
    grad_values = []
    for h in range(HEADS):
        rows = slice(h * HEAD, (h + 1) * HEAD)
        delta = jnp.sum(jnp.where(heads[h], toward, 0.0), -1, keepdims=True)
        scores_ref[h] = dot(grad_mixed_low * heads_low[h], values, NT)
        for first in range(0, WH, 2):
            rows_here = slice(first * SLAB, min(first + 2, WH) * SLAB)
            span = pl.ds(first * SLAB, rows_here.stop - rows_here.start)
            probs = probs_ref[h, span, :].astype(F32)
            grad_ref[h, span, :] = (
                probs * (scores_ref[h, span, :] - delta[rows_here])
            ).astype(BF16)
        grad_scores = grad_ref[h]
        part = dot(grad_scores, keys_low * heads_low[h])
        grad_queries = part if grad_queries is None else grad_queries + part
        grad_keys.append(dot(queries_across[rows], grad_scores))
        grad_values.append(dot(grad_mixed_across[rows], probs_ref[h]))
    grad_queries = (grad_queries * SCALE).astype(BF16)
    grad_keys = unpad_keys(jnp.concatenate(grad_keys, axis=0).T).astype(BF16)
    grad_values = unpad_keys(jnp.concatenate(grad_values, axis=0).T).astype(BF16)
    grad_qkv = jnp.concatenate([grad_queries, grad_keys, grad_values], axis=1)
    grad_normed = dot(grad_qkv, qkv_weight, NT).astype(BF16).astype(F32)
    result = grad_ys + norm_backward(grad_normed, normal1, inv_std1, gain1)

    back_packed = dot(operand("from_window")[:PACKED], result.astype(BF16)).astype(BF16)
    back_out[...] = back_packed
    back_copies = copies(back_out, back_in, send_sems.at[2], recv_sems.at[2], 1)
    for copy in back_copies:
        copy.start()
    back_in[0:kept, :] = back_packed[0:kept]
    to_tile = operand("to_tile")
    for copy in back_copies:
        copy.wait_recv()
    out_ref[...] = dot(to_tile, back_in[...]).astype(BF16).reshape(WH * WW, WT, CHAN)
    for copy in clip_copies + goal_copies + back_copies:
        copy.wait_send()


def shards(
    clip_tokens,
    target,
    norm1_gain,
    norm1_bias,
    qkv_weight,
    qkv_bias,
    bias_table,
    proj_weight,
    proj_bias,
    norm2_gain,
    norm2_bias,
    fc1_weight,
    fc1_bias,
    fc2_weight,
    fc2_bias,
):
    def by_place(tokens):
        return jnp.transpose(tokens, (1, 2, 3, 0, 4)).reshape(WH * WW, WT, CHAN)

    from_tile, from_window = selectors()
    named = {
        "clip": by_place(clip_tokens),
        "from_tile": jnp.asarray(np.pad(from_tile, ((0, 8), (0, 0))), BF16),
        "table": bias_table.T,
        "to_window": jnp.asarray(from_window.T, BF16),
        "gain1": norm1_gain.reshape(1, -1),
        "shift1": norm1_bias.reshape(1, -1),
        "qkv_weight": qkv_weight,
        "qkv_bias": qkv_bias.reshape(3, -1),
        "goal": by_place(target),
        "proj_weight": proj_weight,
        "proj_bias": proj_bias.reshape(1, -1),
        "gain2": norm2_gain.reshape(1, -1),
        "shift2": norm2_bias.reshape(1, -1),
        "fc1_weight": fc1_weight,
        "fc1_bias": fc1_bias.reshape(1, -1),
        "fc2_weight": fc2_weight,
        "fc2_bias": fc2_bias.reshape(1, -1),
        "from_window": jnp.asarray(np.pad(from_window, ((0, 8), (0, 0))), BF16),
        "to_tile": jnp.asarray(from_tile.T, BF16),
    }
    operands = [named[name] for name in OPERANDS]
    plane = (2 * WH - 1) * (2 * WW - 1)
    out = pl.pallas_call(
        kernel,
        out_shape=jax.ShapeDtypeStruct((WH * WW, WT, CHAN), BF16),
        in_specs=[pl.BlockSpec(memory_space=pltpu.HBM)] * len(operands),
        out_specs=pl.BlockSpec(memory_space=pltpu.VMEM),
        scratch_shapes=[pltpu.VMEM(x.shape, x.dtype) for x in operands]
        + [pltpu.SemaphoreType.DMA((len(operands),))]
        + [pltpu.VMEM((PACKED, CHAN), BF16)] * 6
        + [
            pltpu.VMEM((HEADS * (2 * WT - 1), plane), F32),
            pltpu.VMEM((2 * WH - 1, HEADS * (2 * WT - 1), 128), F32),
            pltpu.VMEM((HEADS, 2 * WH - 1, WT, 128), F32),
            pltpu.VMEM((HEADS, 2 * WH - 1, WW, WT, 128), F32),
            pltpu.VMEM((HEADS, TOK, KEYS), F32),
            pltpu.VMEM((HEADS, TOK, KEYS), BF16),
            pltpu.VMEM((HEADS, TOK, KEYS), BF16),
            pltpu.SemaphoreType.DMA((3, len(AWAY))),
            pltpu.SemaphoreType.DMA((3, len(AWAY))),
        ],
        compiler_params=pltpu.CompilerParams(
            collective_id=0, has_side_effects=True, vmem_limit_bytes=54 * 1024 * 1024
        ),
        name="window_block",
    )(*operands)
    return jnp.transpose(out.reshape(1, WH, WW, WT, CHAN), (3, 0, 1, 2, 4))


def solution(mesh):
    return jax.shard_map(
        shards,
        mesh=mesh,
        in_specs=(P("tm", "tile", None, None, None),) * 2 + (P(),) * 13,
        out_specs=P("tm", "tile", None, None, None),
        check_vma=False,
    )
```

```python
import itertools

import jax
import jax.numpy as jnp
import numpy as np
from jax import lax
from jax.experimental import pallas as pl
from jax.experimental.pallas import tpu as pltpu
from jax.sharding import PartitionSpec as P

HEADS = 4
HEAD = 32
CHAN = 128
FF = 512
WT = 8
WH = 7
WW = 7
ST = 4
SH = 3
SW = 3
TCOLS = 4
TROWS = 4
TM = 16
TOK = WT * WH * WW
KEYS = 512
ROWS = 400
CHUNK = 80
TILES = CHUNK // WT

EPSILON = 1e-05
MASKED = -1000000000.0
INV_ROOT_TAU = 0.3989422804014327
ERF_STEP = 0.3275911 * 0.7071067811865476
ERF_TERMS = (0.254829592, -0.284496736, 1.421413741, -1.453152027, 1.061405429)
SCALE = HEAD ** (-0.5)

F32 = jnp.float32
BF16 = jnp.bfloat16
MESH = pl.DeviceIdType.MESH


CUTS = sorted(itertools.product(range(2), range(2), range(2)), reverse=True)
AWAY = CUTS[:-1]
HALVES = (slice(0, 192), slice(192, TOK))


def box(cut, rolled):
    et, er, ec = cut
    if rolled:
        rows, cols, half = (WH - SH if er else 0), (WW - SW if ec else 0), et
    else:
        rows, cols, half = (0 if er else SH), (0 if ec else SW), 1 - et
    return (pl.ds(rows, SH if er else WH - SH), pl.ds(cols, SW if ec else WW - SW), half)


def dot(a, b, dims=((1,), (0,))):
    return lax.dot_general(a, b, (dims, ((), ())), preferred_element_type=F32)


NT = ((1,), (1,))


def row_mean(values):
    return jnp.sum(values, -1, keepdims=True) * (1.0 / CHAN)


def norm_stats(values):
    center = values - row_mean(values)
    inv_std = lax.rsqrt(row_mean(center * center) + EPSILON)
    return center * inv_std, inv_std


def norm_backward(grad_out, normal, inv_std, gain):
    scaled = grad_out * gain
    return inv_std * (scaled - row_mean(scaled) - normal * row_mean(scaled * normal))


def iota(shape, dim):
    return lax.broadcasted_iota(jnp.int32, shape, dim)


def neighbour(sign, cut):
    time_pos = lax.axis_index("tm")
    tile_pos = lax.axis_index("tile")
    row, col = tile_pos // TCOLS, tile_pos % TCOLS
    et, er, ec = cut
    to_time = (time_pos + TM + sign * et) % TM
    to_row = (row + TROWS + sign * er) % TROWS
    to_col = (col + TCOLS + sign * ec) % TCOLS
    return {"tm": to_time, "tile": to_row * TCOLS + to_col}


def exchange(src, dst, send_sems, recv_sems, to_window):
    remote = [
        pltpu.make_async_remote_copy(
            src_ref=src.at[box(cut, not to_window)],
            dst_ref=dst.at[box(cut, to_window)],
            send_sem=send_sems.at[i],
            recv_sem=recv_sems.at[i],
            device_id=neighbour(-1 if to_window else 1, cut),
            device_id_type=MESH,
        )
        for i, cut in enumerate(AWAY)
    ]
    local = pltpu.make_async_copy(
        src.at[box(CUTS[-1], not to_window)],
        dst.at[box(CUTS[-1], to_window)],
        send_sems.at[len(AWAY)],
    )
    return remote, local


def joined(halves):
    halves = halves.astype(F32).reshape(WH * WW, 2, ST, CHAN)
    return jnp.concatenate([halves[:, 0], halves[:, 1]], axis=1).reshape(TOK, CHAN)


def fill_bias(table, slab_ref, spread_ref, skew_ref, bias_ref):
    time_span, row_span, col_span = 2 * WT - 1, 2 * WH - 1, 2 * WW - 1
    plane = row_span * col_span
    for d in range(time_span):
        slab_ref[HEADS * d : HEADS * (d + 1), :] = table[:, d * plane : (d + 1) * plane]
    slabs = slab_ref[...]
    high = slabs.astype(BF16)
    rest = slabs - high.astype(F32)
    middle = rest.astype(BF16)
    low = (rest - middle.astype(F32)).astype(BF16)
    lanes = iota((1, row_span * 128), 1)
    slot = lanes % 128 // WT
    wanted = jnp.where(slot < col_span, lanes // 128 * col_span + (col_span - 1) - slot, -1)
    pick = (iota((plane, row_span * 128), 0) == wanted).astype(F32).astype(BF16)
    spread = (dot(low, pick) + dot(middle, pick)) + dot(high, pick)
    for p in range(row_span):
        spread_ref[p] = spread[:, p * 128 : (p + 1) * 128]
    lane_time = iota((WT, 128), 1) % WT
    first = iota((WT, 128), 1) < 64

    def fill_head(h, _):
        for p in range(row_span):
            skewed = None
            for a in range(WT):
                rows = spread_ref[p, pl.ds((WT - 1 - a) * HEADS + h, WT, stride=HEADS), :]
                skewed = rows if skewed is None else jnp.where(lane_time == a, rows, skewed)
            skew_ref[p] = skewed
        for d in range(row_span):
            one, two = skew_ref[d], skew_ref[max(d - 1, 0)]
            for c in range(WW):
                shift = WT * (WW - 1 - c)
                bias_ref[h, d * WW + c] = jnp.where(
                    first,
                    one if shift == 0 else pltpu.roll(one, 128 - shift, 1),
                    pltpu.roll(two, 64 - shift, 1),
                )
        return _

    lax.fori_loop(0, HEADS, fill_head, 0)


def gelu_parts(pre_act):
    bell = jnp.exp(-0.5 * pre_act * pre_act)
    step = 1.0 / (1.0 + ERF_STEP * jnp.abs(pre_act))
    tail = ERF_TERMS[4]
    for term in ERF_TERMS[3::-1]:
        tail = tail * step + term
    tail = tail * step * (0.5 * bell)
    share = jnp.where(pre_act < 0.0, tail, 1.0 - tail)
    return pre_act * share, share + pre_act * (INV_ROOT_TAU * bell)


def region_classes(row, col, time):
    last_time = lax.axis_index("tm") == TM - 1
    last_row = lax.axis_index("tile") // TCOLS == TROWS - 1
    last_col = lax.axis_index("tile") % TCOLS == TCOLS - 1
    return (
        jnp.where(time >= ST, jnp.where(last_time, 4, 0), 0)
        + jnp.where(row >= WH - SH, jnp.where(last_row, 2, 0), 0)
        + jnp.where(col >= WW - SW, jnp.where(last_col, 1, 0), 0)
    )


def pad_keys(values):
    blocks = values.reshape(WH, WW, WT, CHAN)
    blocks = jnp.concatenate([blocks, jnp.zeros((WH, 1, WT, CHAN), values.dtype)], axis=1)
    blocks = jnp.concatenate([blocks, jnp.zeros((1, 8, WT, CHAN), values.dtype)], axis=0)
    return blocks.reshape(KEYS, CHAN)


def unpad_keys(values):
    return values.reshape(8, 8, WT, CHAN)[:WH, :WW].reshape(TOK, CHAN)


OPERANDS = (
    "table",
    "gain1",
    "shift1",
    "qkv_weight",
    "qkv_bias",
    "proj_weight",
    "proj_bias",
    "gain2",
    "shift2",
    "fc1_weight",
    "fc1_bias",
    "fc2_weight",
    "fc2_bias",
)


def kernel(*refs):
    count = len(OPERANDS)
    clip_ref, goal_ref, *sources = refs[: count + 2]
    out_ref = refs[count + 2]
    held = refs[count + 3 : 2 * count + 3]
    (
        load_sems,
        clip_in,
        goal_in,
        back_out,
        slab_ref,
        spread_ref,
        skew_ref,
        bias_ref,
        scores_ref,
        probs_ref,
        grads_ref,
        queries_ref,
        classes_ref,
        keys_ref,
        barred_ref,
        values_ref,
        mixed_ref,
        mixed_grad_ref,
        toward_ref,
        grad_queries_ref,
        send_sems,
        recv_sems,
    ) = refs[2 * count + 3 :]

    loads = {}

    def load(i):
        name = OPERANDS[i]
        loads[name] = (pltpu.make_async_copy(sources[i], held[i], load_sems.at[i]), held[i])
        loads[name][0].start()

    barrier = pltpu.get_barrier_semaphore()
    for cut in AWAY:
        pl.semaphore_signal(barrier, inc=1, device_id=neighbour(1, cut), device_id_type=MESH)
    clip_copies, clip_local = exchange(clip_ref, clip_in, send_sems.at[0], recv_sems.at[0], True)
    goal_copies, goal_local = exchange(goal_ref, goal_in, send_sems.at[1], recv_sems.at[1], True)
    back_copies, back_local = exchange(back_out, out_ref, send_sems.at[2], recv_sems.at[2], False)
    clip_local.start()
    for i in range(count):
        load(i)
    goal_local.start()

    def operand(name):
        copy, ref = loads[name]
        copy.wait()
        return ref[...]

    pl.semaphore_wait(barrier, len(AWAY))
    for copy in clip_copies:
        copy.start()

    fill_bias(operand("table"), slab_ref, spread_ref, skew_ref, bias_ref)

    lane = iota((1, CHAN), 1)
    spot = lane % HEAD
    head_masks = [lane // HEAD == h for h in range(HEADS)]
    head_lanes = [mask.astype(F32).astype(BF16) for mask in head_masks]
    token = iota((TOK, 1), 0)
    query_class = region_classes(token // (WW * WT), token % (WW * WT) // WT, token % WT)
    classes_ref[...] = jnp.where(query_class == spot, 1.0, 0.0).astype(BF16)
    key = iota((KEYS, 1), 0)
    key_row, key_col = key // 64, key % 64 // WT
    key_class = region_classes(key_row, key_col, key % WT)
    key_class = jnp.where((key_row < WH) & (key_col < WW), key_class, 8)
    barred_ref[...] = jnp.where((key_class != spot) & (spot < 8), MASKED, 0.0).astype(BF16)

    gain1 = operand("gain1")
    shift1 = operand("shift1")
    qkv_weight = operand("qkv_weight")
    qkv_bias = operand("qkv_bias")
    query_weight_across = qkv_weight[:, :CHAN].T
    query_bias_across = jnp.broadcast_to(qkv_bias[0:1], (CHAN, CHAN)).T[:, 0:1]
    for copy in clip_copies:
        copy.wait_recv()
    clip_local.wait()
    frames = joined(clip_in[...])
    normal1, inv_std1 = norm_stats(frames)
    normed1 = (normal1 * gain1 + shift1).astype(BF16)
    projected = dot(normed1, qkv_weight)
    queries_ref[...] = ((projected[:, :CHAN] + qkv_bias[0:1]) * SCALE).astype(BF16)
    keys_ref[...] = pad_keys(projected[:, CHAN : 2 * CHAN] + qkv_bias[1:2]).astype(BF16)
    values_ref[...] = pad_keys(projected[:, 2 * CHAN :] + qkv_bias[2:3]).astype(BF16)

    for copy in goal_copies:
        copy.start()

    def score(h):
        mine, spare = head_lanes[h], head_lanes[(h + 1) % HEADS]
        head_queries = queries_ref[...] * mine + classes_ref[...] * spare
        head_keys = keys_ref[...] * mine + barred_ref[...] * spare
        scores_ref[h, 0:TOK, :] = dot(head_queries, head_keys, NT)

    def weigh(h):
        for chunk in range(ROWS // CHUNK):
            span = pl.ds(chunk * CHUNK, CHUNK)
            bias = [
                bias_ref[h, pl.ds(chunk * TILES + 42 - 14 * m, TILES)].reshape(CHUNK, 128)
                for m in range(4)
            ]
            scores = scores_ref[h, span, :] + jnp.concatenate(bias, axis=1)
            exponent = jnp.exp(scores - jnp.max(scores, -1, keepdims=True))
            probs_ref[h, span, :] = exponent.astype(BF16)

    def mix(h):
        ones = jnp.broadcast_to(head_lanes[h], (KEYS, CHAN))
        sides = jnp.concatenate([values_ref[...] * head_lanes[h], ones], axis=1)
        part = dot(probs_ref[h, 0:TOK, :], sides)
        mixed_ref[...] = part if h == 0 else mixed_ref[...] + part

    score(0)
    for h in range(HEADS):
        if h + 1 < HEADS:
            score(h + 1)
        if h > 0:
            mix(h - 1)
        weigh(h)
    queries_across = dot(query_weight_across, normed1, NT) + query_bias_across
    queries_across = (queries_across * SCALE).astype(BF16)
    mix(HEADS - 1)

    proj_weight = operand("proj_weight")
    proj_bias = operand("proj_bias")
    gain2 = operand("gain2")
    shift2 = operand("shift2")
    fc1_weight = operand("fc1_weight")
    fc1_bias = operand("fc1_bias")
    fc2_weight = operand("fc2_weight")
    fc2_bias = operand("fc2_bias")
    inv_total = 1.0 / mixed_ref[:, CHAN:]
    mixed = mixed_ref[:, :CHAN] * inv_total
    mixed_low = mixed.astype(BF16)
    branch = [(dot(mixed_low[part], proj_weight) + proj_bias).astype(BF16) for part in HALVES]
    ys = [frames[part] + branch[i].astype(F32) for i, part in enumerate(HALVES)]
    stats2 = [norm_stats(y) for y in ys]
    for i, part in enumerate(HALVES):
        normed2 = (stats2[i][0] * gain2 + shift2).astype(BF16)
        scores_ref[0, part, :] = dot(normed2, fc1_weight) + fc1_bias
    inv_total_across = inv_total.T
    for copy in goal_copies:
        copy.wait_recv()
    goal_local.wait()
    goal = joined(goal_in[...])
    grad_out = []
    for i, part in enumerate(HALVES):
        active, slope = gelu_parts(scores_ref[0, part, :])
        scores_ref[1, part, :] = slope
        grad_out.append(ys[i] + dot(active.astype(BF16), fc2_weight) + (fc2_bias - goal[part]))
    grad_pre = [
        (dot(grad_out[i].astype(BF16), fc2_weight, NT) * scores_ref[1, part, :]).astype(BF16)
        for i, part in enumerate(HALVES)
    ]
    grad_norm2 = [dot(grad, fc1_weight, NT) for grad in grad_pre]
    grad_ys = jnp.concatenate(
        [grad_out[i] + norm_backward(grad_norm2[i], *stats2[i], gain2) for i in range(2)], axis=0
    )

    grad_low = grad_ys.astype(BF16)
    grad_mixed = (dot(grad_low, proj_weight, NT) * inv_total).astype(BF16)
    grad_mixed_across = (dot(proj_weight, grad_low, NT) * inv_total_across).astype(BF16)
    mixed_grad_ref[...] = grad_mixed
    toward_ref[0:TOK, :] = grad_mixed.astype(F32) * mixed

    def score_grad(h):
        scores_ref[h, 0:TOK, :] = dot(mixed_grad_ref[...] * head_lanes[h], values_ref[...], NT)

    def weigh_grad(h):
        for chunk in range(ROWS // CHUNK):
            span = pl.ds(chunk * CHUNK, CHUNK)
            own = jnp.where(head_masks[h], toward_ref[span, :], 0.0)
            delta = jnp.sum(own, -1, keepdims=True)
            probs = probs_ref[h, span, :].astype(F32)
            grads_ref[h, span, :] = (probs * (scores_ref[h, span, :] - delta)).astype(BF16)

    def value_grad(h):
        rows = slice(h * HEAD, (h + 1) * HEAD)
        return dot(grad_mixed_across[rows], probs_ref[h, 0:TOK, :]).astype(BF16)

    def key_grad(h):
        rows = slice(h * HEAD, (h + 1) * HEAD)
        return dot(queries_across[rows], grads_ref[h, 0:TOK, :]).astype(BF16)

    def query_grad(h):
        part = dot(grads_ref[h, 0:TOK, :], keys_ref[...] * head_lanes[h])
        grad_queries_ref[...] = part if h == 0 else grad_queries_ref[...] + part

    grad_values = [None] * HEADS
    grad_keys = [None] * HEADS
    score_grad(0)
    for h in range(HEADS):
        if h + 1 < HEADS:
            score_grad(h + 1)
        grad_values[h] = value_grad(h)
        if h > 0:
            query_grad(h - 1)
            grad_keys[h - 1] = key_grad(h - 1)
        weigh_grad(h)
    grad_keys[HEADS - 1] = key_grad(HEADS - 1)
    query_grad(HEADS - 1)

    across = jnp.concatenate(grad_keys + grad_values, axis=0)
    grad_normed = unpad_keys(dot(qkv_weight[:, CHAN:], across).T)
    grad_queries = (grad_queries_ref[...] * SCALE).astype(BF16)
    grad_normed = grad_normed + dot(grad_queries, qkv_weight[:, :CHAN], NT)
    grad_normed = grad_normed.astype(BF16).astype(F32)
    result = grad_ys + norm_backward(grad_normed, normal1, inv_std1, gain1)

    result = result.reshape(WH, WW, WT, CHAN)
    back_out[:, :, 0] = result[:, :, :ST].astype(BF16)
    back_out[:, :, 1] = result[:, :, ST:].astype(BF16)
    for copy in back_copies:
        copy.start()
    back_local.start()
    for copy in back_copies:
        copy.wait_recv()
    back_local.wait()
    for copy in clip_copies + goal_copies + back_copies:
        copy.wait_send()


def shards(
    clip_tokens,
    target,
    norm1_gain,
    norm1_bias,
    qkv_weight,
    qkv_bias,
    bias_table,
    proj_weight,
    proj_bias,
    norm2_gain,
    norm2_bias,
    fc1_weight,
    fc1_bias,
    fc2_weight,
    fc2_bias,
):
    def by_place(tokens):
        return jnp.transpose(tokens, (1, 2, 3, 0, 4)).reshape(WH, WW, 2, ST, CHAN)

    named = {
        "table": bias_table.T,
        "gain1": norm1_gain.reshape(1, -1),
        "shift1": norm1_bias.reshape(1, -1),
        "qkv_weight": qkv_weight,
        "qkv_bias": qkv_bias.reshape(3, -1),
        "proj_weight": proj_weight,
        "proj_bias": proj_bias.reshape(1, -1),
        "gain2": norm2_gain.reshape(1, -1),
        "shift2": norm2_bias.reshape(1, -1),
        "fc1_weight": fc1_weight,
        "fc1_bias": fc1_bias.reshape(1, -1),
        "fc2_weight": fc2_weight,
        "fc2_bias": fc2_bias.reshape(1, -1),
    }
    operands = [named[name] for name in OPERANDS]
    inputs = [by_place(clip_tokens), by_place(target)] + operands
    plane = (2 * WH - 1) * (2 * WW - 1)
    out = pl.pallas_call(
        kernel,
        out_shape=pltpu.VMEM((WH, WW, 2, ST, CHAN), BF16),
        in_specs=[pl.BlockSpec(memory_space=pltpu.HBM)] * len(inputs),
        out_specs=pl.BlockSpec(memory_space=pltpu.VMEM),
        scratch_shapes=[pltpu.VMEM(x.shape, x.dtype) for x in operands]
        + [pltpu.SemaphoreType.DMA((len(operands),))]
        + [pltpu.VMEM((WH, WW, 2, ST, CHAN), BF16)] * 3
        + [
            pltpu.VMEM((HEADS * (2 * WT - 1), plane), F32),
            pltpu.VMEM((2 * WH - 1, HEADS * (2 * WT - 1), 128), F32),
            pltpu.VMEM((2 * WH - 1, WT, 128), F32),
            pltpu.VMEM((HEADS, (2 * WH - 1) * WW + 1, WT, 128), F32),
            pltpu.VMEM((HEADS, ROWS, KEYS), F32),
            pltpu.VMEM((HEADS, ROWS, KEYS), BF16),
            pltpu.VMEM((HEADS, ROWS, KEYS), BF16),
            pltpu.VMEM((TOK, CHAN), BF16),
            pltpu.VMEM((TOK, CHAN), BF16),
            pltpu.VMEM((KEYS, CHAN), BF16),
            pltpu.VMEM((KEYS, CHAN), BF16),
            pltpu.VMEM((KEYS, CHAN), BF16),
            pltpu.VMEM((TOK, 2 * CHAN), F32),
            pltpu.VMEM((TOK, CHAN), BF16),
            pltpu.VMEM((ROWS, CHAN), F32),
            pltpu.VMEM((TOK, CHAN), F32),
            pltpu.SemaphoreType.DMA((3, len(CUTS))),
            pltpu.SemaphoreType.DMA((3, len(AWAY))),
        ],
        compiler_params=pltpu.CompilerParams(
            collective_id=0, has_side_effects=True, vmem_limit_bytes=40 * 1024 * 1024
        ),
        name="window_block",
    )(*[pltpu.with_memory_space_constraint(x, pltpu.HBM) for x in inputs])
    return jnp.transpose(out.reshape(1, WH, WW, WT, CHAN), (3, 0, 1, 2, 4))


def solution(mesh):
    return jax.shard_map(
        shards,
        mesh=mesh,
        in_specs=(P("tm", "tile", None, None, None),) * 2 + (P(),) * 13,
        out_specs=P("tm", "tile", None, None, None),
        check_vma=False,
    )
```

```python
import itertools

import jax
import jax.numpy as jnp
import numpy as np
from jax import lax
from jax.experimental import pallas as pl
from jax.experimental.pallas import tpu as pltpu
from jax.sharding import PartitionSpec as P

HEADS = 4
HEAD = 32
CHAN = 128
FF = 512
WT = 8
WH = 7
WW = 7
ST = 4
SH = 3
SW = 3
TCOLS = 4
TROWS = 4
TM = 16
TOK = WT * WH * WW
KEYS = 512
ROWS = 400
CHUNK = 80
TILES = CHUNK // WT

EPSILON = 1e-05
MASKED = -1000000000.0
INV_ROOT_TAU = 0.3989422804014327
ERF_STEP = 0.3275911 * 0.7071067811865476
ERF_TERMS = (0.254829592, -0.284496736, 1.421413741, -1.453152027, 1.061405429)
SCALE = HEAD ** (-0.5)
LOG2E = 1.4426950408889634

F32 = jnp.float32
BF16 = jnp.bfloat16
MESH = pl.DeviceIdType.MESH


CUTS = sorted(itertools.product(range(2), range(2), range(2)), reverse=True)
AWAY = CUTS[:-1]
HALVES = (slice(0, 192), slice(192, TOK))
QUARTERS = (slice(0, 96), slice(96, 192), slice(192, 288), slice(288, TOK))


def box(cut, rolled):
    et, er, ec = cut
    if rolled:
        rows, cols, half = (WH - SH if er else 0), (WW - SW if ec else 0), et
    else:
        rows, cols, half = (0 if er else SH), (0 if ec else SW), 1 - et
    return (pl.ds(rows, SH if er else WH - SH), pl.ds(cols, SW if ec else WW - SW), half)


def dot(a, b, dims=((1,), (0,))):
    return lax.dot_general(a, b, (dims, ((), ())), preferred_element_type=F32)


NT = ((1,), (1,))


def row_mean(values):
    return jnp.sum(values, -1, keepdims=True) * (1.0 / CHAN)


def norm_stats(values):
    center = values - row_mean(values)
    inv_std = lax.rsqrt(row_mean(center * center) + EPSILON)
    return center * inv_std, inv_std


def norm_backward(grad_out, normal, inv_std, gain):
    scaled = grad_out * gain
    return inv_std * (scaled - row_mean(scaled) - normal * row_mean(scaled * normal))


def iota(shape, dim):
    return lax.broadcasted_iota(jnp.int32, shape, dim)


def neighbour(sign, cut):
    time_pos = lax.axis_index("tm")
    tile_pos = lax.axis_index("tile")
    row, col = tile_pos // TCOLS, tile_pos % TCOLS
    et, er, ec = cut
    to_time = (time_pos + TM + sign * et) % TM
    to_row = (row + TROWS + sign * er) % TROWS
    to_col = (col + TCOLS + sign * ec) % TCOLS
    return {"tm": to_time, "tile": to_row * TCOLS + to_col}


def exchange(src, dst, send_sems, recv_sems, to_window):
    remote = [
        pltpu.make_async_remote_copy(
            src_ref=src.at[box(cut, not to_window)],
            dst_ref=dst.at[box(cut, to_window)],
            send_sem=send_sems.at[i],
            recv_sem=recv_sems.at[i],
            device_id=neighbour(-1 if to_window else 1, cut),
            device_id_type=MESH,
        )
        for i, cut in enumerate(AWAY)
    ]
    local = pltpu.make_async_copy(
        src.at[box(CUTS[-1], not to_window)],
        dst.at[box(CUTS[-1], to_window)],
        send_sems.at[len(AWAY)],
    )
    return remote, local


def joined(halves):
    halves = halves.astype(F32).reshape(WH * WW, 2, ST, CHAN)
    return jnp.concatenate([halves[:, 0], halves[:, 1]], axis=1).reshape(TOK, CHAN)


def spread_bias(table, slab_ref, spread_ref):
    time_span, row_span, col_span = 2 * WT - 1, 2 * WH - 1, 2 * WW - 1
    plane = row_span * col_span
    for d in range(time_span):
        slab_ref[HEADS * d : HEADS * (d + 1), :] = table[:, d * plane : (d + 1) * plane]
    slabs = slab_ref[...] * LOG2E
    high = slabs.astype(BF16)
    rest = slabs - high.astype(F32)
    middle = rest.astype(BF16)
    low = (rest - middle.astype(F32)).astype(BF16)
    lanes = iota((1, row_span * 128), 1)
    slot = lanes % 128 // WT
    wanted = jnp.where(slot < col_span, lanes // 128 * col_span + (col_span - 1) - slot, -1)
    pick = (iota((plane, row_span * 128), 0) == wanted).astype(F32).astype(BF16)
    spread = (dot(low, pick) + dot(middle, pick)) + dot(high, pick)
    for p in range(row_span):
        spread_ref[p] = spread[:, p * 128 : (p + 1) * 128]


def fill_bias(spread_ref, skew_ref, bias_ref):
    row_span = 2 * WH - 1
    lane_time = iota((WT, 128), 1) % WT
    first = iota((WT, 128), 1) < 64

    def fill_head(h, _):
        for p in range(row_span):
            skewed = None
            for a in range(WT):
                rows = spread_ref[p, pl.ds((WT - 1 - a) * HEADS + h, WT, stride=HEADS), :]
                skewed = rows if skewed is None else jnp.where(lane_time == a, rows, skewed)
            skew_ref[p] = skewed
        for d in range(row_span):
            one, two = skew_ref[d], skew_ref[max(d - 1, 0)]
            for c in range(WW):
                shift = WT * (WW - 1 - c)
                bias_ref[h, d * WW + c] = jnp.where(
                    first,
                    one if shift == 0 else pltpu.roll(one, 128 - shift, 1),
                    pltpu.roll(two, 64 - shift, 1),
                )
        return _

    lax.fori_loop(0, HEADS, fill_head, 0)


def gelu_parts(pre_act):
    bell = jnp.exp2((-0.5 * LOG2E) * pre_act * pre_act)
    step = 1.0 / (1.0 + ERF_STEP * jnp.abs(pre_act))
    tail = ERF_TERMS[4]
    for term in ERF_TERMS[3::-1]:
        tail = tail * step + term
    tail = tail * step * (0.5 * bell)
    share = jnp.where(pre_act < 0.0, tail, 1.0 - tail)
    return pre_act * share, share + pre_act * (INV_ROOT_TAU * bell)


def region_classes(row, col, time):
    last_time = lax.axis_index("tm") == TM - 1
    last_row = lax.axis_index("tile") // TCOLS == TROWS - 1
    last_col = lax.axis_index("tile") % TCOLS == TCOLS - 1
    return (
        jnp.where(time >= ST, jnp.where(last_time, 4, 0), 0)
        + jnp.where(row >= WH - SH, jnp.where(last_row, 2, 0), 0)
        + jnp.where(col >= WW - SW, jnp.where(last_col, 1, 0), 0)
    )


def pad_keys(values):
    blocks = values.reshape(WH, WW, WT, CHAN)
    blocks = jnp.concatenate([blocks, jnp.zeros((WH, 1, WT, CHAN), values.dtype)], axis=1)
    blocks = jnp.concatenate([blocks, jnp.zeros((1, 8, WT, CHAN), values.dtype)], axis=0)
    return blocks.reshape(KEYS, CHAN)


def unpad_keys(values):
    return values.reshape(8, 8, WT, CHAN)[:WH, :WW].reshape(TOK, CHAN)


OPERANDS = (
    "table",
    "gain1",
    "shift1",
    "qkv_weight",
    "qkv_bias",
    "proj_weight",
    "proj_bias",
    "gain2",
    "shift2",
    "fc1_weight",
    "fc1_bias",
    "fc2_weight",
    "fc2_bias",
)


def kernel(*refs):
    count = len(OPERANDS)
    clip_ref, goal_ref, *sources = refs[: count + 2]
    out_ref = refs[count + 2]
    held = refs[count + 3 : 2 * count + 3]
    (
        load_sems,
        clip_in,
        goal_in,
        back_out,
        slab_ref,
        spread_ref,
        skew_ref,
        bias_ref,
        scores_ref,
        probs_ref,
        grads_ref,
        queries_ref,
        classes_ref,
        keys_ref,
        barred_ref,
        values_ref,
        mixed_ref,
        mixed_grad_ref,
        toward_ref,
        grad_queries_ref,
        send_sems,
        recv_sems,
    ) = refs[2 * count + 3 :]

    loads = {}

    def load(i):
        name = OPERANDS[i]
        loads[name] = (pltpu.make_async_copy(sources[i], held[i], load_sems.at[i]), held[i])
        loads[name][0].start()

    barrier = pltpu.get_barrier_semaphore()
    for cut in AWAY:
        pl.semaphore_signal(barrier, inc=1, device_id=neighbour(1, cut), device_id_type=MESH)
    clip_copies, clip_local = exchange(clip_ref, clip_in, send_sems.at[0], recv_sems.at[0], True)
    goal_copies, goal_local = exchange(goal_ref, goal_in, send_sems.at[1], recv_sems.at[1], True)
    back_copies, back_local = exchange(back_out, out_ref, send_sems.at[2], recv_sems.at[2], False)
    clip_local.start()
    for i in range(count):
        load(i)
    goal_local.start()

    def operand(name):
        copy, ref = loads[name]
        copy.wait()
        return ref[...]

    pl.semaphore_wait(barrier, len(AWAY))
    for copy in clip_copies:
        copy.start()

    spread_bias(operand("table"), slab_ref, spread_ref)
    for copy in clip_copies:
        copy.wait_send()
    for copy in goal_copies:
        copy.start()
    fill_bias(spread_ref, skew_ref, bias_ref)

    lane = iota((1, CHAN), 1)
    spot = lane % HEAD
    head_masks = [lane // HEAD == h for h in range(HEADS)]
    head_lanes = [mask.astype(F32).astype(BF16) for mask in head_masks]
    token = iota((TOK, 1), 0)
    query_class = region_classes(token // (WW * WT), token % (WW * WT) // WT, token % WT)
    classes_ref[...] = jnp.where(query_class == spot, 1.0, 0.0).astype(BF16)
    key = iota((KEYS, 1), 0)
    key_row, key_col = key // 64, key % 64 // WT
    key_class = region_classes(key_row, key_col, key % WT)
    key_class = jnp.where((key_row < WH) & (key_col < WW), key_class, 8)
    barred_ref[...] = jnp.where((key_class != spot) & (spot < 8), MASKED, 0.0).astype(BF16)

    gain1 = operand("gain1")
    shift1 = operand("shift1")
    qkv_weight = operand("qkv_weight")
    qkv_bias = operand("qkv_bias")
    query_weight_across = qkv_weight[:, :CHAN].T
    query_bias_across = jnp.broadcast_to(qkv_bias[0:1], (CHAN, CHAN)).T[:, 0:1]
    proj_weight = operand("proj_weight")
    proj_bias = operand("proj_bias")
    gain2 = operand("gain2")
    shift2 = operand("shift2")
    fc1_weight = operand("fc1_weight")
    fc1_bias = operand("fc1_bias")
    fc2_weight = operand("fc2_weight")
    fc2_bias = operand("fc2_bias")
    for copy in clip_copies:
        copy.wait_recv()
    clip_local.wait()
    frames = joined(clip_in[...])
    normal1, inv_std1 = norm_stats(frames)
    normed1 = (normal1 * gain1 + shift1).astype(BF16)
    projected = jnp.concatenate([dot(normed1[part], qkv_weight) for part in HALVES], axis=0)
    queries_ref[...] = ((projected[:, :CHAN] + qkv_bias[0:1]) * (SCALE * LOG2E)).astype(BF16)
    keys_ref[...] = pad_keys(projected[:, CHAN : 2 * CHAN] + qkv_bias[1:2]).astype(BF16)
    values_ref[...] = pad_keys(projected[:, 2 * CHAN :] + qkv_bias[2:3]).astype(BF16)

    def score(h):
        mine, spare = head_lanes[h], head_lanes[(h + 1) % HEADS]
        head_queries = queries_ref[...] * mine + classes_ref[...] * spare
        head_keys = keys_ref[...] * mine + barred_ref[...] * spare
        scores_ref[h, 0:TOK, :] = dot(head_queries, head_keys, NT)

    def weigh(h):
        for chunk in range(ROWS // CHUNK):
            span = pl.ds(chunk * CHUNK, CHUNK)
            bias = [
                bias_ref[h, pl.ds(chunk * TILES + 42 - 14 * m, TILES)].reshape(CHUNK, 128)
                for m in range(4)
            ]
            scores = scores_ref[h, span, :] + jnp.concatenate(bias, axis=1)
            exponent = jnp.exp2(scores - jnp.max(scores, -1, keepdims=True))
            probs_ref[h, span, :] = exponent.astype(BF16)

    def mix(h):
        ones = jnp.broadcast_to(head_lanes[h], (KEYS, CHAN))
        sides = jnp.concatenate([values_ref[...] * head_lanes[h], ones], axis=1)
        part = dot(probs_ref[h, 0:TOK, :], sides)
        mixed_ref[...] = part if h == 0 else mixed_ref[...] + part

    score(0)
    for h in range(HEADS):
        if h + 1 < HEADS:
            score(h + 1)
        if h > 0:
            mix(h - 1)
        weigh(h)
    queries_across = dot(query_weight_across, normed1, NT) + query_bias_across
    queries_across = (queries_across * SCALE).astype(BF16)
    mix(HEADS - 1)

    inv_total = 1.0 / mixed_ref[:, CHAN:]
    mixed = mixed_ref[:, :CHAN] * inv_total
    mixed_low = mixed.astype(BF16)
    branch = [(dot(mixed_low[part], proj_weight) + proj_bias).astype(BF16) for part in QUARTERS]
    ys = [frames[part] + branch[i].astype(F32) for i, part in enumerate(QUARTERS)]
    stats2 = [norm_stats(y) for y in ys]
    for i, part in enumerate(QUARTERS):
        normed2 = (stats2[i][0] * gain2 + shift2).astype(BF16)
        scores_ref[0, part, :] = dot(normed2, fc1_weight) + fc1_bias
    inv_total_across = inv_total.T
    outputs = []
    for i, part in enumerate(QUARTERS):
        active, slope = gelu_parts(scores_ref[0, part, :])
        scores_ref[1, part, :] = slope
        outputs.append(ys[i] + dot(active.astype(BF16), fc2_weight) + fc2_bias)
    for copy in goal_copies:
        copy.wait_recv()
    goal_local.wait()
    goal = joined(goal_in[...])
    grad_out = [outputs[i] - goal[part] for i, part in enumerate(QUARTERS)]
    grad_pre = [
        (dot(grad_out[i].astype(BF16), fc2_weight, NT) * scores_ref[1, part, :]).astype(BF16)
        for i, part in enumerate(QUARTERS)
    ]
    grad_norm2 = [dot(grad, fc1_weight, NT) for grad in grad_pre]
    grad_ys = jnp.concatenate(
        [grad_out[i] + norm_backward(grad_norm2[i], *stats2[i], gain2) for i in range(4)], axis=0
    )

    grad_low = grad_ys.astype(BF16)
    grad_mixed = (dot(grad_low, proj_weight, NT) * inv_total).astype(BF16)
    grad_mixed_across = (dot(proj_weight, grad_low, NT) * inv_total_across).astype(BF16)
    mixed_grad_ref[...] = grad_mixed
    toward_ref[0:TOK, :] = grad_mixed.astype(F32) * mixed

    def score_grad(h):
        scores_ref[h, 0:TOK, :] = dot(mixed_grad_ref[...] * head_lanes[h], values_ref[...], NT)

    def weigh_grad(h):
        for chunk in range(ROWS // CHUNK):
            span = pl.ds(chunk * CHUNK, CHUNK)
            own = jnp.where(head_masks[h], toward_ref[span, :], 0.0)
            delta = jnp.sum(own, -1, keepdims=True)
            excess = (scores_ref[h, span, :] - delta).astype(BF16)
            grads_ref[h, span, :] = probs_ref[h, span, :] * excess

    def value_grad(h):
        rows = slice(h * HEAD, (h + 1) * HEAD)
        return dot(grad_mixed_across[rows], probs_ref[h, 0:TOK, :]).astype(BF16)

    def key_grad(h):
        rows = slice(h * HEAD, (h + 1) * HEAD)
        return dot(queries_across[rows], grads_ref[h, 0:TOK, :]).astype(BF16)

    def query_grad(h):
        part = dot(grads_ref[h, 0:TOK, :], keys_ref[...] * head_lanes[h])
        grad_queries_ref[...] = part if h == 0 else grad_queries_ref[...] + part

    grad_values = [None] * HEADS
    grad_keys = [None] * HEADS
    score_grad(0)
    for h in range(HEADS):
        if h + 1 < HEADS:
            score_grad(h + 1)
        grad_values[h] = value_grad(h)
        if h > 0:
            query_grad(h - 1)
            grad_keys[h - 1] = key_grad(h - 1)
        weigh_grad(h)
    grad_keys[HEADS - 1] = key_grad(HEADS - 1)
    query_grad(HEADS - 1)

    across = jnp.concatenate(grad_keys + grad_values, axis=0)
    grad_normed = unpad_keys(dot(qkv_weight[:, CHAN:], across).T)
    grad_queries = (grad_queries_ref[...] * SCALE).astype(BF16)
    for group, rows in enumerate((range(0, WH - SH), range(WH - SH, WH))):
        part = slice(rows.start * WW * WT, rows.stop * WW * WT)
        total = grad_normed[part] + dot(grad_queries[part], qkv_weight[:, :CHAN], NT)
        total = total.astype(BF16).astype(F32)
        result = grad_ys[part] + norm_backward(total, normal1[part], inv_std1[part], gain1)
        result = result.reshape(len(rows), WW, WT, CHAN)
        back_out[rows.start : rows.stop, :, 0] = result[:, :, :ST].astype(BF16)
        back_out[rows.start : rows.stop, :, 1] = result[:, :, ST:].astype(BF16)
        for cut, copy in zip(AWAY, back_copies):
            if cut[1] == group:
                copy.start()
        if group == 0:
            back_local.start()
    for copy in back_copies:
        copy.wait_recv()
    back_local.wait()
    for copy in goal_copies + back_copies:
        copy.wait_send()


def shards(
    clip_tokens,
    target,
    norm1_gain,
    norm1_bias,
    qkv_weight,
    qkv_bias,
    bias_table,
    proj_weight,
    proj_bias,
    norm2_gain,
    norm2_bias,
    fc1_weight,
    fc1_bias,
    fc2_weight,
    fc2_bias,
):
    def by_place(tokens):
        return jnp.transpose(tokens, (1, 2, 3, 0, 4)).reshape(WH, WW, 2, ST, CHAN)

    named = {
        "table": bias_table.T,
        "gain1": norm1_gain.reshape(1, -1),
        "shift1": norm1_bias.reshape(1, -1),
        "qkv_weight": qkv_weight,
        "qkv_bias": qkv_bias.reshape(3, -1),
        "proj_weight": proj_weight,
        "proj_bias": proj_bias.reshape(1, -1),
        "gain2": norm2_gain.reshape(1, -1),
        "shift2": norm2_bias.reshape(1, -1),
        "fc1_weight": fc1_weight,
        "fc1_bias": fc1_bias.reshape(1, -1),
        "fc2_weight": fc2_weight,
        "fc2_bias": fc2_bias.reshape(1, -1),
    }
    operands = [named[name] for name in OPERANDS]
    inputs = [by_place(clip_tokens), by_place(target)] + operands
    plane = (2 * WH - 1) * (2 * WW - 1)
    out = pl.pallas_call(
        kernel,
        out_shape=pltpu.VMEM((WH, WW, 2, ST, CHAN), BF16),
        in_specs=[pl.BlockSpec(memory_space=pltpu.HBM)] * len(inputs),
        out_specs=pl.BlockSpec(memory_space=pltpu.VMEM),
        scratch_shapes=[pltpu.VMEM(x.shape, x.dtype) for x in operands]
        + [pltpu.SemaphoreType.DMA((len(operands),))]
        + [pltpu.VMEM((WH, WW, 2, ST, CHAN), BF16)] * 3
        + [
            pltpu.VMEM((HEADS * (2 * WT - 1), plane), F32),
            pltpu.VMEM((2 * WH - 1, HEADS * (2 * WT - 1), 128), F32),
            pltpu.VMEM((2 * WH - 1, WT, 128), F32),
            pltpu.VMEM((HEADS, (2 * WH - 1) * WW + 1, WT, 128), F32),
            pltpu.VMEM((HEADS, ROWS, KEYS), F32),
            pltpu.VMEM((HEADS, ROWS, KEYS), BF16),
            pltpu.VMEM((HEADS, ROWS, KEYS), BF16),
            pltpu.VMEM((TOK, CHAN), BF16),
            pltpu.VMEM((TOK, CHAN), BF16),
            pltpu.VMEM((KEYS, CHAN), BF16),
            pltpu.VMEM((KEYS, CHAN), BF16),
            pltpu.VMEM((KEYS, CHAN), BF16),
            pltpu.VMEM((TOK, 2 * CHAN), F32),
            pltpu.VMEM((TOK, CHAN), BF16),
            pltpu.VMEM((ROWS, CHAN), F32),
            pltpu.VMEM((TOK, CHAN), F32),
            pltpu.SemaphoreType.DMA((3, len(CUTS))),
            pltpu.SemaphoreType.DMA((3, len(AWAY))),
        ],
        compiler_params=pltpu.CompilerParams(
            collective_id=0, has_side_effects=True, vmem_limit_bytes=40 * 1024 * 1024
        ),
        name="window_block",
    )(*[pltpu.with_memory_space_constraint(x, pltpu.HBM) for x in inputs])
    return jnp.transpose(out.reshape(1, WH, WW, WT, CHAN), (3, 0, 1, 2, 4))


def solution(mesh):
    return jax.shard_map(
        shards,
        mesh=mesh,
        in_specs=(P("tm", "tile", None, None, None),) * 2 + (P(),) * 13,
        out_specs=P("tm", "tile", None, None, None),
        check_vma=False,
    )
```

```python
import itertools

import jax
import jax.numpy as jnp
import numpy as np
from jax import lax
from jax.experimental import pallas as pl
from jax.experimental.pallas import tpu as pltpu
from jax.sharding import PartitionSpec as P

HEADS = 4
HEAD = 32
CHAN = 128
FF = 512
WT = 8
WH = 7
WW = 7
ST = 4
SH = 3
SW = 3
TCOLS = 4
TROWS = 4
TM = 16
TOK = WT * WH * WW
KEYS = 512
ROWS = 400
CHUNK = 80
TILES = CHUNK // WT

EPSILON = 1e-05
MASKED = -1000000000.0
INV_ROOT_TAU = 0.3989422804014327
ERF_STEP = 0.3275911 * 0.7071067811865476
ERF_TERMS = (0.254829592, -0.284496736, 1.421413741, -1.453152027, 1.061405429)
SCALE = HEAD ** (-0.5)
LOG2E = 1.4426950408889634

F32 = jnp.float32
BF16 = jnp.bfloat16
MESH = pl.DeviceIdType.MESH


CUTS = sorted(itertools.product(range(2), range(2), range(2)), reverse=True)
AWAY = CUTS[:-1]
IN_TIME = [cut for cut in AWAY if cut[0]]
RELAY = TM // 2 - 1
HALVES = (slice(0, 192), slice(192, TOK))
QUARTERS = (slice(0, 96), slice(96, 192), slice(192, 288), slice(288, TOK))


def box(cut, rolled):
    et, er, ec = cut
    if rolled:
        rows, cols, half = (WH - SH if er else 0), (WW - SW if ec else 0), et
    else:
        rows, cols, half = (0 if er else SH), (0 if ec else SW), 1 - et
    return (pl.ds(rows, SH if er else WH - SH), pl.ds(cols, SW if ec else WW - SW), half)


def dot(a, b, dims=((1,), (0,))):
    return lax.dot_general(a, b, (dims, ((), ())), preferred_element_type=F32)


NT = ((1,), (1,))


def row_mean(values):
    return jnp.sum(values, -1, keepdims=True) * (1.0 / CHAN)


def norm_stats(values):
    center = values - row_mean(values)
    inv_std = lax.rsqrt(row_mean(center * center) + EPSILON)
    return center * inv_std, inv_std


def norm_backward(grad_out, normal, inv_std, gain):
    scaled = grad_out * gain
    return inv_std * (scaled - row_mean(scaled) - normal * row_mean(scaled * normal))


def iota(shape, dim):
    return lax.broadcasted_iota(jnp.int32, shape, dim)


def position():
    tile_pos = lax.axis_index("tile")
    return lax.axis_index("tm"), tile_pos // TCOLS, tile_pos % TCOLS


def device(time, row, col):
    return {"tm": time, "tile": row * TCOLS + col}


def neighbour(sign, cut):
    time, row, col = position()
    et, er, ec = cut
    return (
        (time + TM + sign * et) % TM,
        (row + TROWS + sign * er) % TROWS,
        (col + TCOLS + sign * ec) % TCOLS,
    )


def opposite(row):
    return (row + TROWS // 2) % TROWS


def sender(cut):
    time, row, col = neighbour(1, cut)
    if cut[0]:
        last = position()[0] == TM - 1
        time, row = jnp.where(last, RELAY, time), jnp.where(last, opposite(row), row)
    return device(time, row, col)


class Exchange:
    def __init__(self, src, dst, sems, to_window, relay=None):
        send_sems, recv_sems = sems[:2]
        self.to_window = to_window
        self.remote = {
            cut: pltpu.make_async_remote_copy(
                src_ref=src.at[box(cut, not to_window)],
                dst_ref=dst.at[box(cut, to_window)],
                send_sem=send_sems.at[i],
                recv_sem=recv_sems.at[i],
                device_id=device(*neighbour(-1 if to_window else 1, cut)),
                device_id_type=MESH,
            )
            for i, cut in enumerate(AWAY)
        }
        self.local = pltpu.make_async_copy(
            src.at[box(CUTS[-1], not to_window)],
            dst.at[box(CUTS[-1], to_window)],
            send_sems.at[len(AWAY)],
        )
        if not to_window:
            return
        relay_sems, onward_sems = sems[2:]
        self.time, row, col = position()
        self.hand_over = pltpu.make_async_remote_copy(
            src_ref=src.at[:, :, 0],
            dst_ref=relay,
            send_sem=relay_sems.at[0],
            recv_sem=relay_sems.at[1],
            device_id=device(RELAY, opposite(row), col),
            device_id_type=MESH,
        )
        self.onward = [
            pltpu.make_async_remote_copy(
                src_ref=relay.at[box(cut, False)[:2]],
                dst_ref=dst.at[box(cut, True)],
                send_sem=onward_sems.at[i],
                recv_sem=recv_sems.at[AWAY.index(cut)],
                device_id=device(
                    TM - 1,
                    (opposite(row) + TROWS - cut[1]) % TROWS,
                    (col + TCOLS - cut[2]) % TCOLS,
                ),
                device_id_type=MESH,
            )
            for i, cut in enumerate(IN_TIME)
        ]

    def start(self):
        @pl.when(self.time == 0)
        def _():
            self.hand_over.start()

        @pl.when(self.time != 0)
        def _():
            for cut in IN_TIME:
                self.remote[cut].start()

        for cut in AWAY:
            if not cut[0]:
                self.remote[cut].start()

    def pass_on(self):
        @pl.when(self.time == RELAY)
        def _():
            self.hand_over.wait_recv()
            for copy in self.onward:
                copy.start()

    def wait_sent(self):
        @pl.when(self.time == 0)
        def _():
            self.hand_over.wait_send()

        @pl.when(self.time != 0)
        def _():
            for cut in IN_TIME:
                self.remote[cut].wait_send()

        for cut in AWAY:
            if not cut[0]:
                self.remote[cut].wait_send()

    def wait_passed_on(self):
        @pl.when(self.time == RELAY)
        def _():
            for copy in self.onward:
                copy.wait_send()

    def wait_received(self):
        for cut in AWAY:
            self.remote[cut].wait_recv()
        self.local.wait()


def joined(halves):
    halves = halves.astype(F32).reshape(WH * WW, 2, ST, CHAN)
    return jnp.concatenate([halves[:, 0], halves[:, 1]], axis=1).reshape(TOK, CHAN)


def spread_bias(table, slab_ref, spread_ref):
    time_span, row_span, col_span = 2 * WT - 1, 2 * WH - 1, 2 * WW - 1
    plane = row_span * col_span
    for d in range(time_span):
        slab_ref[HEADS * d : HEADS * (d + 1), :] = table[:, d * plane : (d + 1) * plane]
    slabs = slab_ref[...] * LOG2E
    high = slabs.astype(BF16)
    rest = slabs - high.astype(F32)
    middle = rest.astype(BF16)
    low = (rest - middle.astype(F32)).astype(BF16)
    lanes = iota((1, row_span * 128), 1)
    slot = lanes % 128 // WT
    wanted = jnp.where(slot < col_span, lanes // 128 * col_span + (col_span - 1) - slot, -1)
    pick = (iota((plane, row_span * 128), 0) == wanted).astype(F32).astype(BF16)
    spread = (dot(low, pick) + dot(middle, pick)) + dot(high, pick)
    for p in range(row_span):
        spread_ref[p] = spread[:, p * 128 : (p + 1) * 128]


def fill_bias(spread_ref, skew_ref, bias_ref):
    row_span = 2 * WH - 1
    lane_time = iota((WT, 128), 1) % WT
    first = iota((WT, 128), 1) < 64

    def fill_head(h, _):
        for p in range(row_span):
            skewed = None
            for a in range(WT):
                rows = spread_ref[p, pl.ds((WT - 1 - a) * HEADS + h, WT, stride=HEADS), :]
                skewed = rows if skewed is None else jnp.where(lane_time == a, rows, skewed)
            skew_ref[p] = skewed
        for d in range(row_span):
            one, two = skew_ref[d], skew_ref[max(d - 1, 0)]
            for c in range(WW):
                shift = WT * (WW - 1 - c)
                bias_ref[h, d * WW + c] = jnp.where(
                    first,
                    one if shift == 0 else pltpu.roll(one, 128 - shift, 1),
                    pltpu.roll(two, 64 - shift, 1),
                )
        return _

    lax.fori_loop(0, HEADS, fill_head, 0)


def gelu_parts(pre_act):
    bell = jnp.exp2((-0.5 * LOG2E) * pre_act * pre_act)
    step = 1.0 / (1.0 + ERF_STEP * jnp.abs(pre_act))
    tail = ERF_TERMS[4]
    for term in ERF_TERMS[3::-1]:
        tail = tail * step + term
    tail = tail * step * (0.5 * bell)
    share = jnp.where(pre_act < 0.0, tail, 1.0 - tail)
    return pre_act * share, share + pre_act * (INV_ROOT_TAU * bell)


def region_classes(row, col, time):
    last_time = lax.axis_index("tm") == TM - 1
    last_row = lax.axis_index("tile") // TCOLS == TROWS - 1
    last_col = lax.axis_index("tile") % TCOLS == TCOLS - 1
    return (
        jnp.where(time >= ST, jnp.where(last_time, 4, 0), 0)
        + jnp.where(row >= WH - SH, jnp.where(last_row, 2, 0), 0)
        + jnp.where(col >= WW - SW, jnp.where(last_col, 1, 0), 0)
    )


def pad_keys(values):
    blocks = values.reshape(WH, WW, WT, CHAN)
    blocks = jnp.concatenate([blocks, jnp.zeros((WH, 1, WT, CHAN), values.dtype)], axis=1)
    blocks = jnp.concatenate([blocks, jnp.zeros((1, 8, WT, CHAN), values.dtype)], axis=0)
    return blocks.reshape(KEYS, CHAN)


def unpad_keys(values):
    return values.reshape(8, 8, WT, CHAN)[:WH, :WW].reshape(TOK, CHAN)


OPERANDS = (
    "table",
    "gain1",
    "shift1",
    "qkv_weight",
    "qkv_bias",
    "proj_weight",
    "proj_bias",
    "gain2",
    "shift2",
    "fc1_weight",
    "fc1_bias",
    "fc2_weight",
    "fc2_bias",
)


def kernel(*refs):
    count = len(OPERANDS)
    clip_ref, goal_ref, *sources = refs[: count + 2]
    out_ref = refs[count + 2]
    held = refs[count + 3 : 2 * count + 3]
    (
        load_sems,
        clip_in,
        goal_in,
        back_out,
        clip_relay,
        goal_relay,
        slab_ref,
        spread_ref,
        skew_ref,
        bias_ref,
        scores_ref,
        probs_ref,
        grads_ref,
        queries_ref,
        classes_ref,
        keys_ref,
        barred_ref,
        values_ref,
        mixed_ref,
        mixed_grad_ref,
        toward_ref,
        grad_queries_ref,
        send_sems,
        recv_sems,
        relay_sems,
        onward_sems,
    ) = refs[2 * count + 3 :]

    loads = {}

    def load(i):
        name = OPERANDS[i]
        loads[name] = (pltpu.make_async_copy(sources[i], held[i], load_sems.at[i]), held[i])
        loads[name][0].start()

    time_pos, row_pos, col_pos = position()
    barrier = pltpu.get_barrier_semaphore()
    for cut in AWAY:
        pl.semaphore_signal(barrier, inc=1, device_id=sender(cut), device_id_type=MESH)

    @pl.when(time_pos == RELAY)
    def _():
        first_block = device(0, opposite(row_pos), col_pos)
        pl.semaphore_signal(barrier, inc=1, device_id=first_block, device_id_type=MESH)

    def sems_of(k):
        return send_sems.at[k], recv_sems.at[k], relay_sems.at[k], onward_sems.at[k]

    clip = Exchange(clip_ref, clip_in, sems_of(0), True, clip_relay)
    goal = Exchange(goal_ref, goal_in, sems_of(1), True, goal_relay)
    back = Exchange(back_out, out_ref, (send_sems.at[2], recv_sems.at[2]), False)
    clip.local.start()
    for i in range(count):
        load(i)
    goal.local.start()

    def operand(name):
        copy, ref = loads[name]
        copy.wait()
        return ref[...]

    targets = len(AWAY) + jnp.where(time_pos == RELAY, len(IN_TIME), 0)
    targets = targets - jnp.where(time_pos == 0, len(IN_TIME) - 1, 0)
    pl.semaphore_wait(barrier, targets)
    clip.start()
    clip.pass_on()
    spread_bias(operand("table"), slab_ref, spread_ref)
    clip.wait_sent()
    goal.start()
    fill_bias(spread_ref, skew_ref, bias_ref)
    goal.pass_on()

    lane = iota((1, CHAN), 1)
    spot = lane % HEAD
    head_masks = [lane // HEAD == h for h in range(HEADS)]
    head_lanes = [mask.astype(F32).astype(BF16) for mask in head_masks]
    token = iota((TOK, 1), 0)
    query_class = region_classes(token // (WW * WT), token % (WW * WT) // WT, token % WT)
    classes_ref[...] = jnp.where(query_class == spot, 1.0, 0.0).astype(BF16)
    key = iota((KEYS, 1), 0)
    key_row, key_col = key // 64, key % 64 // WT
    key_class = region_classes(key_row, key_col, key % WT)
    key_class = jnp.where((key_row < WH) & (key_col < WW), key_class, 8)
    barred_ref[...] = jnp.where((key_class != spot) & (spot < 8), MASKED, 0.0).astype(BF16)

    gain1 = operand("gain1")
    shift1 = operand("shift1")
    qkv_weight = operand("qkv_weight")
    qkv_bias = operand("qkv_bias")
    query_weight_across = qkv_weight[:, :CHAN].T
    query_bias_across = jnp.broadcast_to(qkv_bias[0:1], (CHAN, CHAN)).T[:, 0:1]
    proj_weight = operand("proj_weight")
    proj_bias = operand("proj_bias")
    gain2 = operand("gain2")
    shift2 = operand("shift2")
    fc1_weight = operand("fc1_weight")
    fc1_bias = operand("fc1_bias")
    fc2_weight = operand("fc2_weight")
    fc2_bias = operand("fc2_bias")
    clip.wait_received()
    frames = joined(clip_in[...])
    normal1, inv_std1 = norm_stats(frames)
    normed1 = (normal1 * gain1 + shift1).astype(BF16)
    projected = jnp.concatenate([dot(normed1[part], qkv_weight) for part in HALVES], axis=0)
    queries_ref[...] = ((projected[:, :CHAN] + qkv_bias[0:1]) * (SCALE * LOG2E)).astype(BF16)
    keys_ref[...] = pad_keys(projected[:, CHAN : 2 * CHAN] + qkv_bias[1:2]).astype(BF16)
    values_ref[...] = pad_keys(projected[:, 2 * CHAN :] + qkv_bias[2:3]).astype(BF16)

    def score(h):
        mine, spare = head_lanes[h], head_lanes[(h + 1) % HEADS]
        head_queries = queries_ref[...] * mine + classes_ref[...] * spare
        head_keys = keys_ref[...] * mine + barred_ref[...] * spare
        scores_ref[h, 0:TOK, :] = dot(head_queries, head_keys, NT)

    def weigh(h):
        for chunk in range(ROWS // CHUNK):
            span = pl.ds(chunk * CHUNK, CHUNK)
            bias = [
                bias_ref[h, pl.ds(chunk * TILES + 42 - 14 * m, TILES)].reshape(CHUNK, 128)
                for m in range(4)
            ]
            scores = scores_ref[h, span, :] + jnp.concatenate(bias, axis=1)
            exponent = jnp.exp2(scores - jnp.max(scores, -1, keepdims=True))
            probs_ref[h, span, :] = exponent.astype(BF16)

    def mix(h):
        ones = jnp.broadcast_to(head_lanes[h], (KEYS, CHAN))
        sides = jnp.concatenate([values_ref[...] * head_lanes[h], ones], axis=1)
        part = dot(probs_ref[h, 0:TOK, :], sides)
        mixed_ref[...] = part if h == 0 else mixed_ref[...] + part

    score(0)
    for h in range(HEADS):
        if h + 1 < HEADS:
            score(h + 1)
        if h > 0:
            mix(h - 1)
        weigh(h)
    queries_across = dot(query_weight_across, normed1, NT) + query_bias_across
    queries_across = (queries_across * SCALE).astype(BF16)
    mix(HEADS - 1)

    inv_total = 1.0 / mixed_ref[:, CHAN:]
    mixed = mixed_ref[:, :CHAN] * inv_total
    mixed_low = mixed.astype(BF16)
    branch = [(dot(mixed_low[part], proj_weight) + proj_bias).astype(BF16) for part in QUARTERS]
    ys = [frames[part] + branch[i].astype(F32) for i, part in enumerate(QUARTERS)]
    stats2 = [norm_stats(y) for y in ys]
    for i, part in enumerate(QUARTERS):
        normed2 = (stats2[i][0] * gain2 + shift2).astype(BF16)
        scores_ref[0, part, :] = dot(normed2, fc1_weight) + fc1_bias
    inv_total_across = inv_total.T
    outputs = []
    for i, part in enumerate(QUARTERS):
        active, slope = gelu_parts(scores_ref[0, part, :])
        scores_ref[1, part, :] = slope
        outputs.append(ys[i] + dot(active.astype(BF16), fc2_weight) + fc2_bias)
    goal.wait_received()
    wanted = joined(goal_in[...])
    grad_out = [outputs[i] - wanted[part] for i, part in enumerate(QUARTERS)]
    grad_pre = [
        (dot(grad_out[i].astype(BF16), fc2_weight, NT) * scores_ref[1, part, :]).astype(BF16)
        for i, part in enumerate(QUARTERS)
    ]
    grad_norm2 = [dot(grad, fc1_weight, NT) for grad in grad_pre]
    grad_ys = jnp.concatenate(
        [grad_out[i] + norm_backward(grad_norm2[i], *stats2[i], gain2) for i in range(4)], axis=0
    )

    grad_low = grad_ys.astype(BF16)
    grad_mixed = (dot(grad_low, proj_weight, NT) * inv_total).astype(BF16)
    grad_mixed_across = (dot(proj_weight, grad_low, NT) * inv_total_across).astype(BF16)
    mixed_grad_ref[...] = grad_mixed
    toward_ref[0:TOK, :] = grad_mixed.astype(F32) * mixed

    def score_grad(h):
        scores_ref[h, 0:TOK, :] = dot(mixed_grad_ref[...] * head_lanes[h], values_ref[...], NT)

    def weigh_grad(h):
        for chunk in range(ROWS // CHUNK):
            span = pl.ds(chunk * CHUNK, CHUNK)
            own = jnp.where(head_masks[h], toward_ref[span, :], 0.0)
            delta = jnp.sum(own, -1, keepdims=True)
            excess = (scores_ref[h, span, :] - delta).astype(BF16)
            grads_ref[h, span, :] = probs_ref[h, span, :] * excess

    def value_grad(h):
        rows = slice(h * HEAD, (h + 1) * HEAD)
        return dot(grad_mixed_across[rows], probs_ref[h, 0:TOK, :]).astype(BF16)

    def key_grad(h):
        rows = slice(h * HEAD, (h + 1) * HEAD)
        return dot(queries_across[rows], grads_ref[h, 0:TOK, :]).astype(BF16)

    def query_grad(h):
        part = dot(grads_ref[h, 0:TOK, :], keys_ref[...] * head_lanes[h])
        grad_queries_ref[...] = part if h == 0 else grad_queries_ref[...] + part

    grad_values = [None] * HEADS
    grad_keys = [None] * HEADS
    score_grad(0)
    for h in range(HEADS):
        if h + 1 < HEADS:
            score_grad(h + 1)
        grad_values[h] = value_grad(h)
        if h > 0:
            query_grad(h - 1)
            grad_keys[h - 1] = key_grad(h - 1)
        weigh_grad(h)
    grad_keys[HEADS - 1] = key_grad(HEADS - 1)
    query_grad(HEADS - 1)

    across = jnp.concatenate(grad_keys + grad_values, axis=0)
    grad_normed = unpad_keys(dot(qkv_weight[:, CHAN:], across).T)
    grad_queries = (grad_queries_ref[...] * SCALE).astype(BF16)
    for group, rows in enumerate((range(0, WH - SH), range(WH - SH, WH))):
        part = slice(rows.start * WW * WT, rows.stop * WW * WT)
        total = grad_normed[part] + dot(grad_queries[part], qkv_weight[:, :CHAN], NT)
        total = total.astype(BF16).astype(F32)
        result = grad_ys[part] + norm_backward(total, normal1[part], inv_std1[part], gain1)
        result = result.reshape(len(rows), WW, WT, CHAN)
        back_out[rows.start : rows.stop, :, 0] = result[:, :, :ST].astype(BF16)
        back_out[rows.start : rows.stop, :, 1] = result[:, :, ST:].astype(BF16)
        for cut in AWAY:
            if cut[1] == group:
                back.remote[cut].start()
        if group == 0:
            back.local.start()
    back.wait_received()
    goal.wait_sent()
    clip.wait_passed_on()
    goal.wait_passed_on()
    for cut in AWAY:
        back.remote[cut].wait_send()


def shards(
    clip_tokens,
    target,
    norm1_gain,
    norm1_bias,
    qkv_weight,
    qkv_bias,
    bias_table,
    proj_weight,
    proj_bias,
    norm2_gain,
    norm2_bias,
    fc1_weight,
    fc1_bias,
    fc2_weight,
    fc2_bias,
):
    def by_place(tokens):
        return jnp.transpose(tokens, (1, 2, 3, 0, 4)).reshape(WH, WW, 2, ST, CHAN)

    named = {
        "table": bias_table.T,
        "gain1": norm1_gain.reshape(1, -1),
        "shift1": norm1_bias.reshape(1, -1),
        "qkv_weight": qkv_weight,
        "qkv_bias": qkv_bias.reshape(3, -1),
        "proj_weight": proj_weight,
        "proj_bias": proj_bias.reshape(1, -1),
        "gain2": norm2_gain.reshape(1, -1),
        "shift2": norm2_bias.reshape(1, -1),
        "fc1_weight": fc1_weight,
        "fc1_bias": fc1_bias.reshape(1, -1),
        "fc2_weight": fc2_weight,
        "fc2_bias": fc2_bias.reshape(1, -1),
    }
    operands = [named[name] for name in OPERANDS]
    inputs = [by_place(clip_tokens), by_place(target)] + operands
    plane = (2 * WH - 1) * (2 * WW - 1)
    out = pl.pallas_call(
        kernel,
        out_shape=pltpu.VMEM((WH, WW, 2, ST, CHAN), BF16),
        in_specs=[pl.BlockSpec(memory_space=pltpu.HBM)] * len(inputs),
        out_specs=pl.BlockSpec(memory_space=pltpu.VMEM),
        scratch_shapes=[pltpu.VMEM(x.shape, x.dtype) for x in operands]
        + [pltpu.SemaphoreType.DMA((len(operands),))]
        + [pltpu.VMEM((WH, WW, 2, ST, CHAN), BF16)] * 3
        + [pltpu.VMEM((WH, WW, ST, CHAN), BF16)] * 2
        + [
            pltpu.VMEM((HEADS * (2 * WT - 1), plane), F32),
            pltpu.VMEM((2 * WH - 1, HEADS * (2 * WT - 1), 128), F32),
            pltpu.VMEM((2 * WH - 1, WT, 128), F32),
            pltpu.VMEM((HEADS, (2 * WH - 1) * WW + 1, WT, 128), F32),
            pltpu.VMEM((HEADS, ROWS, KEYS), F32),
            pltpu.VMEM((HEADS, ROWS, KEYS), BF16),
            pltpu.VMEM((HEADS, ROWS, KEYS), BF16),
            pltpu.VMEM((TOK, CHAN), BF16),
            pltpu.VMEM((TOK, CHAN), BF16),
            pltpu.VMEM((KEYS, CHAN), BF16),
            pltpu.VMEM((KEYS, CHAN), BF16),
            pltpu.VMEM((KEYS, CHAN), BF16),
            pltpu.VMEM((TOK, 2 * CHAN), F32),
            pltpu.VMEM((TOK, CHAN), BF16),
            pltpu.VMEM((ROWS, CHAN), F32),
            pltpu.VMEM((TOK, CHAN), F32),
            pltpu.SemaphoreType.DMA((3, len(CUTS))),
            pltpu.SemaphoreType.DMA((3, len(AWAY))),
            pltpu.SemaphoreType.DMA((2, 2)),
            pltpu.SemaphoreType.DMA((2, len(IN_TIME))),
        ],
        compiler_params=pltpu.CompilerParams(
            collective_id=0, has_side_effects=True, vmem_limit_bytes=40 * 1024 * 1024
        ),
        name="window_block",
    )(*[pltpu.with_memory_space_constraint(x, pltpu.HBM) for x in inputs])
    return jnp.transpose(out.reshape(1, WH, WW, WT, CHAN), (3, 0, 1, 2, 4))


def solution(mesh):
    return jax.shard_map(
        shards,
        mesh=mesh,
        in_specs=(P("tm", "tile", None, None, None),) * 2 + (P(),) * 13,
        out_specs=P("tm", "tile", None, None, None),
        check_vma=False,
    )
```

```python
import itertools

import jax
import jax.numpy as jnp
import numpy as np
from jax import lax
from jax.experimental import pallas as pl
from jax.experimental.pallas import tpu as pltpu
from jax.sharding import PartitionSpec as P

HEADS = 4
HEAD = 32
CHAN = 128
FF = 512
WT = 8
WH = 7
WW = 7
ST = 4
SH = 3
SW = 3
TCOLS = 4
TROWS = 4
TM = 16
TOK = WT * WH * WW
KEYS = 512
ROWS = 400
CHUNK = 80
TILES = CHUNK // WT

EPSILON = 1e-05
MASKED = -1000000000.0
INV_ROOT_TAU = 0.3989422804014327
ERF_STEP = 0.3275911 * 0.7071067811865476
ERF_TERMS = (0.254829592, -0.284496736, 1.421413741, -1.453152027, 1.061405429)
SCALE = HEAD ** (-0.5)
LOG2E = 1.4426950408889634

F32 = jnp.float32
BF16 = jnp.bfloat16
MESH = pl.DeviceIdType.MESH


CUTS = sorted(itertools.product(range(2), range(2), range(2)), reverse=True)
AWAY, STAYS = CUTS[:-1], CUTS[-1]
HALVES = (slice(0, 192), slice(192, TOK))
QUARTERS = (slice(0, 96), slice(96, 192), slice(192, 288), slice(288, TOK))


def box(cut, rolled):
    et, er, ec = cut
    if rolled:
        rows, cols, half = (WH - SH if er else 0), (WW - SW if ec else 0), et
    else:
        rows, cols, half = (0 if er else SH), (0 if ec else SW), 1 - et
    return (pl.ds(rows, SH if er else WH - SH), pl.ds(cols, SW if ec else WW - SW), half)


def dot(a, b, dims=((1,), (0,))):
    return lax.dot_general(a, b, (dims, ((), ())), preferred_element_type=F32)


NT = ((1,), (1,))


def row_mean(values):
    return jnp.sum(values, -1, keepdims=True) * (1.0 / CHAN)


def norm_stats(values):
    center = values - row_mean(values)
    inv_std = lax.rsqrt(row_mean(center * center) + EPSILON)
    return center * inv_std, inv_std


def norm_backward(grad_out, normal, inv_std, gain):
    scaled = grad_out * gain
    return inv_std * (scaled - row_mean(scaled) - normal * row_mean(scaled * normal))


def iota(shape, dim):
    return lax.broadcasted_iota(jnp.int32, shape, dim)


def position():
    tile_pos = lax.axis_index("tile")
    return lax.axis_index("tm"), tile_pos // TCOLS, tile_pos % TCOLS


def crosses(time):
    return time % (TM // 2) == TM // 2 - 1


def swapped(time, row):
    return jnp.where(crosses(time), (row + TROWS // 2) % TROWS, row)


def device(time, row, col):
    return {"tm": time, "tile": row * TCOLS + col}


def target(cut):
    time, row, col = position()
    time = (time + TM - cut[0]) % TM
    row = swapped(time, (row + TROWS - cut[1]) % TROWS)
    return device(time, row, (col + TCOLS - cut[2]) % TCOLS)


def source(cut):
    time, row, col = position()
    row = swapped(time, row)
    return device((time + cut[0]) % TM, (row + cut[1]) % TROWS, (col + cut[2]) % TCOLS)


class Exchange:
    def __init__(self, src, dst, send_sems, recv_sems, local_sem, to_window):
        self.away = crosses(position()[0])
        self.remote = {
            cut: pltpu.make_async_remote_copy(
                src_ref=src.at[box(cut, not to_window)],
                dst_ref=dst.at[box(cut, to_window)],
                send_sem=send_sems.at[i],
                recv_sem=recv_sems.at[i],
                device_id=target(cut) if to_window else source(cut),
                device_id_type=MESH,
            )
            for i, cut in enumerate(CUTS)
        }
        self.local = pltpu.make_async_copy(
            src.at[box(STAYS, not to_window)], dst.at[box(STAYS, to_window)], local_sem
        )

    def start(self, cuts):
        for cut in cuts:
            if cut == STAYS:
                pl.when(self.away)(self.remote[cut].start)
                pl.when(jnp.logical_not(self.away))(self.local.start)
            else:
                self.remote[cut].start()

    def wait_sent(self):
        for cut in AWAY:
            self.remote[cut].wait_send()
        pl.when(self.away)(self.remote[STAYS].wait_send)

    def wait_received(self):
        for cut in AWAY:
            self.remote[cut].wait_recv()
        pl.when(self.away)(self.remote[STAYS].wait_recv)
        pl.when(jnp.logical_not(self.away))(self.local.wait)


def joined(halves):
    halves = halves.astype(F32).reshape(WH * WW, 2, ST, CHAN)
    return jnp.concatenate([halves[:, 0], halves[:, 1]], axis=1).reshape(TOK, CHAN)


def spread_bias(table, slab_ref, spread_ref):
    time_span, row_span, col_span = 2 * WT - 1, 2 * WH - 1, 2 * WW - 1
    plane = row_span * col_span
    for d in range(time_span):
        slab_ref[HEADS * d : HEADS * (d + 1), :] = table[:, d * plane : (d + 1) * plane]
    slabs = slab_ref[...] * LOG2E
    high = slabs.astype(BF16)
    rest = slabs - high.astype(F32)
    middle = rest.astype(BF16)
    low = (rest - middle.astype(F32)).astype(BF16)
    lanes = iota((1, row_span * 128), 1)
    slot = lanes % 128 // WT
    wanted = jnp.where(slot < col_span, lanes // 128 * col_span + (col_span - 1) - slot, -1)
    pick = (iota((plane, row_span * 128), 0) == wanted).astype(F32).astype(BF16)
    spread = (dot(low, pick) + dot(middle, pick)) + dot(high, pick)
    for p in range(row_span):
        spread_ref[p] = spread[:, p * 128 : (p + 1) * 128]


def fill_bias(spread_ref, skew_ref, bias_ref):
    row_span = 2 * WH - 1
    lane_time = iota((WT, 128), 1) % WT
    first = iota((WT, 128), 1) < 64

    def fill_head(h, _):
        for p in range(row_span):
            skewed = None
            for a in range(WT):
                rows = spread_ref[p, pl.ds((WT - 1 - a) * HEADS + h, WT, stride=HEADS), :]
                skewed = rows if skewed is None else jnp.where(lane_time == a, rows, skewed)
            skew_ref[p] = skewed
        for d in range(row_span):
            one, two = skew_ref[d], skew_ref[max(d - 1, 0)]
            for c in range(WW):
                shift = WT * (WW - 1 - c)
                bias_ref[h, d * WW + c] = jnp.where(
                    first,
                    one if shift == 0 else pltpu.roll(one, 128 - shift, 1),
                    pltpu.roll(two, 64 - shift, 1),
                )
        return _

    lax.fori_loop(0, HEADS, fill_head, 0)


def gelu_parts(pre_act):
    bell = jnp.exp2((-0.5 * LOG2E) * pre_act * pre_act)
    step = 1.0 / (1.0 + ERF_STEP * jnp.abs(pre_act))
    tail = ERF_TERMS[4]
    for term in ERF_TERMS[3::-1]:
        tail = tail * step + term
    tail = tail * step * (0.5 * bell)
    share = jnp.where(pre_act < 0.0, tail, 1.0 - tail)
    return pre_act * share, share + pre_act * (INV_ROOT_TAU * bell)


def region_classes(row, col, time):
    time_pos, row_pos, col_pos = position()
    last_time = time_pos == TM - 1
    last_row = swapped(time_pos, row_pos) == TROWS - 1
    last_col = col_pos == TCOLS - 1
    return (
        jnp.where(time >= ST, jnp.where(last_time, 4, 0), 0)
        + jnp.where(row >= WH - SH, jnp.where(last_row, 2, 0), 0)
        + jnp.where(col >= WW - SW, jnp.where(last_col, 1, 0), 0)
    )


def pad_keys(values):
    blocks = values.reshape(WH, WW, WT, CHAN)
    blocks = jnp.concatenate([blocks, jnp.zeros((WH, 1, WT, CHAN), values.dtype)], axis=1)
    blocks = jnp.concatenate([blocks, jnp.zeros((1, 8, WT, CHAN), values.dtype)], axis=0)
    return blocks.reshape(KEYS, CHAN)


def unpad_keys(values):
    return values.reshape(8, 8, WT, CHAN)[:WH, :WW].reshape(TOK, CHAN)


OPERANDS = (
    "table",
    "gain1",
    "shift1",
    "qkv_weight",
    "qkv_bias",
    "proj_weight",
    "proj_bias",
    "gain2",
    "shift2",
    "fc1_weight",
    "fc1_bias",
    "fc2_weight",
    "fc2_bias",
)


def kernel(*refs):
    count = len(OPERANDS)
    clip_ref, goal_ref, *sources = refs[: count + 2]
    out_ref = refs[count + 2]
    held = refs[count + 3 : 2 * count + 3]
    (
        load_sems,
        clip_in,
        goal_in,
        back_out,
        slab_ref,
        spread_ref,
        skew_ref,
        bias_ref,
        scores_ref,
        probs_ref,
        grads_ref,
        queries_ref,
        classes_ref,
        keys_ref,
        barred_ref,
        values_ref,
        mixed_ref,
        mixed_grad_ref,
        toward_ref,
        grad_queries_ref,
        send_sems,
        recv_sems,
        local_sems,
    ) = refs[2 * count + 3 :]

    loads = {}

    def load(i):
        name = OPERANDS[i]
        loads[name] = (pltpu.make_async_copy(sources[i], held[i], load_sems.at[i]), held[i])
        loads[name][0].start()

    away = crosses(position()[0])
    barrier = pltpu.get_barrier_semaphore()
    for cut in AWAY:
        pl.semaphore_signal(barrier, inc=1, device_id=source(cut), device_id_type=MESH)

    @pl.when(away)
    def _():
        pl.semaphore_signal(barrier, inc=1, device_id=source(STAYS), device_id_type=MESH)

    clip, goal, back = (
        Exchange(src, dst, send_sems.at[k], recv_sems.at[k], local_sems.at[k], k < 2)
        for k, (src, dst) in enumerate(
            ((clip_ref, clip_in), (goal_ref, goal_in), (back_out, out_ref))
        )
    )
    for i in range(count):
        load(i)

    def operand(name):
        copy, ref = loads[name]
        copy.wait()
        return ref[...]

    pl.semaphore_wait(barrier, jnp.where(away, len(CUTS), len(AWAY)))
    clip.start(CUTS)
    spread_bias(operand("table"), slab_ref, spread_ref)
    clip.wait_sent()
    goal.start(CUTS)
    fill_bias(spread_ref, skew_ref, bias_ref)

    lane = iota((1, CHAN), 1)
    spot = lane % HEAD
    head_masks = [lane // HEAD == h for h in range(HEADS)]
    head_lanes = [mask.astype(F32).astype(BF16) for mask in head_masks]
    token = iota((TOK, 1), 0)
    query_class = region_classes(token // (WW * WT), token % (WW * WT) // WT, token % WT)
    classes_ref[...] = jnp.where(query_class == spot, 1.0, 0.0).astype(BF16)
    key = iota((KEYS, 1), 0)
    key_row, key_col = key // 64, key % 64 // WT
    key_class = region_classes(key_row, key_col, key % WT)
    key_class = jnp.where((key_row < WH) & (key_col < WW), key_class, 8)
    barred_ref[...] = jnp.where((key_class != spot) & (spot < 8), MASKED, 0.0).astype(BF16)

    gain1 = operand("gain1")
    shift1 = operand("shift1")
    qkv_weight = operand("qkv_weight")
    qkv_bias = operand("qkv_bias")
    query_weight_across = qkv_weight[:, :CHAN].T
    query_bias_across = jnp.broadcast_to(qkv_bias[0:1], (CHAN, CHAN)).T[:, 0:1]
    proj_weight = operand("proj_weight")
    proj_bias = operand("proj_bias")
    gain2 = operand("gain2")
    shift2 = operand("shift2")
    fc1_weight = operand("fc1_weight")
    fc1_bias = operand("fc1_bias")
    fc2_weight = operand("fc2_weight")
    fc2_bias = operand("fc2_bias")
    clip.wait_received()
    frames = joined(clip_in[...])
    normal1, inv_std1 = norm_stats(frames)
    normed1 = (normal1 * gain1 + shift1).astype(BF16)
    projected = jnp.concatenate([dot(normed1[part], qkv_weight) for part in HALVES], axis=0)
    queries_ref[...] = ((projected[:, :CHAN] + qkv_bias[0:1]) * (SCALE * LOG2E)).astype(BF16)
    keys_ref[...] = pad_keys(projected[:, CHAN : 2 * CHAN] + qkv_bias[1:2]).astype(BF16)
    values_ref[...] = pad_keys(projected[:, 2 * CHAN :] + qkv_bias[2:3]).astype(BF16)

    def score(h):
        mine, spare = head_lanes[h], head_lanes[(h + 1) % HEADS]
        head_queries = queries_ref[...] * mine + classes_ref[...] * spare
        head_keys = keys_ref[...] * mine + barred_ref[...] * spare
        scores_ref[h, 0:TOK, :] = dot(head_queries, head_keys, NT)

    def weigh(h):
        for chunk in range(ROWS // CHUNK):
            span = pl.ds(chunk * CHUNK, CHUNK)
            bias = [
                bias_ref[h, pl.ds(chunk * TILES + 42 - 14 * m, TILES)].reshape(CHUNK, 128)
                for m in range(4)
            ]
            scores = scores_ref[h, span, :] + jnp.concatenate(bias, axis=1)
            exponent = jnp.exp2(scores - jnp.max(scores, -1, keepdims=True))
            probs_ref[h, span, :] = exponent.astype(BF16)

    def mix(h):
        ones = jnp.broadcast_to(head_lanes[h], (KEYS, CHAN))
        sides = jnp.concatenate([values_ref[...] * head_lanes[h], ones], axis=1)
        part = dot(probs_ref[h, 0:TOK, :], sides)
        mixed_ref[...] = part if h == 0 else mixed_ref[...] + part

    score(0)
    for h in range(HEADS):
        if h + 1 < HEADS:
            score(h + 1)
        if h > 0:
            mix(h - 1)
        weigh(h)
    queries_across = dot(query_weight_across, normed1, NT) + query_bias_across
    queries_across = (queries_across * SCALE).astype(BF16)
    mix(HEADS - 1)

    inv_total = 1.0 / mixed_ref[:, CHAN:]
    mixed = mixed_ref[:, :CHAN] * inv_total
    mixed_low = mixed.astype(BF16)
    branch = [(dot(mixed_low[part], proj_weight) + proj_bias).astype(BF16) for part in QUARTERS]
    ys = [frames[part] + branch[i].astype(F32) for i, part in enumerate(QUARTERS)]
    stats2 = [norm_stats(y) for y in ys]
    for i, part in enumerate(QUARTERS):
        normed2 = (stats2[i][0] * gain2 + shift2).astype(BF16)
        scores_ref[0, part, :] = dot(normed2, fc1_weight) + fc1_bias
    inv_total_across = inv_total.T
    outputs = []
    for i, part in enumerate(QUARTERS):
        active, slope = gelu_parts(scores_ref[0, part, :])
        scores_ref[1, part, :] = slope
        outputs.append(ys[i] + dot(active.astype(BF16), fc2_weight) + fc2_bias)
    goal.wait_received()
    wanted = joined(goal_in[...])
    grad_out = [outputs[i] - wanted[part] for i, part in enumerate(QUARTERS)]
    grad_pre = [
        (dot(grad_out[i].astype(BF16), fc2_weight, NT) * scores_ref[1, part, :]).astype(BF16)
        for i, part in enumerate(QUARTERS)
    ]
    grad_norm2 = [dot(grad, fc1_weight, NT) for grad in grad_pre]
    grad_ys = jnp.concatenate(
        [grad_out[i] + norm_backward(grad_norm2[i], *stats2[i], gain2) for i in range(4)], axis=0
    )

    grad_low = grad_ys.astype(BF16)
    grad_mixed = (dot(grad_low, proj_weight, NT) * inv_total).astype(BF16)
    grad_mixed_across = (dot(proj_weight, grad_low, NT) * inv_total_across).astype(BF16)
    mixed_grad_ref[...] = grad_mixed
    toward_ref[0:TOK, :] = grad_mixed.astype(F32) * mixed

    def score_grad(h):
        scores_ref[h, 0:TOK, :] = dot(mixed_grad_ref[...] * head_lanes[h], values_ref[...], NT)

    def weigh_grad(h):
        for chunk in range(ROWS // CHUNK):
            span = pl.ds(chunk * CHUNK, CHUNK)
            own = jnp.where(head_masks[h], toward_ref[span, :], 0.0)
            delta = jnp.sum(own, -1, keepdims=True)
            excess = (scores_ref[h, span, :] - delta).astype(BF16)
            grads_ref[h, span, :] = probs_ref[h, span, :] * excess

    def value_grad(h):
        rows = slice(h * HEAD, (h + 1) * HEAD)
        return dot(grad_mixed_across[rows], probs_ref[h, 0:TOK, :]).astype(BF16)

    def key_grad(h):
        rows = slice(h * HEAD, (h + 1) * HEAD)
        return dot(queries_across[rows], grads_ref[h, 0:TOK, :]).astype(BF16)

    def query_grad(h):
        part = dot(grads_ref[h, 0:TOK, :], keys_ref[...] * head_lanes[h])
        grad_queries_ref[...] = part if h == 0 else grad_queries_ref[...] + part

    grad_values = [None] * HEADS
    grad_keys = [None] * HEADS
    score_grad(0)
    for h in range(HEADS):
        if h + 1 < HEADS:
            score_grad(h + 1)
        grad_values[h] = value_grad(h)
        if h > 0:
            query_grad(h - 1)
            grad_keys[h - 1] = key_grad(h - 1)
        weigh_grad(h)
    grad_keys[HEADS - 1] = key_grad(HEADS - 1)
    query_grad(HEADS - 1)

    across = jnp.concatenate(grad_keys + grad_values, axis=0)
    grad_normed = unpad_keys(dot(qkv_weight[:, CHAN:], across).T)
    grad_queries = (grad_queries_ref[...] * SCALE).astype(BF16)
    for group, rows in enumerate((range(0, WH - SH), range(WH - SH, WH))):
        part = slice(rows.start * WW * WT, rows.stop * WW * WT)
        total = grad_normed[part] + dot(grad_queries[part], qkv_weight[:, :CHAN], NT)
        total = total.astype(BF16).astype(F32)
        result = grad_ys[part] + norm_backward(total, normal1[part], inv_std1[part], gain1)
        result = result.reshape(len(rows), WW, WT, CHAN)
        back_out[rows.start : rows.stop, :, 0] = result[:, :, :ST].astype(BF16)
        back_out[rows.start : rows.stop, :, 1] = result[:, :, ST:].astype(BF16)
        back.start([cut for cut in CUTS if cut[1] == group])
    back.wait_received()
    goal.wait_sent()
    back.wait_sent()


def shards(
    clip_tokens,
    target,
    norm1_gain,
    norm1_bias,
    qkv_weight,
    qkv_bias,
    bias_table,
    proj_weight,
    proj_bias,
    norm2_gain,
    norm2_bias,
    fc1_weight,
    fc1_bias,
    fc2_weight,
    fc2_bias,
):
    def by_place(tokens):
        return jnp.transpose(tokens, (1, 2, 3, 0, 4)).reshape(WH, WW, 2, ST, CHAN)

    named = {
        "table": bias_table.T,
        "gain1": norm1_gain.reshape(1, -1),
        "shift1": norm1_bias.reshape(1, -1),
        "qkv_weight": qkv_weight,
        "qkv_bias": qkv_bias.reshape(3, -1),
        "proj_weight": proj_weight,
        "proj_bias": proj_bias.reshape(1, -1),
        "gain2": norm2_gain.reshape(1, -1),
        "shift2": norm2_bias.reshape(1, -1),
        "fc1_weight": fc1_weight,
        "fc1_bias": fc1_bias.reshape(1, -1),
        "fc2_weight": fc2_weight,
        "fc2_bias": fc2_bias.reshape(1, -1),
    }
    operands = [named[name] for name in OPERANDS]
    inputs = [by_place(clip_tokens), by_place(target)] + operands
    plane = (2 * WH - 1) * (2 * WW - 1)
    out = pl.pallas_call(
        kernel,
        out_shape=pltpu.VMEM((WH, WW, 2, ST, CHAN), BF16),
        in_specs=[pl.BlockSpec(memory_space=pltpu.HBM)] * len(inputs),
        out_specs=pl.BlockSpec(memory_space=pltpu.VMEM),
        scratch_shapes=[pltpu.VMEM(x.shape, x.dtype) for x in operands]
        + [pltpu.SemaphoreType.DMA((len(operands),))]
        + [pltpu.VMEM((WH, WW, 2, ST, CHAN), BF16)] * 3
        + [
            pltpu.VMEM((HEADS * (2 * WT - 1), plane), F32),
            pltpu.VMEM((2 * WH - 1, HEADS * (2 * WT - 1), 128), F32),
            pltpu.VMEM((2 * WH - 1, WT, 128), F32),
            pltpu.VMEM((HEADS, (2 * WH - 1) * WW + 1, WT, 128), F32),
            pltpu.VMEM((HEADS, ROWS, KEYS), F32),
            pltpu.VMEM((HEADS, ROWS, KEYS), BF16),
            pltpu.VMEM((HEADS, ROWS, KEYS), BF16),
            pltpu.VMEM((TOK, CHAN), BF16),
            pltpu.VMEM((TOK, CHAN), BF16),
            pltpu.VMEM((KEYS, CHAN), BF16),
            pltpu.VMEM((KEYS, CHAN), BF16),
            pltpu.VMEM((KEYS, CHAN), BF16),
            pltpu.VMEM((TOK, 2 * CHAN), F32),
            pltpu.VMEM((TOK, CHAN), BF16),
            pltpu.VMEM((ROWS, CHAN), F32),
            pltpu.VMEM((TOK, CHAN), F32),
            pltpu.SemaphoreType.DMA((3, len(CUTS))),
            pltpu.SemaphoreType.DMA((3, len(CUTS))),
            pltpu.SemaphoreType.DMA((3,)),
        ],
        compiler_params=pltpu.CompilerParams(
            collective_id=0, has_side_effects=True, vmem_limit_bytes=40 * 1024 * 1024
        ),
        name="window_block",
    )(*[pltpu.with_memory_space_constraint(x, pltpu.HBM) for x in inputs])
    return jnp.transpose(out.reshape(1, WH, WW, WT, CHAN), (3, 0, 1, 2, 4))


def solution(mesh):
    return jax.shard_map(
        shards,
        mesh=mesh,
        in_specs=(P("tm", "tile", None, None, None),) * 2 + (P(),) * 13,
        out_specs=P("tm", "tile", None, None, None),
        check_vma=False,
    )
```

```python
import itertools

import jax
import jax.numpy as jnp
import numpy as np
from jax import lax
from jax.experimental import pallas as pl
from jax.experimental.pallas import tpu as pltpu
from jax.sharding import PartitionSpec as P

HEADS = 4
HEAD = 32
CHAN = 128
FF = 512
WT = 8
WH = 7
WW = 7
ST = 4
SH = 3
SW = 3
TCOLS = 4
TROWS = 4
TM = 16
TOK = WT * WH * WW
KEYS = 512
ROWS = 400
CHUNK = 80
TILES = CHUNK // WT

EPSILON = 1e-05
MASKED = -1000000000.0
INV_ROOT_TAU = 0.3989422804014327
ERF_STEP = 0.3275911 * 0.7071067811865476
ERF_TERMS = (0.254829592, -0.284496736, 1.421413741, -1.453152027, 1.061405429)
SCALE = HEAD ** (-0.5)
LOG2E = 1.4426950408889634

F32 = jnp.float32
BF16 = jnp.bfloat16
MESH = pl.DeviceIdType.MESH


CUTS = sorted(itertools.product(range(2), range(2), range(2)), reverse=True)
AWAY, STAYS = CUTS[:-1], CUTS[-1]
IN_TIME = [cut for cut in AWAY if cut[0]]
RELAY = TM // 2 - 1
HALVES = (slice(0, 192), slice(192, TOK))
QUARTERS = (slice(0, 96), slice(96, 192), slice(192, 288), slice(288, TOK))


def box(cut, rolled):
    et, er, ec = cut
    if rolled:
        rows, cols, half = (WH - SH if er else 0), (WW - SW if ec else 0), et
    else:
        rows, cols, half = (0 if er else SH), (0 if ec else SW), 1 - et
    return (pl.ds(rows, SH if er else WH - SH), pl.ds(cols, SW if ec else WW - SW), half)


def dot(a, b, dims=((1,), (0,))):
    return lax.dot_general(a, b, (dims, ((), ())), preferred_element_type=F32)


NT = ((1,), (1,))


def row_mean(values):
    return jnp.sum(values, -1, keepdims=True) * (1.0 / CHAN)


def norm_stats(values):
    center = values - row_mean(values)
    inv_std = lax.rsqrt(row_mean(center * center) + EPSILON)
    return center * inv_std, inv_std


def norm_backward(grad_out, normal, inv_std, gain):
    scaled = grad_out * gain
    return inv_std * (scaled - row_mean(scaled) - normal * row_mean(scaled * normal))


def iota(shape, dim):
    return lax.broadcasted_iota(jnp.int32, shape, dim)


def position():
    tile_pos = lax.axis_index("tile")
    return lax.axis_index("tm"), tile_pos // TCOLS, tile_pos % TCOLS


def crosses(time):
    return time % (TM // 2) == TM // 2 - 1


def swapped(time, row):
    return jnp.where(crosses(time), (row + TROWS // 2) % TROWS, row)


def device(time, row, col):
    return {"tm": time, "tile": row * TCOLS + col}


def target(cut):
    time, row, col = position()
    time = (time + TM - cut[0]) % TM
    row = swapped(time, (row + TROWS - cut[1]) % TROWS)
    return device(time, row, (col + TCOLS - cut[2]) % TCOLS)


def source(cut):
    time, row, col = position()
    row = swapped(time, row)
    return device((time + cut[0]) % TM, (row + cut[1]) % TROWS, (col + cut[2]) % TCOLS)


def sender(cut):
    where = source(cut)
    if cut[0]:
        where["tm"] = jnp.where(position()[0] == TM - 1, RELAY, where["tm"])
    return where


class Exchange:
    def __init__(self, src, dst, sems, to_window, relay=None):
        send_sems, recv_sems, local_sem = sems[:3]
        self.time, row, col = position()
        self.away = crosses(self.time)
        self.remote = {
            cut: pltpu.make_async_remote_copy(
                src_ref=src.at[box(cut, not to_window)],
                dst_ref=dst.at[box(cut, to_window)],
                send_sem=send_sems.at[i],
                recv_sem=recv_sems.at[i],
                device_id=target(cut) if to_window else source(cut),
                device_id_type=MESH,
            )
            for i, cut in enumerate(CUTS)
        }
        self.local = pltpu.make_async_copy(
            src.at[box(STAYS, not to_window)], dst.at[box(STAYS, to_window)], local_sem
        )
        self.relayed = to_window
        if not to_window:
            return
        relay_sems, onward_sems = sems[3:]
        self.hand_over = pltpu.make_async_remote_copy(
            src_ref=src.at[:, :, 0],
            dst_ref=relay,
            send_sem=relay_sems.at[0],
            recv_sem=relay_sems.at[1],
            device_id=device(RELAY, row, col),
            device_id_type=MESH,
        )
        self.onward = [
            pltpu.make_async_remote_copy(
                src_ref=relay.at[box(cut, False)[:2]],
                dst_ref=dst.at[box(cut, True)],
                send_sem=onward_sems.at[i],
                recv_sem=recv_sems.at[CUTS.index(cut)],
                device_id=device(
                    TM - 1,
                    swapped(TM - 1, (row + TROWS - cut[1]) % TROWS),
                    (col + TCOLS - cut[2]) % TCOLS,
                ),
                device_id_type=MESH,
            )
            for i, cut in enumerate(IN_TIME)
        ]

    def over_time(self, act):
        if not self.relayed:
            for cut in IN_TIME:
                act(self.remote[cut])
            return

        @pl.when(self.time == 0)
        def _():
            act(self.hand_over)

        @pl.when(self.time != 0)
        def _():
            for cut in IN_TIME:
                act(self.remote[cut])

    def start(self, cuts):
        if self.relayed:
            self.over_time(lambda copy: copy.start())
            cuts = [cut for cut in cuts if not cut[0]]
        for cut in cuts:
            if cut == STAYS:
                pl.when(self.away)(self.remote[cut].start)
                pl.when(jnp.logical_not(self.away))(self.local.start)
            else:
                self.remote[cut].start()

    def pass_on(self):
        @pl.when(self.time == RELAY)
        def _():
            self.hand_over.wait_recv()
            for copy in self.onward:
                copy.start()

    def wait_passed_on(self):
        @pl.when(self.time == RELAY)
        def _():
            for copy in self.onward:
                copy.wait_send()

    def wait_sent(self):
        self.over_time(lambda copy: copy.wait_send())
        for cut in AWAY:
            if not cut[0]:
                self.remote[cut].wait_send()
        pl.when(self.away)(self.remote[STAYS].wait_send)

    def wait_received(self):
        for cut in AWAY:
            self.remote[cut].wait_recv()
        pl.when(self.away)(self.remote[STAYS].wait_recv)
        pl.when(jnp.logical_not(self.away))(self.local.wait)


def joined(halves):
    halves = halves.astype(F32).reshape(WH * WW, 2, ST, CHAN)
    return jnp.concatenate([halves[:, 0], halves[:, 1]], axis=1).reshape(TOK, CHAN)


def spread_bias(table, slab_ref, spread_ref):
    time_span, row_span, col_span = 2 * WT - 1, 2 * WH - 1, 2 * WW - 1
    plane = row_span * col_span
    for d in range(time_span):
        slab_ref[HEADS * d : HEADS * (d + 1), :] = table[:, d * plane : (d + 1) * plane]
    slabs = slab_ref[...] * LOG2E
    high = slabs.astype(BF16)
    rest = slabs - high.astype(F32)
    middle = rest.astype(BF16)
    low = (rest - middle.astype(F32)).astype(BF16)
    lanes = iota((1, row_span * 128), 1)
    slot = lanes % 128 // WT
    wanted = jnp.where(slot < col_span, lanes // 128 * col_span + (col_span - 1) - slot, -1)
    pick = (iota((plane, row_span * 128), 0) == wanted).astype(F32).astype(BF16)
    spread = (dot(low, pick) + dot(middle, pick)) + dot(high, pick)
    for p in range(row_span):
        spread_ref[p] = spread[:, p * 128 : (p + 1) * 128]


def fill_bias(spread_ref, skew_ref, bias_ref):
    row_span = 2 * WH - 1
    lane_time = iota((WT, 128), 1) % WT
    first = iota((WT, 128), 1) < 64

    def fill_head(h, _):
        for p in range(row_span):
            skewed = None
            for a in range(WT):
                rows = spread_ref[p, pl.ds((WT - 1 - a) * HEADS + h, WT, stride=HEADS), :]
                skewed = rows if skewed is None else jnp.where(lane_time == a, rows, skewed)
            skew_ref[p] = skewed
        for d in range(row_span):
            one, two = skew_ref[d], skew_ref[max(d - 1, 0)]
            for c in range(WW):
                shift = WT * (WW - 1 - c)
                bias_ref[h, d * WW + c] = jnp.where(
                    first,
                    one if shift == 0 else pltpu.roll(one, 128 - shift, 1),
                    pltpu.roll(two, 64 - shift, 1),
                )
        return _

    lax.fori_loop(0, HEADS, fill_head, 0)


def gelu_parts(pre_act):
    bell = jnp.exp2((-0.5 * LOG2E) * pre_act * pre_act)
    step = 1.0 / (1.0 + ERF_STEP * jnp.abs(pre_act))
    tail = ERF_TERMS[4]
    for term in ERF_TERMS[3::-1]:
        tail = tail * step + term
    tail = tail * step * (0.5 * bell)
    share = jnp.where(pre_act < 0.0, tail, 1.0 - tail)
    return pre_act * share, share + pre_act * (INV_ROOT_TAU * bell)


def region_classes(row, col, time):
    time_pos, row_pos, col_pos = position()
    last_time = time_pos == TM - 1
    last_row = swapped(time_pos, row_pos) == TROWS - 1
    last_col = col_pos == TCOLS - 1
    return (
        jnp.where(time >= ST, jnp.where(last_time, 4, 0), 0)
        + jnp.where(row >= WH - SH, jnp.where(last_row, 2, 0), 0)
        + jnp.where(col >= WW - SW, jnp.where(last_col, 1, 0), 0)
    )


def pad_keys(values):
    blocks = values.reshape(WH, WW, WT, CHAN)
    blocks = jnp.concatenate([blocks, jnp.zeros((WH, 1, WT, CHAN), values.dtype)], axis=1)
    blocks = jnp.concatenate([blocks, jnp.zeros((1, 8, WT, CHAN), values.dtype)], axis=0)
    return blocks.reshape(KEYS, CHAN)


def unpad_keys(values):
    return values.reshape(8, 8, WT, CHAN)[:WH, :WW].reshape(TOK, CHAN)


OPERANDS = (
    "table",
    "gain1",
    "shift1",
    "qkv_weight",
    "qkv_bias",
    "proj_weight",
    "proj_bias",
    "gain2",
    "shift2",
    "fc1_weight",
    "fc1_bias",
    "fc2_weight",
    "fc2_bias",
)


def kernel(*refs):
    count = len(OPERANDS)
    clip_ref, goal_ref, *sources = refs[: count + 2]
    out_ref = refs[count + 2]
    held = refs[count + 3 : 2 * count + 3]
    (
        load_sems,
        clip_in,
        goal_in,
        back_out,
        clip_relay,
        goal_relay,
        slab_ref,
        spread_ref,
        skew_ref,
        bias_ref,
        scores_ref,
        probs_ref,
        grads_ref,
        queries_ref,
        classes_ref,
        keys_ref,
        barred_ref,
        values_ref,
        mixed_ref,
        mixed_grad_ref,
        toward_ref,
        grad_queries_ref,
        send_sems,
        recv_sems,
        local_sems,
        relay_sems,
        onward_sems,
    ) = refs[2 * count + 3 :]

    loads = {}

    def load(i):
        name = OPERANDS[i]
        loads[name] = (pltpu.make_async_copy(sources[i], held[i], load_sems.at[i]), held[i])
        loads[name][0].start()

    time_pos, row_pos, col_pos = position()
    away = crosses(time_pos)
    barrier = pltpu.get_barrier_semaphore()
    for cut in AWAY:
        pl.semaphore_signal(barrier, inc=1, device_id=sender(cut), device_id_type=MESH)

    @pl.when(away)
    def _():
        pl.semaphore_signal(barrier, inc=1, device_id=source(STAYS), device_id_type=MESH)

    @pl.when(time_pos == RELAY)
    def _():
        first_block = device(0, row_pos, col_pos)
        pl.semaphore_signal(barrier, inc=1, device_id=first_block, device_id_type=MESH)

    sems = [
        (send_sems.at[k], recv_sems.at[k], local_sems.at[k], relay_sems.at[k], onward_sems.at[k])
        for k in range(2)
    ]
    clip = Exchange(clip_ref, clip_in, sems[0], True, clip_relay)
    goal = Exchange(goal_ref, goal_in, sems[1], True, goal_relay)
    back_sems = (send_sems.at[2], recv_sems.at[2], local_sems.at[2])
    back = Exchange(back_out, out_ref, back_sems, False)
    for i in range(count):
        load(i)

    def operand(name):
        copy, ref = loads[name]
        copy.wait()
        return ref[...]

    targets = jnp.where(away, len(CUTS), len(AWAY))
    targets = targets + jnp.where(time_pos == RELAY, len(IN_TIME), 0)
    targets = targets - jnp.where(time_pos == 0, len(IN_TIME) - 1, 0)
    pl.semaphore_wait(barrier, targets)
    clip.start(CUTS)
    clip.pass_on()
    spread_bias(operand("table"), slab_ref, spread_ref)
    clip.wait_sent()
    goal.start(CUTS)
    fill_bias(spread_ref, skew_ref, bias_ref)
    goal.pass_on()

    lane = iota((1, CHAN), 1)
    spot = lane % HEAD
    head_masks = [lane // HEAD == h for h in range(HEADS)]
    head_lanes = [mask.astype(F32).astype(BF16) for mask in head_masks]
    token = iota((TOK, 1), 0)
    query_class = region_classes(token // (WW * WT), token % (WW * WT) // WT, token % WT)
    classes_ref[...] = jnp.where(query_class == spot, 1.0, 0.0).astype(BF16)
    key = iota((KEYS, 1), 0)
    key_row, key_col = key // 64, key % 64 // WT
    key_class = region_classes(key_row, key_col, key % WT)
    key_class = jnp.where((key_row < WH) & (key_col < WW), key_class, 8)
    barred_ref[...] = jnp.where((key_class != spot) & (spot < 8), MASKED, 0.0).astype(BF16)

    gain1 = operand("gain1")
    shift1 = operand("shift1")
    qkv_weight = operand("qkv_weight")
    qkv_bias = operand("qkv_bias")
    query_weight_across = qkv_weight[:, :CHAN].T
    query_bias_across = jnp.broadcast_to(qkv_bias[0:1], (CHAN, CHAN)).T[:, 0:1]
    proj_weight = operand("proj_weight")
    proj_bias = operand("proj_bias")
    gain2 = operand("gain2")
    shift2 = operand("shift2")
    fc1_weight = operand("fc1_weight")
    fc1_bias = operand("fc1_bias")
    fc2_weight = operand("fc2_weight")
    fc2_bias = operand("fc2_bias")
    clip.wait_received()
    frames = joined(clip_in[...])
    normal1, inv_std1 = norm_stats(frames)
    normed1 = (normal1 * gain1 + shift1).astype(BF16)
    projected = jnp.concatenate([dot(normed1[part], qkv_weight) for part in HALVES], axis=0)
    queries_ref[...] = ((projected[:, :CHAN] + qkv_bias[0:1]) * (SCALE * LOG2E)).astype(BF16)
    keys_ref[...] = pad_keys(projected[:, CHAN : 2 * CHAN] + qkv_bias[1:2]).astype(BF16)
    values_ref[...] = pad_keys(projected[:, 2 * CHAN :] + qkv_bias[2:3]).astype(BF16)

    def score(h):
        mine, spare = head_lanes[h], head_lanes[(h + 1) % HEADS]
        head_queries = queries_ref[...] * mine + classes_ref[...] * spare
        head_keys = keys_ref[...] * mine + barred_ref[...] * spare
        scores_ref[h, 0:TOK, :] = dot(head_queries, head_keys, NT)

    def weigh(h):
        for chunk in range(ROWS // CHUNK):
            span = pl.ds(chunk * CHUNK, CHUNK)
            bias = [
                bias_ref[h, pl.ds(chunk * TILES + 42 - 14 * m, TILES)].reshape(CHUNK, 128)
                for m in range(4)
            ]
            scores = scores_ref[h, span, :] + jnp.concatenate(bias, axis=1)
            exponent = jnp.exp2(scores - jnp.max(scores, -1, keepdims=True))
            probs_ref[h, span, :] = exponent.astype(BF16)

    def mix(h):
        ones = jnp.broadcast_to(head_lanes[h], (KEYS, CHAN))
        sides = jnp.concatenate([values_ref[...] * head_lanes[h], ones], axis=1)
        part = dot(probs_ref[h, 0:TOK, :], sides)
        mixed_ref[...] = part if h == 0 else mixed_ref[...] + part

    score(0)
    for h in range(HEADS):
        if h + 1 < HEADS:
            score(h + 1)
        if h > 0:
            mix(h - 1)
        weigh(h)
    queries_across = dot(query_weight_across, normed1, NT) + query_bias_across
    queries_across = (queries_across * SCALE).astype(BF16)
    mix(HEADS - 1)

    inv_total = 1.0 / mixed_ref[:, CHAN:]
    mixed = mixed_ref[:, :CHAN] * inv_total
    mixed_low = mixed.astype(BF16)
    branch = [(dot(mixed_low[part], proj_weight) + proj_bias).astype(BF16) for part in QUARTERS]
    ys = [frames[part] + branch[i].astype(F32) for i, part in enumerate(QUARTERS)]
    stats2 = [norm_stats(y) for y in ys]
    for i, part in enumerate(QUARTERS):
        normed2 = (stats2[i][0] * gain2 + shift2).astype(BF16)
        scores_ref[0, part, :] = dot(normed2, fc1_weight) + fc1_bias
    inv_total_across = inv_total.T
    outputs = []
    for i, part in enumerate(QUARTERS):
        active, slope = gelu_parts(scores_ref[0, part, :])
        scores_ref[1, part, :] = slope
        outputs.append(ys[i] + dot(active.astype(BF16), fc2_weight) + fc2_bias)
    goal.wait_received()
    wanted = joined(goal_in[...])
    grad_out = [outputs[i] - wanted[part] for i, part in enumerate(QUARTERS)]
    grad_pre = [
        (dot(grad_out[i].astype(BF16), fc2_weight, NT) * scores_ref[1, part, :]).astype(BF16)
        for i, part in enumerate(QUARTERS)
    ]
    grad_norm2 = [dot(grad, fc1_weight, NT) for grad in grad_pre]
    grad_ys = jnp.concatenate(
        [grad_out[i] + norm_backward(grad_norm2[i], *stats2[i], gain2) for i in range(4)], axis=0
    )

    grad_low = grad_ys.astype(BF16)
    grad_mixed = (dot(grad_low, proj_weight, NT) * inv_total).astype(BF16)
    grad_mixed_across = (dot(proj_weight, grad_low, NT) * inv_total_across).astype(BF16)
    mixed_grad_ref[...] = grad_mixed
    toward_ref[0:TOK, :] = grad_mixed.astype(F32) * mixed

    def score_grad(h):
        scores_ref[h, 0:TOK, :] = dot(mixed_grad_ref[...] * head_lanes[h], values_ref[...], NT)

    def weigh_grad(h):
        for chunk in range(ROWS // CHUNK):
            span = pl.ds(chunk * CHUNK, CHUNK)
            own = jnp.where(head_masks[h], toward_ref[span, :], 0.0)
            delta = jnp.sum(own, -1, keepdims=True)
            excess = (scores_ref[h, span, :] - delta).astype(BF16)
            grads_ref[h, span, :] = probs_ref[h, span, :] * excess

    def value_grad(h):
        rows = slice(h * HEAD, (h + 1) * HEAD)
        return dot(grad_mixed_across[rows], probs_ref[h, 0:TOK, :]).astype(BF16)

    def key_grad(h):
        rows = slice(h * HEAD, (h + 1) * HEAD)
        return dot(queries_across[rows], grads_ref[h, 0:TOK, :]).astype(BF16)

    def query_grad(h):
        part = dot(grads_ref[h, 0:TOK, :], keys_ref[...] * head_lanes[h])
        grad_queries_ref[...] = part if h == 0 else grad_queries_ref[...] + part

    grad_values = [None] * HEADS
    grad_keys = [None] * HEADS
    score_grad(0)
    for h in range(HEADS):
        if h + 1 < HEADS:
            score_grad(h + 1)
        grad_values[h] = value_grad(h)
        if h > 0:
            query_grad(h - 1)
            grad_keys[h - 1] = key_grad(h - 1)
        weigh_grad(h)
    grad_keys[HEADS - 1] = key_grad(HEADS - 1)
    query_grad(HEADS - 1)

    across = jnp.concatenate(grad_keys + grad_values, axis=0)
    grad_normed = unpad_keys(dot(qkv_weight[:, CHAN:], across).T)
    grad_queries = (grad_queries_ref[...] * SCALE).astype(BF16)
    for group, rows in enumerate((range(0, WH - SH), range(WH - SH, WH))):
        part = slice(rows.start * WW * WT, rows.stop * WW * WT)
        total = grad_normed[part] + dot(grad_queries[part], qkv_weight[:, :CHAN], NT)
        total = total.astype(BF16).astype(F32)
        result = grad_ys[part] + norm_backward(total, normal1[part], inv_std1[part], gain1)
        result = result.reshape(len(rows), WW, WT, CHAN)
        back_out[rows.start : rows.stop, :, 0] = result[:, :, :ST].astype(BF16)
        back_out[rows.start : rows.stop, :, 1] = result[:, :, ST:].astype(BF16)
        back.start([cut for cut in CUTS if cut[1] == group])
    back.wait_received()
    goal.wait_sent()
    clip.wait_passed_on()
    goal.wait_passed_on()
    back.wait_sent()


def shards(
    clip_tokens,
    target,
    norm1_gain,
    norm1_bias,
    qkv_weight,
    qkv_bias,
    bias_table,
    proj_weight,
    proj_bias,
    norm2_gain,
    norm2_bias,
    fc1_weight,
    fc1_bias,
    fc2_weight,
    fc2_bias,
):
    def by_place(tokens):
        return jnp.transpose(tokens, (1, 2, 3, 0, 4)).reshape(WH, WW, 2, ST, CHAN)

    named = {
        "table": bias_table.T,
        "gain1": norm1_gain.reshape(1, -1),
        "shift1": norm1_bias.reshape(1, -1),
        "qkv_weight": qkv_weight,
        "qkv_bias": qkv_bias.reshape(3, -1),
        "proj_weight": proj_weight,
        "proj_bias": proj_bias.reshape(1, -1),
        "gain2": norm2_gain.reshape(1, -1),
        "shift2": norm2_bias.reshape(1, -1),
        "fc1_weight": fc1_weight,
        "fc1_bias": fc1_bias.reshape(1, -1),
        "fc2_weight": fc2_weight,
        "fc2_bias": fc2_bias.reshape(1, -1),
    }
    operands = [named[name] for name in OPERANDS]
    inputs = [by_place(clip_tokens), by_place(target)] + operands
    plane = (2 * WH - 1) * (2 * WW - 1)
    out = pl.pallas_call(
        kernel,
        out_shape=pltpu.VMEM((WH, WW, 2, ST, CHAN), BF16),
        in_specs=[pl.BlockSpec(memory_space=pltpu.HBM)] * len(inputs),
        out_specs=pl.BlockSpec(memory_space=pltpu.VMEM),
        scratch_shapes=[pltpu.VMEM(x.shape, x.dtype) for x in operands]
        + [pltpu.SemaphoreType.DMA((len(operands),))]
        + [pltpu.VMEM((WH, WW, 2, ST, CHAN), BF16)] * 3
        + [pltpu.VMEM((WH, WW, ST, CHAN), BF16)] * 2
        + [
            pltpu.VMEM((HEADS * (2 * WT - 1), plane), F32),
            pltpu.VMEM((2 * WH - 1, HEADS * (2 * WT - 1), 128), F32),
            pltpu.VMEM((2 * WH - 1, WT, 128), F32),
            pltpu.VMEM((HEADS, (2 * WH - 1) * WW + 1, WT, 128), F32),
            pltpu.VMEM((HEADS, ROWS, KEYS), F32),
            pltpu.VMEM((HEADS, ROWS, KEYS), BF16),
            pltpu.VMEM((HEADS, ROWS, KEYS), BF16),
            pltpu.VMEM((TOK, CHAN), BF16),
            pltpu.VMEM((TOK, CHAN), BF16),
            pltpu.VMEM((KEYS, CHAN), BF16),
            pltpu.VMEM((KEYS, CHAN), BF16),
            pltpu.VMEM((KEYS, CHAN), BF16),
            pltpu.VMEM((TOK, 2 * CHAN), F32),
            pltpu.VMEM((TOK, CHAN), BF16),
            pltpu.VMEM((ROWS, CHAN), F32),
            pltpu.VMEM((TOK, CHAN), F32),
            pltpu.SemaphoreType.DMA((3, len(CUTS))),
            pltpu.SemaphoreType.DMA((3, len(CUTS))),
            pltpu.SemaphoreType.DMA((3,)),
            pltpu.SemaphoreType.DMA((2, 2)),
            pltpu.SemaphoreType.DMA((2, len(IN_TIME))),
        ],
        compiler_params=pltpu.CompilerParams(
            collective_id=0, has_side_effects=True, vmem_limit_bytes=40 * 1024 * 1024
        ),
        name="window_block",
    )(*[pltpu.with_memory_space_constraint(x, pltpu.HBM) for x in inputs])
    return jnp.transpose(out.reshape(1, WH, WW, WT, CHAN), (3, 0, 1, 2, 4))


def solution(mesh):
    return jax.shard_map(
        shards,
        mesh=mesh,
        in_specs=(P("tm", "tile", None, None, None),) * 2 + (P(),) * 13,
        out_specs=P("tm", "tile", None, None, None),
        check_vma=False,
    )
```

```python
import itertools

import jax
import jax.numpy as jnp
import numpy as np
from jax import lax
from jax.experimental import pallas as pl
from jax.experimental.pallas import tpu as pltpu
from jax.sharding import PartitionSpec as P

HEADS = 4
HEAD = 32
CHAN = 128
FF = 512
WT = 8
WH = 7
WW = 7
ST = 4
SH = 3
SW = 3
TCOLS = 4
TROWS = 4
TM = 16
TOK = WT * WH * WW
KEYS = 512
ROWS = 400
CHUNK = 80
TILES = CHUNK // WT

EPSILON = 1e-05
MASKED = -1000000000.0
INV_ROOT_TAU = 0.3989422804014327
ERF_STEP = 0.3275911 * 0.7071067811865476
ERF_TERMS = (0.254829592, -0.284496736, 1.421413741, -1.453152027, 1.061405429)
SCALE = HEAD ** (-0.5)
LOG2E = 1.4426950408889634

F32 = jnp.float32
BF16 = jnp.bfloat16
MESH = pl.DeviceIdType.MESH


CUTS = sorted(itertools.product(range(2), range(2), range(2)), reverse=True)
AWAY, STAYS = CUTS[:-1], CUTS[-1]
IN_TIME = [cut for cut in AWAY if cut[0]]
RELAY = TM // 2 - 1
HALVES = (slice(0, 192), slice(192, TOK))
QUARTERS = (slice(0, 96), slice(96, 192), slice(192, 288), slice(288, TOK))


def box(cut, rolled):
    et, er, ec = cut
    if rolled:
        rows, cols, half = (WH - SH if er else 0), (WW - SW if ec else 0), et
    else:
        rows, cols, half = (0 if er else SH), (0 if ec else SW), 1 - et
    return (pl.ds(rows, SH if er else WH - SH), pl.ds(cols, SW if ec else WW - SW), half)


def dot(a, b, dims=((1,), (0,))):
    return lax.dot_general(a, b, (dims, ((), ())), preferred_element_type=F32)


NT = ((1,), (1,))


def row_mean(values):
    return jnp.sum(values, -1, keepdims=True) * (1.0 / CHAN)


def norm_stats(values):
    center = values - row_mean(values)
    inv_std = lax.rsqrt(row_mean(center * center) + EPSILON)
    return center * inv_std, inv_std


def norm_backward(grad_out, normal, inv_std, gain):
    scaled = grad_out * gain
    return inv_std * (scaled - row_mean(scaled) - normal * row_mean(scaled * normal))


def iota(shape, dim):
    return lax.broadcasted_iota(jnp.int32, shape, dim)


def position():
    tile_pos = lax.axis_index("tile")
    return lax.axis_index("tm"), tile_pos // TCOLS, tile_pos % TCOLS


def crosses(time):
    return time % (TM // 2) == TM // 2 - 1


def swapped(time, row):
    return jnp.where(crosses(time), (row + TROWS // 2) % TROWS, row)


def device(time, row, col):
    return {"tm": time, "tile": row * TCOLS + col}


def target(cut):
    time, row, col = position()
    time = (time + TM - cut[0]) % TM
    row = swapped(time, (row + TROWS - cut[1]) % TROWS)
    return device(time, row, (col + TCOLS - cut[2]) % TCOLS)


def source(cut):
    time, row, col = position()
    row = swapped(time, row)
    return device((time + cut[0]) % TM, (row + cut[1]) % TROWS, (col + cut[2]) % TCOLS)


def sender(cut):
    where = source(cut)
    if cut[0]:
        where["tm"] = jnp.where(position()[0] == TM - 1, RELAY, where["tm"])
    return where


class Exchange:
    def __init__(self, src, dst, sems, to_window, relay=None):
        send_sems, recv_sems, local_sem = sems[:3]
        self.time, row, col = position()
        self.away = crosses(self.time)
        self.remote = {
            cut: pltpu.make_async_remote_copy(
                src_ref=src.at[box(cut, not to_window)],
                dst_ref=dst.at[box(cut, to_window)],
                send_sem=send_sems.at[i],
                recv_sem=recv_sems.at[i],
                device_id=target(cut) if to_window else source(cut),
                device_id_type=MESH,
            )
            for i, cut in enumerate(CUTS)
        }
        self.local = pltpu.make_async_copy(
            src.at[box(STAYS, not to_window)], dst.at[box(STAYS, to_window)], local_sem
        )
        self.relayed = to_window
        if not to_window:
            return
        relay_sems, onward_sems = sems[3:]
        self.hand_over = pltpu.make_async_remote_copy(
            src_ref=src.at[:, :, 0],
            dst_ref=relay,
            send_sem=relay_sems.at[0],
            recv_sem=relay_sems.at[1],
            device_id=device(RELAY, row, col),
            device_id_type=MESH,
        )
        self.onward = [
            pltpu.make_async_remote_copy(
                src_ref=relay.at[box(cut, False)[:2]],
                dst_ref=dst.at[box(cut, True)],
                send_sem=onward_sems.at[i],
                recv_sem=recv_sems.at[CUTS.index(cut)],
                device_id=device(
                    TM - 1,
                    swapped(TM - 1, (row + TROWS - cut[1]) % TROWS),
                    (col + TCOLS - cut[2]) % TCOLS,
                ),
                device_id_type=MESH,
            )
            for i, cut in enumerate(IN_TIME)
        ]

    def over_time(self, act):
        if not self.relayed:
            for cut in IN_TIME:
                act(self.remote[cut])
            return

        @pl.when(self.time == 0)
        def _():
            act(self.hand_over)

        @pl.when(self.time != 0)
        def _():
            for cut in IN_TIME:
                act(self.remote[cut])

    def start(self, cuts):
        if self.relayed:
            self.over_time(lambda copy: copy.start())
            cuts = [cut for cut in cuts if not cut[0]]
        for cut in cuts:
            if cut == STAYS:
                pl.when(self.away)(self.remote[cut].start)
                pl.when(jnp.logical_not(self.away))(self.local.start)
            else:
                self.remote[cut].start()

    def pass_on(self):
        @pl.when(self.time == RELAY)
        def _():
            self.hand_over.wait_recv()
            for copy in self.onward:
                copy.start()

    def wait_passed_on(self):
        @pl.when(self.time == RELAY)
        def _():
            for copy in self.onward:
                copy.wait_send()

    def wait_sent(self):
        self.over_time(lambda copy: copy.wait_send())
        for cut in AWAY:
            if not cut[0]:
                self.remote[cut].wait_send()
        pl.when(self.away)(self.remote[STAYS].wait_send)

    def wait_received(self):
        for cut in AWAY:
            self.remote[cut].wait_recv()
        pl.when(self.away)(self.remote[STAYS].wait_recv)
        pl.when(jnp.logical_not(self.away))(self.local.wait)


def joined(halves):
    halves = halves.astype(F32).reshape(WH * WW, 2, ST, CHAN)
    return jnp.concatenate([halves[:, 0], halves[:, 1]], axis=1).reshape(TOK, CHAN)


def spread_bias(table, slab_ref, spread_ref):
    time_span, row_span, col_span = 2 * WT - 1, 2 * WH - 1, 2 * WW - 1
    plane = row_span * col_span
    slab_ref[HEADS * time_span :, :] = jnp.zeros((HEADS, plane), F32)
    for d in range(time_span):
        slab_ref[HEADS * d : HEADS * (d + 1), :] = table[:, d * plane : (d + 1) * plane]
    slabs = slab_ref[...] * LOG2E
    high = slabs.astype(BF16)
    rest = slabs - high.astype(F32)
    middle = rest.astype(BF16)
    low = (rest - middle.astype(F32)).astype(BF16)
    lanes = iota((1, row_span * 128), 1)
    slot = lanes % 128 // WT
    wanted = jnp.where(slot < col_span, lanes // 128 * col_span + (col_span - 1) - slot, -1)
    pick = (iota((plane, row_span * 128), 0) == wanted).astype(F32).astype(BF16)
    spread = dot(jnp.concatenate([low, middle, high], axis=0), pick)
    count = slabs.shape[0]
    spread = (spread[:count] + spread[count : 2 * count]) + spread[2 * count :]
    for p in range(row_span):
        spread_ref[p] = spread[:, p * 128 : (p + 1) * 128]


def fill_bias(heads, spread_ref, skew_ref, bias_ref):
    row_span = 2 * WH - 1
    lane_time = iota((WT, 128), 1) % WT
    first = iota((WT, 128), 1) < 64

    for h in heads:
        for p in range(row_span):
            skewed = None
            for a in range(WT):
                rows = spread_ref[p, pl.ds((WT - 1 - a) * HEADS + h, WT, stride=HEADS), :]
                skewed = rows if skewed is None else jnp.where(lane_time == a, rows, skewed)
            skew_ref[h, p] = skewed
    for h in heads:
        for d in range(row_span):
            one, two = skew_ref[h, d], skew_ref[h, max(d - 1, 0)]
            for c in range(WW):
                shift = WT * (WW - 1 - c)
                bias_ref[h, d * WW + c] = jnp.where(
                    first,
                    one if shift == 0 else pltpu.roll(one, 128 - shift, 1),
                    pltpu.roll(two, 64 - shift, 1),
                )


def gelu_parts(pre_act):
    bell = jnp.exp2((-0.5 * LOG2E) * pre_act * pre_act)
    step = 1.0 / (1.0 + ERF_STEP * jnp.abs(pre_act))
    tail = ERF_TERMS[4]
    for term in ERF_TERMS[3::-1]:
        tail = tail * step + term
    tail = tail * step * (0.5 * bell)
    share = jnp.where(pre_act < 0.0, tail, 1.0 - tail)
    return pre_act * share, share + pre_act * (INV_ROOT_TAU * bell)


def region_classes(row, col, time):
    time_pos, row_pos, col_pos = position()
    last_time = time_pos == TM - 1
    last_row = swapped(time_pos, row_pos) == TROWS - 1
    last_col = col_pos == TCOLS - 1
    return (
        jnp.where(time >= ST, jnp.where(last_time, 4, 0), 0)
        + jnp.where(row >= WH - SH, jnp.where(last_row, 2, 0), 0)
        + jnp.where(col >= WW - SW, jnp.where(last_col, 1, 0), 0)
    )


def pad_keys(values):
    blocks = values.reshape(WH, WW, WT, CHAN)
    blocks = jnp.concatenate([blocks, jnp.zeros((WH, 1, WT, CHAN), values.dtype)], axis=1)
    blocks = jnp.concatenate([blocks, jnp.zeros((1, 8, WT, CHAN), values.dtype)], axis=0)
    return blocks.reshape(KEYS, CHAN)


def unpad_keys(values):
    return values.reshape(8, 8, WT, CHAN)[:WH, :WW].reshape(TOK, CHAN)


OPERANDS = (
    "table",
    "gain1",
    "shift1",
    "qkv_weight",
    "qkv_bias",
    "proj_weight",
    "proj_bias",
    "gain2",
    "shift2",
    "fc1_weight",
    "fc1_bias",
    "fc2_weight",
    "fc2_bias",
)


def kernel(*refs):
    count = len(OPERANDS)
    clip_ref, goal_ref, *sources = refs[: count + 2]
    out_ref = refs[count + 2]
    held = refs[count + 3 : 2 * count + 3]
    (
        load_sems,
        clip_in,
        goal_in,
        back_out,
        clip_relay,
        goal_relay,
        slab_ref,
        spread_ref,
        skew_ref,
        bias_ref,
        scores_ref,
        probs_ref,
        grads_ref,
        queries_ref,
        classes_ref,
        keys_ref,
        barred_ref,
        values_ref,
        mixed_ref,
        mixed_grad_ref,
        toward_ref,
        grad_queries_ref,
        send_sems,
        recv_sems,
        local_sems,
        relay_sems,
        onward_sems,
    ) = refs[2 * count + 3 :]

    loads = {}

    def load(i):
        name = OPERANDS[i]
        loads[name] = (pltpu.make_async_copy(sources[i], held[i], load_sems.at[i]), held[i])
        loads[name][0].start()

    time_pos, row_pos, col_pos = position()
    away = crosses(time_pos)
    barrier = pltpu.get_barrier_semaphore()
    for cut in AWAY:
        pl.semaphore_signal(barrier, inc=1, device_id=sender(cut), device_id_type=MESH)

    @pl.when(away)
    def _():
        pl.semaphore_signal(barrier, inc=1, device_id=source(STAYS), device_id_type=MESH)

    @pl.when(time_pos == RELAY)
    def _():
        first_block = device(0, row_pos, col_pos)
        pl.semaphore_signal(barrier, inc=1, device_id=first_block, device_id_type=MESH)

    sems = [
        (send_sems.at[k], recv_sems.at[k], local_sems.at[k], relay_sems.at[k], onward_sems.at[k])
        for k in range(2)
    ]
    clip = Exchange(clip_ref, clip_in, sems[0], True, clip_relay)
    goal = Exchange(goal_ref, goal_in, sems[1], True, goal_relay)
    back_sems = (send_sems.at[2], recv_sems.at[2], local_sems.at[2])
    back = Exchange(back_out, out_ref, back_sems, False)
    for i in range(count):
        load(i)

    def operand(name):
        copy, ref = loads[name]
        copy.wait()
        return ref[...]

    targets = jnp.where(away, len(CUTS), len(AWAY))
    targets = targets + jnp.where(time_pos == RELAY, len(IN_TIME), 0)
    targets = targets - jnp.where(time_pos == 0, len(IN_TIME) - 1, 0)
    pl.semaphore_wait(barrier, targets)
    clip.start(CUTS)
    clip.pass_on()
    spread_bias(operand("table"), slab_ref, spread_ref)
    fill_bias((0, 1), spread_ref, skew_ref, bias_ref)
    clip.wait_sent()
    goal.start(CUTS)
    fill_bias((2, 3), spread_ref, skew_ref, bias_ref)
    goal.pass_on()

    lane = iota((1, CHAN), 1)
    spot = lane % HEAD
    head_masks = [lane // HEAD == h for h in range(HEADS)]
    head_lanes = [mask.astype(F32).astype(BF16) for mask in head_masks]
    token = iota((TOK, 1), 0)
    query_class = region_classes(token // (WW * WT), token % (WW * WT) // WT, token % WT)
    classes_ref[...] = jnp.where(query_class == spot, 1.0, 0.0).astype(BF16)
    key = iota((KEYS, 1), 0)
    key_row, key_col = key // 64, key % 64 // WT
    key_class = region_classes(key_row, key_col, key % WT)
    key_class = jnp.where((key_row < WH) & (key_col < WW), key_class, 8)
    barred_ref[...] = jnp.where((key_class != spot) & (spot < 8), MASKED, 0.0).astype(BF16)

    gain1 = operand("gain1")
    shift1 = operand("shift1")
    qkv_weight = operand("qkv_weight")
    qkv_bias = operand("qkv_bias")
    query_weight_across = qkv_weight[:, :CHAN].T
    query_bias_across = jnp.broadcast_to(qkv_bias[0:1], (CHAN, CHAN)).T[:, 0:1]
    proj_weight = operand("proj_weight")
    proj_bias = operand("proj_bias")
    gain2 = operand("gain2")
    shift2 = operand("shift2")
    fc1_weight = operand("fc1_weight")
    fc1_bias = operand("fc1_bias")
    fc2_weight = operand("fc2_weight")
    fc2_bias = operand("fc2_bias")
    clip.wait_received()
    frames = joined(clip_in[...])
    normal1, inv_std1 = norm_stats(frames)
    normed1 = (normal1 * gain1 + shift1).astype(BF16)
    projected = jnp.concatenate([dot(normed1[part], qkv_weight) for part in HALVES], axis=0)
    queries_ref[...] = ((projected[:, :CHAN] + qkv_bias[0:1]) * (SCALE * LOG2E)).astype(BF16)
    keys_ref[...] = pad_keys(projected[:, CHAN : 2 * CHAN] + qkv_bias[1:2]).astype(BF16)
    values_ref[...] = pad_keys(projected[:, 2 * CHAN :] + qkv_bias[2:3]).astype(BF16)

    def score(h):
        mine, spare = head_lanes[h], head_lanes[(h + 1) % HEADS]
        head_queries = queries_ref[...] * mine + classes_ref[...] * spare
        head_keys = keys_ref[...] * mine + barred_ref[...] * spare
        scores_ref[h, 0:TOK, :] = dot(head_queries, head_keys, NT)

    def weigh(h):
        for chunk in range(ROWS // CHUNK):
            span = pl.ds(chunk * CHUNK, CHUNK)
            bias = [
                bias_ref[h, pl.ds(chunk * TILES + 42 - 14 * m, TILES)].reshape(CHUNK, 128)
                for m in range(4)
            ]
            scores = scores_ref[h, span, :] + jnp.concatenate(bias, axis=1)
            exponent = jnp.exp2(scores - jnp.max(scores, -1, keepdims=True))
            probs_ref[h, span, :] = exponent.astype(BF16)

    def mix(h):
        ones = jnp.broadcast_to(head_lanes[h], (KEYS, CHAN))
        sides = jnp.concatenate([values_ref[...] * head_lanes[h], ones], axis=1)
        part = dot(probs_ref[h, 0:TOK, :], sides)
        mixed_ref[...] = part if h == 0 else mixed_ref[...] + part

    score(0)
    for h in range(HEADS):
        if h + 1 < HEADS:
            score(h + 1)
        if h > 0:
            mix(h - 1)
        weigh(h)
    queries_across = dot(query_weight_across, normed1, NT) + query_bias_across
    queries_across = (queries_across * SCALE).astype(BF16)
    mix(HEADS - 1)

    inv_total = 1.0 / mixed_ref[:, CHAN:]
    mixed = mixed_ref[:, :CHAN] * inv_total
    mixed_low = mixed.astype(BF16)
    branch = [(dot(mixed_low[part], proj_weight) + proj_bias).astype(BF16) for part in QUARTERS]
    ys = [frames[part] + branch[i].astype(F32) for i, part in enumerate(QUARTERS)]
    stats2 = [norm_stats(y) for y in ys]
    for i, part in enumerate(QUARTERS):
        normed2 = (stats2[i][0] * gain2 + shift2).astype(BF16)
        scores_ref[0, part, :] = dot(normed2, fc1_weight) + fc1_bias
    inv_total_across = inv_total.T
    outputs = []
    for i, part in enumerate(QUARTERS):
        active, slope = gelu_parts(scores_ref[0, part, :])
        scores_ref[1, part, :] = slope
        outputs.append(ys[i] + dot(active.astype(BF16), fc2_weight) + fc2_bias)
    goal.wait_received()
    wanted = joined(goal_in[...])
    grad_out = [outputs[i] - wanted[part] for i, part in enumerate(QUARTERS)]
    grad_pre = [
        (dot(grad_out[i].astype(BF16), fc2_weight, NT) * scores_ref[1, part, :]).astype(BF16)
        for i, part in enumerate(QUARTERS)
    ]
    grad_norm2 = [dot(grad, fc1_weight, NT) for grad in grad_pre]
    grad_ys = jnp.concatenate(
        [grad_out[i] + norm_backward(grad_norm2[i], *stats2[i], gain2) for i in range(4)], axis=0
    )

    grad_low = grad_ys.astype(BF16)
    grad_mixed = (dot(grad_low, proj_weight, NT) * inv_total).astype(BF16)
    grad_mixed_across = (dot(proj_weight, grad_low, NT) * inv_total_across).astype(BF16)
    mixed_grad_ref[...] = grad_mixed
    toward_ref[0:TOK, :] = grad_mixed.astype(F32) * mixed

    def score_grad(h):
        scores_ref[h, 0:TOK, :] = dot(mixed_grad_ref[...] * head_lanes[h], values_ref[...], NT)

    def weigh_grad(h):
        for chunk in range(ROWS // CHUNK):
            span = pl.ds(chunk * CHUNK, CHUNK)
            own = jnp.where(head_masks[h], toward_ref[span, :], 0.0)
            delta = jnp.sum(own, -1, keepdims=True)
            excess = (scores_ref[h, span, :] - delta).astype(BF16)
            grads_ref[h, span, :] = probs_ref[h, span, :] * excess

    def value_grad(h):
        rows = slice(h * HEAD, (h + 1) * HEAD)
        return dot(grad_mixed_across[rows], probs_ref[h, 0:TOK, :]).astype(BF16)

    def key_grad(h):
        rows = slice(h * HEAD, (h + 1) * HEAD)
        return dot(queries_across[rows], grads_ref[h, 0:TOK, :]).astype(BF16)

    def query_grad(h):
        part = dot(grads_ref[h, 0:TOK, :], keys_ref[...] * head_lanes[h])
        grad_queries_ref[...] = part if h == 0 else grad_queries_ref[...] + part

    grad_values = [None] * HEADS
    grad_keys = [None] * HEADS
    score_grad(0)
    for h in range(HEADS):
        if h + 1 < HEADS:
            score_grad(h + 1)
        grad_values[h] = value_grad(h)
        if h > 0:
            query_grad(h - 1)
            grad_keys[h - 1] = key_grad(h - 1)
        weigh_grad(h)
    grad_keys[HEADS - 1] = key_grad(HEADS - 1)
    query_grad(HEADS - 1)

    across = jnp.concatenate(grad_keys + grad_values, axis=0)
    grad_normed = unpad_keys(dot(qkv_weight[:, CHAN:], across).T)
    grad_queries = (grad_queries_ref[...] * SCALE).astype(BF16)
    for group, rows in enumerate((range(0, WH - SH), range(WH - SH, WH))):
        part = slice(rows.start * WW * WT, rows.stop * WW * WT)
        total = grad_normed[part] + dot(grad_queries[part], qkv_weight[:, :CHAN], NT)
        total = total.astype(BF16).astype(F32)
        result = grad_ys[part] + norm_backward(total, normal1[part], inv_std1[part], gain1)
        result = result.reshape(len(rows), WW, WT, CHAN)
        back_out[rows.start : rows.stop, :, 0] = result[:, :, :ST].astype(BF16)
        back_out[rows.start : rows.stop, :, 1] = result[:, :, ST:].astype(BF16)
        back.start([cut for cut in CUTS if cut[1] == group])
    back.wait_received()
    goal.wait_sent()
    clip.wait_passed_on()
    goal.wait_passed_on()
    back.wait_sent()


def shards(
    clip_tokens,
    target,
    norm1_gain,
    norm1_bias,
    qkv_weight,
    qkv_bias,
    bias_table,
    proj_weight,
    proj_bias,
    norm2_gain,
    norm2_bias,
    fc1_weight,
    fc1_bias,
    fc2_weight,
    fc2_bias,
):
    def by_place(tokens):
        return jnp.transpose(tokens, (1, 2, 3, 0, 4)).reshape(WH, WW, 2, ST, CHAN)

    named = {
        "table": bias_table.T,
        "gain1": norm1_gain.reshape(1, -1),
        "shift1": norm1_bias.reshape(1, -1),
        "qkv_weight": qkv_weight,
        "qkv_bias": qkv_bias.reshape(3, -1),
        "proj_weight": proj_weight,
        "proj_bias": proj_bias.reshape(1, -1),
        "gain2": norm2_gain.reshape(1, -1),
        "shift2": norm2_bias.reshape(1, -1),
        "fc1_weight": fc1_weight,
        "fc1_bias": fc1_bias.reshape(1, -1),
        "fc2_weight": fc2_weight,
        "fc2_bias": fc2_bias.reshape(1, -1),
    }
    operands = [named[name] for name in OPERANDS]
    inputs = [by_place(clip_tokens), by_place(target)] + operands
    plane = (2 * WH - 1) * (2 * WW - 1)
    out = pl.pallas_call(
        kernel,
        out_shape=pltpu.VMEM((WH, WW, 2, ST, CHAN), BF16),
        in_specs=[pl.BlockSpec(memory_space=pltpu.HBM)] * len(inputs),
        out_specs=pl.BlockSpec(memory_space=pltpu.VMEM),
        scratch_shapes=[pltpu.VMEM(x.shape, x.dtype) for x in operands]
        + [pltpu.SemaphoreType.DMA((len(operands),))]
        + [pltpu.VMEM((WH, WW, 2, ST, CHAN), BF16)] * 3
        + [pltpu.VMEM((WH, WW, ST, CHAN), BF16)] * 2
        + [
            pltpu.VMEM((HEADS * 2 * WT, plane), F32),
            pltpu.VMEM((2 * WH - 1, HEADS * 2 * WT, 128), F32),
            pltpu.VMEM((HEADS, 2 * WH - 1, WT, 128), F32),
            pltpu.VMEM((HEADS, (2 * WH - 1) * WW + 1, WT, 128), F32),
            pltpu.VMEM((HEADS, ROWS, KEYS), F32),
            pltpu.VMEM((HEADS, ROWS, KEYS), BF16),
            pltpu.VMEM((HEADS, ROWS, KEYS), BF16),
            pltpu.VMEM((TOK, CHAN), BF16),
            pltpu.VMEM((TOK, CHAN), BF16),
            pltpu.VMEM((KEYS, CHAN), BF16),
            pltpu.VMEM((KEYS, CHAN), BF16),
            pltpu.VMEM((KEYS, CHAN), BF16),
            pltpu.VMEM((TOK, 2 * CHAN), F32),
            pltpu.VMEM((TOK, CHAN), BF16),
            pltpu.VMEM((ROWS, CHAN), F32),
            pltpu.VMEM((TOK, CHAN), F32),
            pltpu.SemaphoreType.DMA((3, len(CUTS))),
            pltpu.SemaphoreType.DMA((3, len(CUTS))),
            pltpu.SemaphoreType.DMA((3,)),
            pltpu.SemaphoreType.DMA((2, 2)),
            pltpu.SemaphoreType.DMA((2, len(IN_TIME))),
        ],
        compiler_params=pltpu.CompilerParams(
            collective_id=0, has_side_effects=True, vmem_limit_bytes=40 * 1024 * 1024
        ),
        name="window_block",
    )(*[pltpu.with_memory_space_constraint(x, pltpu.HBM) for x in inputs])
    return jnp.transpose(out.reshape(1, WH, WW, WT, CHAN), (3, 0, 1, 2, 4))


def solution(mesh):
    return jax.shard_map(
        shards,
        mesh=mesh,
        in_specs=(P("tm", "tile", None, None, None),) * 2 + (P(),) * 13,
        out_specs=P("tm", "tile", None, None, None),
        check_vma=False,
    )
```

```python
import itertools

import jax
import jax.numpy as jnp
import numpy as np
from jax import lax
from jax.experimental import pallas as pl
from jax.experimental.pallas import tpu as pltpu
from jax.sharding import PartitionSpec as P

HEADS = 4
HEAD = 32
CHAN = 128
FF = 512
WT = 8
WH = 7
WW = 7
ST = 4
SH = 3
SW = 3
TCOLS = 4
TROWS = 4
TM = 16
TOK = WT * WH * WW
KEYS = 512
ROWS = 400
CHUNK = 80
TILES = CHUNK // WT

EPSILON = 1e-05
MASKED = -1000000000.0
INV_ROOT_TAU = 0.3989422804014327
ERF_STEP = 0.3275911 * 0.7071067811865476
ERF_TERMS = (0.254829592, -0.284496736, 1.421413741, -1.453152027, 1.061405429)
SCALE = HEAD ** (-0.5)
LOG2E = 1.4426950408889634

F32 = jnp.float32
BF16 = jnp.bfloat16
MESH = pl.DeviceIdType.MESH


CUTS = sorted(itertools.product(range(2), range(2), range(2)), reverse=True)
IN_TIME = [cut for cut in CUTS if cut[0]]
IN_PLACE = [cut for cut in CUTS if not cut[0]]
RELAY = TM // 2 - 1
HALVES = (slice(0, 192), slice(192, TOK))
QUARTERS = (slice(0, 96), slice(96, 192), slice(192, 288), slice(288, TOK))


def box(cut, rolled):
    et, er, ec = cut
    if rolled:
        rows, cols, half = (WH - SH if er else 0), (WW - SW if ec else 0), et
    else:
        rows, cols, half = (0 if er else SH), (0 if ec else SW), 1 - et
    return (pl.ds(rows, SH if er else WH - SH), pl.ds(cols, SW if ec else WW - SW), half)


def dot(a, b, dims=((1,), (0,))):
    return lax.dot_general(a, b, (dims, ((), ())), preferred_element_type=F32)


NT = ((1,), (1,))


def row_mean(values):
    return jnp.sum(values, -1, keepdims=True) * (1.0 / CHAN)


def norm_stats(values):
    center = values - row_mean(values)
    inv_std = lax.rsqrt(row_mean(center * center) + EPSILON)
    return center * inv_std, inv_std


def norm_backward(grad_out, normal, inv_std, gain):
    scaled = grad_out * gain
    return inv_std * (scaled - row_mean(scaled) - normal * row_mean(scaled * normal))


def iota(shape, dim):
    return lax.broadcasted_iota(jnp.int32, shape, dim)


def position():
    tile_pos = lax.axis_index("tile")
    return lax.axis_index("tm"), tile_pos // TCOLS, tile_pos % TCOLS


def crosses(time):
    return time % (TM // 2) == TM // 2 - 1


def spread_out(window):
    return jnp.where(window == 0, 0, jnp.where(window == 3, 1, window + 1))


def gathered(place):
    return jnp.where(place == 0, 0, jnp.where(place == 1, 3, place - 1))


def row_place(time, window):
    return jnp.where(crosses(time), (window + TROWS // 2) % TROWS, spread_out(window))


def window_position():
    time, row, col = position()
    window_row = jnp.where(crosses(time), (row + TROWS // 2) % TROWS, gathered(row))
    return time, window_row, gathered(col)


def device(time, row, col):
    return {"tm": time, "tile": row * TCOLS + col}


def target(cut):
    time, row, col = position()
    time = (time + TM - cut[0]) % TM
    row = row_place(time, (row + TROWS - cut[1]) % TROWS)
    return device(time, row, spread_out((col + TCOLS - cut[2]) % TCOLS))


def source(cut):
    time, row, col = window_position()
    return device((time + cut[0]) % TM, (row + cut[1]) % TROWS, (col + cut[2]) % TCOLS)


def stays(cut):
    return source(cut)["tile"] == lax.axis_index("tile")


def where_it_lies(cut, local, remote):
    if cut[0]:
        remote()
    else:
        pl.when(stays(cut))(local)
        pl.when(jnp.logical_not(stays(cut)))(remote)


def nothing():
    pass


def sender(cut):
    where = source(cut)
    if cut[0]:
        where["tm"] = jnp.where(position()[0] == TM - 1, RELAY, where["tm"])
    return where


class Exchange:
    def __init__(self, src, dst, sems, to_window, relay=None):
        send_sems, recv_sems, local_sems = sems[:3]
        self.time, row, col = position()
        self.remote = {
            cut: pltpu.make_async_remote_copy(
                src_ref=src.at[box(cut, not to_window)],
                dst_ref=dst.at[box(cut, to_window)],
                send_sem=send_sems.at[i],
                recv_sem=recv_sems.at[i],
                device_id=target(cut) if to_window else source(cut),
                device_id_type=MESH,
            )
            for i, cut in enumerate(CUTS)
        }
        self.local = {
            cut: pltpu.make_async_copy(
                src.at[box(cut, not to_window)], dst.at[box(cut, to_window)], local_sems.at[i]
            )
            for i, cut in enumerate(CUTS)
            if not cut[0]
        }
        self.relayed = to_window
        if not to_window:
            return
        relay_sems, onward_sems = sems[3:]
        self.hand_over = pltpu.make_async_remote_copy(
            src_ref=src.at[:, :, 0],
            dst_ref=relay,
            send_sem=relay_sems.at[0],
            recv_sem=relay_sems.at[1],
            device_id=device(RELAY, row, col),
            device_id_type=MESH,
        )
        self.onward = [
            pltpu.make_async_remote_copy(
                src_ref=relay.at[box(cut, False)[:2]],
                dst_ref=dst.at[box(cut, True)],
                send_sem=onward_sems.at[i],
                recv_sem=recv_sems.at[CUTS.index(cut)],
                device_id=device(
                    TM - 1,
                    row_place(TM - 1, (row + TROWS - cut[1]) % TROWS),
                    spread_out((col + TCOLS - cut[2]) % TCOLS),
                ),
                device_id_type=MESH,
            )
            for i, cut in enumerate(IN_TIME)
        ]

    def over_time(self, act):
        if not self.relayed:
            for cut in IN_TIME:
                act(self.remote[cut])
            return

        @pl.when(self.time == 0)
        def _():
            act(self.hand_over)

        @pl.when(self.time != 0)
        def _():
            for cut in IN_TIME:
                act(self.remote[cut])

    def start(self, cuts):
        if self.relayed:
            self.over_time(lambda copy: copy.start())
            cuts = [cut for cut in cuts if not cut[0]]
        for cut in cuts:
            if cut[0]:
                self.remote[cut].start()
            else:
                where_it_lies(cut, self.local[cut].start, self.remote[cut].start)

    def pass_on(self):
        @pl.when(self.time == RELAY)
        def _():
            self.hand_over.wait_recv()
            for copy in self.onward:
                copy.start()

    def wait_passed_on(self):
        @pl.when(self.time == RELAY)
        def _():
            for copy in self.onward:
                copy.wait_send()

    def wait_sent(self):
        self.over_time(lambda copy: copy.wait_send())
        for cut in IN_PLACE:
            where_it_lies(cut, nothing, self.remote[cut].wait_send)

    def wait_received(self):
        for cut in IN_TIME:
            self.remote[cut].wait_recv()
        for cut in IN_PLACE:
            where_it_lies(cut, self.local[cut].wait, self.remote[cut].wait_recv)


def joined(halves):
    halves = halves.astype(F32).reshape(WH * WW, 2, ST, CHAN)
    return jnp.concatenate([halves[:, 0], halves[:, 1]], axis=1).reshape(TOK, CHAN)


def spread_bias(table, slab_ref, spread_ref):
    time_span, row_span, col_span = 2 * WT - 1, 2 * WH - 1, 2 * WW - 1
    plane = row_span * col_span
    slab_ref[HEADS * time_span :, :] = jnp.zeros((HEADS, plane), F32)
    for d in range(time_span):
        slab_ref[HEADS * d : HEADS * (d + 1), :] = table[:, d * plane : (d + 1) * plane]
    slabs = slab_ref[...] * LOG2E
    high = slabs.astype(BF16)
    rest = slabs - high.astype(F32)
    middle = rest.astype(BF16)
    low = (rest - middle.astype(F32)).astype(BF16)
    lanes = iota((1, row_span * 128), 1)
    slot = lanes % 128 // WT
    wanted = jnp.where(slot < col_span, lanes // 128 * col_span + (col_span - 1) - slot, -1)
    pick = (iota((plane, row_span * 128), 0) == wanted).astype(F32).astype(BF16)
    spread = dot(jnp.concatenate([low, middle, high], axis=0), pick)
    count = slabs.shape[0]
    spread = (spread[:count] + spread[count : 2 * count]) + spread[2 * count :]
    for p in range(row_span):
        spread_ref[p] = spread[:, p * 128 : (p + 1) * 128]


def fill_bias(heads, spread_ref, skew_ref, bias_ref):
    row_span = 2 * WH - 1
    lane_time = iota((WT, 128), 1) % WT
    first = iota((WT, 128), 1) < 64

    for h in heads:
        for p in range(row_span):
            skewed = None
            for a in range(WT):
                rows = spread_ref[p, pl.ds((WT - 1 - a) * HEADS + h, WT, stride=HEADS), :]
                skewed = rows if skewed is None else jnp.where(lane_time == a, rows, skewed)
            skew_ref[h, p] = skewed
    for h in heads:
        for d in range(row_span):
            one, two = skew_ref[h, d], skew_ref[h, max(d - 1, 0)]
            for c in range(WW):
                shift = WT * (WW - 1 - c)
                bias_ref[h, d * WW + c] = jnp.where(
                    first,
                    one if shift == 0 else pltpu.roll(one, 128 - shift, 1),
                    pltpu.roll(two, 64 - shift, 1),
                )


def gelu_parts(pre_act):
    bell = jnp.exp2((-0.5 * LOG2E) * pre_act * pre_act)
    step = 1.0 / (1.0 + ERF_STEP * jnp.abs(pre_act))
    tail = ERF_TERMS[4]
    for term in ERF_TERMS[3::-1]:
        tail = tail * step + term
    tail = tail * step * (0.5 * bell)
    share = jnp.where(pre_act < 0.0, tail, 1.0 - tail)
    return pre_act * share, share + pre_act * (INV_ROOT_TAU * bell)


def region_classes(row, col, time):
    window_time, window_row, window_col = window_position()
    last_time = window_time == TM - 1
    last_row = window_row == TROWS - 1
    last_col = window_col == TCOLS - 1
    return (
        jnp.where(time >= ST, jnp.where(last_time, 4, 0), 0)
        + jnp.where(row >= WH - SH, jnp.where(last_row, 2, 0), 0)
        + jnp.where(col >= WW - SW, jnp.where(last_col, 1, 0), 0)
    )


def pad_keys(values):
    blocks = values.reshape(WH, WW, WT, CHAN)
    blocks = jnp.concatenate([blocks, jnp.zeros((WH, 1, WT, CHAN), values.dtype)], axis=1)
    blocks = jnp.concatenate([blocks, jnp.zeros((1, 8, WT, CHAN), values.dtype)], axis=0)
    return blocks.reshape(KEYS, CHAN)


def unpad_keys(values):
    return values.reshape(8, 8, WT, CHAN)[:WH, :WW].reshape(TOK, CHAN)


OPERANDS = (
    "table",
    "gain1",
    "shift1",
    "qkv_weight",
    "qkv_bias",
    "proj_weight",
    "proj_bias",
    "gain2",
    "shift2",
    "fc1_weight",
    "fc1_bias",
    "fc2_weight",
    "fc2_bias",
)


def kernel(*refs):
    count = len(OPERANDS)
    clip_ref, goal_ref, *sources = refs[: count + 2]
    out_ref = refs[count + 2]
    held = refs[count + 3 : 2 * count + 3]
    (
        load_sems,
        clip_in,
        goal_in,
        back_out,
        clip_relay,
        goal_relay,
        slab_ref,
        spread_ref,
        skew_ref,
        bias_ref,
        scores_ref,
        probs_ref,
        grads_ref,
        queries_ref,
        classes_ref,
        keys_ref,
        barred_ref,
        values_ref,
        mixed_ref,
        mixed_grad_ref,
        toward_ref,
        grad_queries_ref,
        send_sems,
        recv_sems,
        local_sems,
        relay_sems,
        onward_sems,
    ) = refs[2 * count + 3 :]

    loads = {}

    def load(i):
        name = OPERANDS[i]
        loads[name] = (pltpu.make_async_copy(sources[i], held[i], load_sems.at[i]), held[i])
        loads[name][0].start()

    time_pos, row_pos, col_pos = position()
    barrier = pltpu.get_barrier_semaphore()

    def greet(cut):
        pl.semaphore_signal(barrier, inc=1, device_id=sender(cut), device_id_type=MESH)

    for cut in CUTS:
        where_it_lies(cut, nothing, lambda cut=cut: greet(cut))

    @pl.when(time_pos == RELAY)
    def _():
        first_block = device(0, row_pos, col_pos)
        pl.semaphore_signal(barrier, inc=1, device_id=first_block, device_id_type=MESH)

    sems = [
        (send_sems.at[k], recv_sems.at[k], local_sems.at[k], relay_sems.at[k], onward_sems.at[k])
        for k in range(2)
    ]
    clip = Exchange(clip_ref, clip_in, sems[0], True, clip_relay)
    goal = Exchange(goal_ref, goal_in, sems[1], True, goal_relay)
    back_sems = (send_sems.at[2], recv_sems.at[2], local_sems.at[2])
    back = Exchange(back_out, out_ref, back_sems, False)
    for i in range(count):
        load(i)

    def operand(name):
        copy, ref = loads[name]
        copy.wait()
        return ref[...]

    targets = len(CUTS)
    for cut in IN_PLACE:
        targets = targets - jnp.where(stays(cut), 1, 0)
    targets = targets + jnp.where(time_pos == RELAY, len(IN_TIME), 0)
    targets = targets - jnp.where(time_pos == 0, len(IN_TIME) - 1, 0)
    pl.semaphore_wait(barrier, targets)
    clip.start(CUTS)
    clip.pass_on()
    spread_bias(operand("table"), slab_ref, spread_ref)
    fill_bias((0, 1), spread_ref, skew_ref, bias_ref)
    clip.wait_sent()
    goal.start(CUTS)
    fill_bias((2, 3), spread_ref, skew_ref, bias_ref)
    goal.pass_on()

    lane = iota((1, CHAN), 1)
    spot = lane % HEAD
    head_masks = [lane // HEAD == h for h in range(HEADS)]
    head_lanes = [mask.astype(F32).astype(BF16) for mask in head_masks]
    token = iota((TOK, 1), 0)
    query_class = region_classes(token // (WW * WT), token % (WW * WT) // WT, token % WT)
    classes_ref[...] = jnp.where(query_class == spot, 1.0, 0.0).astype(BF16)
    key = iota((KEYS, 1), 0)
    key_row, key_col = key // 64, key % 64 // WT
    key_class = region_classes(key_row, key_col, key % WT)
    key_class = jnp.where((key_row < WH) & (key_col < WW), key_class, 8)
    barred_ref[...] = jnp.where((key_class != spot) & (spot < 8), MASKED, 0.0).astype(BF16)

    gain1 = operand("gain1")
    shift1 = operand("shift1")
    qkv_weight = operand("qkv_weight")
    qkv_bias = operand("qkv_bias")
    query_weight_across = qkv_weight[:, :CHAN].T
    query_bias_across = jnp.broadcast_to(qkv_bias[0:1], (CHAN, CHAN)).T[:, 0:1]
    proj_weight = operand("proj_weight")
    proj_bias = operand("proj_bias")
    gain2 = operand("gain2")
    shift2 = operand("shift2")
    fc1_weight = operand("fc1_weight")
    fc1_bias = operand("fc1_bias")
    fc2_weight = operand("fc2_weight")
    fc2_bias = operand("fc2_bias")
    clip.wait_received()
    frames = joined(clip_in[...])
    normal1, inv_std1 = norm_stats(frames)
    normed1 = (normal1 * gain1 + shift1).astype(BF16)
    projected = jnp.concatenate([dot(normed1[part], qkv_weight) for part in HALVES], axis=0)
    queries_ref[...] = ((projected[:, :CHAN] + qkv_bias[0:1]) * (SCALE * LOG2E)).astype(BF16)
    keys_ref[...] = pad_keys(projected[:, CHAN : 2 * CHAN] + qkv_bias[1:2]).astype(BF16)
    values_ref[...] = pad_keys(projected[:, 2 * CHAN :] + qkv_bias[2:3]).astype(BF16)

    def score(h):
        mine, spare = head_lanes[h], head_lanes[(h + 1) % HEADS]
        head_queries = queries_ref[...] * mine + classes_ref[...] * spare
        head_keys = keys_ref[...] * mine + barred_ref[...] * spare
        scores_ref[h, 0:TOK, :] = dot(head_queries, head_keys, NT)

    def weigh(h):
        for chunk in range(ROWS // CHUNK):
            span = pl.ds(chunk * CHUNK, CHUNK)
            bias = [
                bias_ref[h, pl.ds(chunk * TILES + 42 - 14 * m, TILES)].reshape(CHUNK, 128)
                for m in range(4)
            ]
            scores = scores_ref[h, span, :] + jnp.concatenate(bias, axis=1)
            exponent = jnp.exp2(scores - jnp.max(scores, -1, keepdims=True))
            probs_ref[h, span, :] = exponent.astype(BF16)

    def mix(h):
        ones = jnp.broadcast_to(head_lanes[h], (KEYS, CHAN))
        sides = jnp.concatenate([values_ref[...] * head_lanes[h], ones], axis=1)
        part = dot(probs_ref[h, 0:TOK, :], sides)
        mixed_ref[...] = part if h == 0 else mixed_ref[...] + part

    score(0)
    for h in range(HEADS):
        if h + 1 < HEADS:
            score(h + 1)
        if h > 0:
            mix(h - 1)
        weigh(h)
    queries_across = dot(query_weight_across, normed1, NT) + query_bias_across
    queries_across = (queries_across * SCALE).astype(BF16)
    mix(HEADS - 1)

    inv_total = 1.0 / mixed_ref[:, CHAN:]
    mixed = mixed_ref[:, :CHAN] * inv_total
    mixed_low = mixed.astype(BF16)
    branch = [(dot(mixed_low[part], proj_weight) + proj_bias).astype(BF16) for part in QUARTERS]
    ys = [frames[part] + branch[i].astype(F32) for i, part in enumerate(QUARTERS)]
    stats2 = [norm_stats(y) for y in ys]
    for i, part in enumerate(QUARTERS):
        normed2 = (stats2[i][0] * gain2 + shift2).astype(BF16)
        scores_ref[0, part, :] = dot(normed2, fc1_weight) + fc1_bias
    inv_total_across = inv_total.T
    outputs = []
    for i, part in enumerate(QUARTERS):
        active, slope = gelu_parts(scores_ref[0, part, :])
        scores_ref[1, part, :] = slope
        outputs.append(ys[i] + dot(active.astype(BF16), fc2_weight) + fc2_bias)
    goal.wait_received()
    wanted = joined(goal_in[...])
    grad_out = [outputs[i] - wanted[part] for i, part in enumerate(QUARTERS)]
    grad_pre = [
        (dot(grad_out[i].astype(BF16), fc2_weight, NT) * scores_ref[1, part, :]).astype(BF16)
        for i, part in enumerate(QUARTERS)
    ]
    grad_norm2 = [dot(grad, fc1_weight, NT) for grad in grad_pre]
    grad_ys = jnp.concatenate(
        [grad_out[i] + norm_backward(grad_norm2[i], *stats2[i], gain2) for i in range(4)], axis=0
    )

    grad_low = grad_ys.astype(BF16)
    grad_mixed = (dot(grad_low, proj_weight, NT) * inv_total).astype(BF16)
    grad_mixed_across = (dot(proj_weight, grad_low, NT) * inv_total_across).astype(BF16)
    mixed_grad_ref[...] = grad_mixed
    toward_ref[0:TOK, :] = grad_mixed.astype(F32) * mixed

    def score_grad(h):
        scores_ref[h, 0:TOK, :] = dot(mixed_grad_ref[...] * head_lanes[h], values_ref[...], NT)

    def weigh_grad(h):
        for chunk in range(ROWS // CHUNK):
            span = pl.ds(chunk * CHUNK, CHUNK)
            own = jnp.where(head_masks[h], toward_ref[span, :], 0.0)
            delta = jnp.sum(own, -1, keepdims=True)
            excess = (scores_ref[h, span, :] - delta).astype(BF16)
            grads_ref[h, span, :] = probs_ref[h, span, :] * excess

    def value_grad(h):
        rows = slice(h * HEAD, (h + 1) * HEAD)
        return dot(grad_mixed_across[rows], probs_ref[h, 0:TOK, :]).astype(BF16)

    def key_grad(h):
        rows = slice(h * HEAD, (h + 1) * HEAD)
        return dot(queries_across[rows], grads_ref[h, 0:TOK, :]).astype(BF16)

    def query_grad(h):
        part = dot(grads_ref[h, 0:TOK, :], keys_ref[...] * head_lanes[h])
        grad_queries_ref[...] = part if h == 0 else grad_queries_ref[...] + part

    grad_values = [None] * HEADS
    grad_keys = [None] * HEADS
    score_grad(0)
    for h in range(HEADS):
        if h + 1 < HEADS:
            score_grad(h + 1)
        grad_values[h] = value_grad(h)
        if h > 0:
            query_grad(h - 1)
            grad_keys[h - 1] = key_grad(h - 1)
        weigh_grad(h)
    grad_keys[HEADS - 1] = key_grad(HEADS - 1)
    query_grad(HEADS - 1)

    across = jnp.concatenate(grad_keys + grad_values, axis=0)
    grad_normed = unpad_keys(dot(qkv_weight[:, CHAN:], across).T)
    grad_queries = (grad_queries_ref[...] * SCALE).astype(BF16)
    for group, rows in enumerate((range(0, WH - SH), range(WH - SH, WH))):
        part = slice(rows.start * WW * WT, rows.stop * WW * WT)
        total = grad_normed[part] + dot(grad_queries[part], qkv_weight[:, :CHAN], NT)
        total = total.astype(BF16).astype(F32)
        result = grad_ys[part] + norm_backward(total, normal1[part], inv_std1[part], gain1)
        result = result.reshape(len(rows), WW, WT, CHAN)
        back_out[rows.start : rows.stop, :, 0] = result[:, :, :ST].astype(BF16)
        back_out[rows.start : rows.stop, :, 1] = result[:, :, ST:].astype(BF16)
        back.start([cut for cut in CUTS if cut[1] == group])
    back.wait_received()
    goal.wait_sent()
    clip.wait_passed_on()
    goal.wait_passed_on()
    back.wait_sent()


def shards(
    clip_tokens,
    target,
    norm1_gain,
    norm1_bias,
    qkv_weight,
    qkv_bias,
    bias_table,
    proj_weight,
    proj_bias,
    norm2_gain,
    norm2_bias,
    fc1_weight,
    fc1_bias,
    fc2_weight,
    fc2_bias,
):
    def by_place(tokens):
        return jnp.transpose(tokens, (1, 2, 3, 0, 4)).reshape(WH, WW, 2, ST, CHAN)

    named = {
        "table": bias_table.T,
        "gain1": norm1_gain.reshape(1, -1),
        "shift1": norm1_bias.reshape(1, -1),
        "qkv_weight": qkv_weight,
        "qkv_bias": qkv_bias.reshape(3, -1),
        "proj_weight": proj_weight,
        "proj_bias": proj_bias.reshape(1, -1),
        "gain2": norm2_gain.reshape(1, -1),
        "shift2": norm2_bias.reshape(1, -1),
        "fc1_weight": fc1_weight,
        "fc1_bias": fc1_bias.reshape(1, -1),
        "fc2_weight": fc2_weight,
        "fc2_bias": fc2_bias.reshape(1, -1),
    }
    operands = [named[name] for name in OPERANDS]
    inputs = [by_place(clip_tokens), by_place(target)] + operands
    plane = (2 * WH - 1) * (2 * WW - 1)
    out = pl.pallas_call(
        kernel,
        out_shape=pltpu.VMEM((WH, WW, 2, ST, CHAN), BF16),
        in_specs=[pl.BlockSpec(memory_space=pltpu.HBM)] * len(inputs),
        out_specs=pl.BlockSpec(memory_space=pltpu.VMEM),
        scratch_shapes=[pltpu.VMEM(x.shape, x.dtype) for x in operands]
        + [pltpu.SemaphoreType.DMA((len(operands),))]
        + [pltpu.VMEM((WH, WW, 2, ST, CHAN), BF16)] * 3
        + [pltpu.VMEM((WH, WW, ST, CHAN), BF16)] * 2
        + [
            pltpu.VMEM((HEADS * 2 * WT, plane), F32),
            pltpu.VMEM((2 * WH - 1, HEADS * 2 * WT, 128), F32),
            pltpu.VMEM((HEADS, 2 * WH - 1, WT, 128), F32),
            pltpu.VMEM((HEADS, (2 * WH - 1) * WW + 1, WT, 128), F32),
            pltpu.VMEM((HEADS, ROWS, KEYS), F32),
            pltpu.VMEM((HEADS, ROWS, KEYS), BF16),
            pltpu.VMEM((HEADS, ROWS, KEYS), BF16),
            pltpu.VMEM((TOK, CHAN), BF16),
            pltpu.VMEM((TOK, CHAN), BF16),
            pltpu.VMEM((KEYS, CHAN), BF16),
            pltpu.VMEM((KEYS, CHAN), BF16),
            pltpu.VMEM((KEYS, CHAN), BF16),
            pltpu.VMEM((TOK, 2 * CHAN), F32),
            pltpu.VMEM((TOK, CHAN), BF16),
            pltpu.VMEM((ROWS, CHAN), F32),
            pltpu.VMEM((TOK, CHAN), F32),
            pltpu.SemaphoreType.DMA((3, len(CUTS))),
            pltpu.SemaphoreType.DMA((3, len(CUTS))),
            pltpu.SemaphoreType.DMA((3, len(CUTS))),
            pltpu.SemaphoreType.DMA((2, 2)),
            pltpu.SemaphoreType.DMA((2, len(IN_TIME))),
        ],
        compiler_params=pltpu.CompilerParams(
            collective_id=0, has_side_effects=True, vmem_limit_bytes=40 * 1024 * 1024
        ),
        name="window_block",
    )(*[pltpu.with_memory_space_constraint(x, pltpu.HBM) for x in inputs])
    return jnp.transpose(out.reshape(1, WH, WW, WT, CHAN), (3, 0, 1, 2, 4))


def solution(mesh):
    return jax.shard_map(
        shards,
        mesh=mesh,
        in_specs=(P("tm", "tile", None, None, None),) * 2 + (P(),) * 13,
        out_specs=P("tm", "tile", None, None, None),
        check_vma=False,
    )
```

```python
import itertools

import jax
import jax.numpy as jnp
import numpy as np
from jax import lax
from jax.experimental import pallas as pl
from jax.experimental.pallas import tpu as pltpu
from jax.sharding import PartitionSpec as P

HEADS = 4
HEAD = 32
CHAN = 128
FF = 512
WT = 8
WH = 7
WW = 7
ST = 4
SH = 3
SW = 3
TCOLS = 4
TROWS = 4
TM = 16
TOK = WT * WH * WW
KEYS = 512
ROWS = 400
CHUNK = 80
TILES = CHUNK // WT

EPSILON = 1e-05
MASKED = -1000000000.0
INV_ROOT_TAU = 0.3989422804014327
ERF_STEP = 0.3275911 * 0.7071067811865476
ERF_TERMS = (0.254829592, -0.284496736, 1.421413741, -1.453152027, 1.061405429)
SCALE = HEAD ** (-0.5)
LOG2E = 1.4426950408889634

F32 = jnp.float32
BF16 = jnp.bfloat16
MESH = pl.DeviceIdType.MESH


CUTS = sorted(itertools.product(range(2), range(2), range(2)), reverse=True)
IN_TIME = [cut for cut in CUTS if cut[0]]
IN_PLACE = [cut for cut in CUTS if not cut[0]]
RELAY = TM // 2 - 1
HALVES = (slice(0, 192), slice(192, TOK))
QUARTERS = (slice(0, 96), slice(96, 192), slice(192, 288), slice(288, TOK))


def box(cut, rolled):
    et, er, ec = cut
    if rolled:
        rows, cols, half = (WH - SH if er else 0), (WW - SW if ec else 0), et
    else:
        rows, cols, half = (0 if er else SH), (0 if ec else SW), 1 - et
    return (pl.ds(rows, SH if er else WH - SH), pl.ds(cols, SW if ec else WW - SW), half)


def dot(a, b, dims=((1,), (0,))):
    return lax.dot_general(a, b, (dims, ((), ())), preferred_element_type=F32)


NT = ((1,), (1,))


def row_mean(values):
    return jnp.sum(values, -1, keepdims=True) * (1.0 / CHAN)


def norm_stats(values):
    center = values - row_mean(values)
    inv_std = lax.rsqrt(row_mean(center * center) + EPSILON)
    return center * inv_std, inv_std


def norm_backward(grad_out, normal, inv_std, gain):
    scaled = grad_out * gain
    return inv_std * (scaled - row_mean(scaled) - normal * row_mean(scaled * normal))


def iota(shape, dim):
    return lax.broadcasted_iota(jnp.int32, shape, dim)


def position():
    tile_pos = lax.axis_index("tile")
    return lax.axis_index("tm"), tile_pos // TCOLS, tile_pos % TCOLS


def crosses(time):
    return time % (TM // 2) == TM // 2 - 1


def spread_out(window):
    return jnp.where(window == 0, 0, jnp.where(window == 3, 1, window + 1))


def gathered(place):
    return jnp.where(place == 0, 0, jnp.where(place == 1, 3, place - 1))


def row_place(time, window):
    return jnp.where(crosses(time), (window + TROWS // 2) % TROWS, spread_out(window))


def window_position():
    time, row, col = position()
    window_row = jnp.where(crosses(time), (row + TROWS // 2) % TROWS, gathered(row))
    return time, window_row, gathered(col)


def device(time, row, col):
    return {"tm": time, "tile": row * TCOLS + col}


def target(cut):
    time, row, col = position()
    time = (time + TM - cut[0]) % TM
    row = row_place(time, (row + TROWS - cut[1]) % TROWS)
    return device(time, row, spread_out((col + TCOLS - cut[2]) % TCOLS))


def source(cut):
    time, row, col = window_position()
    return device((time + cut[0]) % TM, (row + cut[1]) % TROWS, (col + cut[2]) % TCOLS)


def stays(cut):
    return source(cut)["tile"] == lax.axis_index("tile")


def where_it_lies(cut, local, remote):
    if cut[0]:
        remote()
    else:
        pl.when(stays(cut))(local)
        pl.when(jnp.logical_not(stays(cut)))(remote)


def nothing():
    pass


def sender(cut):
    where = source(cut)
    if cut[0]:
        time, _, col = position()
        relay = device(RELAY, where["tile"] // TCOLS, col)
        where = {axis: jnp.where(time == TM - 1, relay[axis], where[axis]) for axis in where}
    return where


class Exchange:
    def __init__(self, src, dst, sems, to_window, relay=None):
        send_sems, recv_sems, local_sems = sems[:3]
        self.time, row, col = position()
        self.remote = {
            cut: pltpu.make_async_remote_copy(
                src_ref=src.at[box(cut, not to_window)],
                dst_ref=dst.at[box(cut, to_window)],
                send_sem=send_sems.at[i],
                recv_sem=recv_sems.at[i],
                device_id=target(cut) if to_window else source(cut),
                device_id_type=MESH,
            )
            for i, cut in enumerate(CUTS)
        }
        self.local = {
            cut: pltpu.make_async_copy(
                src.at[box(cut, not to_window)], dst.at[box(cut, to_window)], local_sems.at[i]
            )
            for i, cut in enumerate(CUTS)
            if not cut[0]
        }
        self.relayed = to_window
        if not to_window:
            return
        relay_sems, onward_sems = sems[3:]
        self.hand_over = [
            pltpu.make_async_remote_copy(
                src_ref=src.at[:, box((1, 0, ec), False)[1], 0],
                dst_ref=relay.at[:, box((1, 0, ec), True)[1]],
                send_sem=relay_sems.at[0, ec],
                recv_sem=relay_sems.at[1, ec],
                device_id=device(RELAY, row, spread_out((col + TCOLS - ec) % TCOLS)),
                device_id_type=MESH,
            )
            for ec in range(2)
        ]
        self.onward = [
            pltpu.make_async_remote_copy(
                src_ref=relay.at[box(cut, False)[0], box(cut, True)[1]],
                dst_ref=dst.at[box(cut, True)],
                send_sem=onward_sems.at[i],
                recv_sem=recv_sems.at[CUTS.index(cut)],
                device_id=device(TM - 1, row_place(TM - 1, (row + TROWS - cut[1]) % TROWS), col),
                device_id_type=MESH,
            )
            for i, cut in enumerate(IN_TIME)
        ]

    def over_time(self, act):
        if not self.relayed:
            for cut in IN_TIME:
                act(self.remote[cut])
            return

        @pl.when(self.time == 0)
        def _():
            for copy in self.hand_over:
                act(copy)

        @pl.when(self.time != 0)
        def _():
            for cut in IN_TIME:
                act(self.remote[cut])

    def start(self, cuts):
        if self.relayed:
            self.over_time(lambda copy: copy.start())
            cuts = [cut for cut in cuts if not cut[0]]
        for cut in cuts:
            if cut[0]:
                self.remote[cut].start()
            else:
                where_it_lies(cut, self.local[cut].start, self.remote[cut].start)

    def pass_on(self):
        @pl.when(self.time == RELAY)
        def _():
            for copy in self.hand_over:
                copy.wait_recv()
            for copy in self.onward:
                copy.start()

    def wait_passed_on(self):
        @pl.when(self.time == RELAY)
        def _():
            for copy in self.onward:
                copy.wait_send()

    def wait_sent(self):
        self.over_time(lambda copy: copy.wait_send())
        for cut in IN_PLACE:
            where_it_lies(cut, nothing, self.remote[cut].wait_send)

    def wait_received(self):
        for cut in IN_TIME:
            self.remote[cut].wait_recv()
        for cut in IN_PLACE:
            where_it_lies(cut, self.local[cut].wait, self.remote[cut].wait_recv)


def joined(halves):
    halves = halves.astype(F32).reshape(WH * WW, 2, ST, CHAN)
    return jnp.concatenate([halves[:, 0], halves[:, 1]], axis=1).reshape(TOK, CHAN)


def spread_bias(table, slab_ref, spread_ref):
    time_span, row_span, col_span = 2 * WT - 1, 2 * WH - 1, 2 * WW - 1
    plane = row_span * col_span
    slab_ref[HEADS * time_span :, :] = jnp.zeros((HEADS, plane), F32)
    for d in range(time_span):
        slab_ref[HEADS * d : HEADS * (d + 1), :] = table[:, d * plane : (d + 1) * plane]
    slabs = slab_ref[...] * LOG2E
    high = slabs.astype(BF16)
    rest = slabs - high.astype(F32)
    middle = rest.astype(BF16)
    low = (rest - middle.astype(F32)).astype(BF16)
    lanes = iota((1, row_span * 128), 1)
    slot = lanes % 128 // WT
    wanted = jnp.where(slot < col_span, lanes // 128 * col_span + (col_span - 1) - slot, -1)
    pick = (iota((plane, row_span * 128), 0) == wanted).astype(F32).astype(BF16)
    spread = dot(jnp.concatenate([low, middle, high], axis=0), pick)
    count = slabs.shape[0]
    spread = (spread[:count] + spread[count : 2 * count]) + spread[2 * count :]
    for p in range(row_span):
        spread_ref[p] = spread[:, p * 128 : (p + 1) * 128]


def fill_bias(heads, spread_ref, skew_ref, bias_ref):
    row_span = 2 * WH - 1
    lane_time = iota((WT, 128), 1) % WT
    first = iota((WT, 128), 1) < 64

    for h in heads:
        for p in range(row_span):
            skewed = None
            for a in range(WT):
                rows = spread_ref[p, pl.ds((WT - 1 - a) * HEADS + h, WT, stride=HEADS), :]
                skewed = rows if skewed is None else jnp.where(lane_time == a, rows, skewed)
            skew_ref[h, p] = skewed
    for h in heads:
        for d in range(row_span):
            one, two = skew_ref[h, d], skew_ref[h, max(d - 1, 0)]
            for c in range(WW):
                shift = WT * (WW - 1 - c)
                bias_ref[h, d * WW + c] = jnp.where(
                    first,
                    one if shift == 0 else pltpu.roll(one, 128 - shift, 1),
                    pltpu.roll(two, 64 - shift, 1),
                )


def gelu_parts(pre_act):
    bell = jnp.exp2((-0.5 * LOG2E) * pre_act * pre_act)
    step = 1.0 / (1.0 + ERF_STEP * jnp.abs(pre_act))
    tail = ERF_TERMS[4]
    for term in ERF_TERMS[3::-1]:
        tail = tail * step + term
    tail = tail * step * (0.5 * bell)
    share = jnp.where(pre_act < 0.0, tail, 1.0 - tail)
    return pre_act * share, share + pre_act * (INV_ROOT_TAU * bell)


def region_classes(row, col, time):
    window_time, window_row, window_col = window_position()
    last_time = window_time == TM - 1
    last_row = window_row == TROWS - 1
    last_col = window_col == TCOLS - 1
    return (
        jnp.where(time >= ST, jnp.where(last_time, 4, 0), 0)
        + jnp.where(row >= WH - SH, jnp.where(last_row, 2, 0), 0)
        + jnp.where(col >= WW - SW, jnp.where(last_col, 1, 0), 0)
    )


def pad_keys(values):
    blocks = values.reshape(WH, WW, WT, CHAN)
    blocks = jnp.concatenate([blocks, jnp.zeros((WH, 1, WT, CHAN), values.dtype)], axis=1)
    blocks = jnp.concatenate([blocks, jnp.zeros((1, 8, WT, CHAN), values.dtype)], axis=0)
    return blocks.reshape(KEYS, CHAN)


def unpad_keys(values):
    return values.reshape(8, 8, WT, CHAN)[:WH, :WW].reshape(TOK, CHAN)


OPERANDS = (
    "table",
    "gain1",
    "shift1",
    "qkv_weight",
    "qkv_bias",
    "proj_weight",
    "proj_bias",
    "gain2",
    "shift2",
    "fc1_weight",
    "fc1_bias",
    "fc2_weight",
    "fc2_bias",
)


def kernel(*refs):
    count = len(OPERANDS)
    clip_ref, goal_ref, *sources = refs[: count + 2]
    out_ref = refs[count + 2]
    held = refs[count + 3 : 2 * count + 3]
    (
        load_sems,
        clip_in,
        goal_in,
        back_out,
        clip_relay,
        goal_relay,
        slab_ref,
        spread_ref,
        skew_ref,
        bias_ref,
        scores_ref,
        probs_ref,
        grads_ref,
        queries_ref,
        classes_ref,
        keys_ref,
        barred_ref,
        values_ref,
        mixed_ref,
        mixed_grad_ref,
        toward_ref,
        grad_queries_ref,
        send_sems,
        recv_sems,
        local_sems,
        relay_sems,
        onward_sems,
    ) = refs[2 * count + 3 :]

    loads = {}

    def load(i):
        name = OPERANDS[i]
        loads[name] = (pltpu.make_async_copy(sources[i], held[i], load_sems.at[i]), held[i])
        loads[name][0].start()

    time_pos, row_pos, col_pos = position()
    barrier = pltpu.get_barrier_semaphore()

    def greet(cut):
        pl.semaphore_signal(barrier, inc=1, device_id=sender(cut), device_id_type=MESH)

    for cut in CUTS:
        where_it_lies(cut, nothing, lambda cut=cut: greet(cut))

    @pl.when(time_pos == RELAY)
    def _():
        for ec in range(2):
            first_block = device(0, row_pos, (gathered(col_pos) + ec) % TCOLS)
            pl.semaphore_signal(barrier, inc=1, device_id=first_block, device_id_type=MESH)

    sems = [
        (send_sems.at[k], recv_sems.at[k], local_sems.at[k], relay_sems.at[k], onward_sems.at[k])
        for k in range(2)
    ]
    clip = Exchange(clip_ref, clip_in, sems[0], True, clip_relay)
    goal = Exchange(goal_ref, goal_in, sems[1], True, goal_relay)
    back_sems = (send_sems.at[2], recv_sems.at[2], local_sems.at[2])
    back = Exchange(back_out, out_ref, back_sems, False)
    for i in range(count):
        load(i)

    def operand(name):
        copy, ref = loads[name]
        copy.wait()
        return ref[...]

    targets = len(CUTS)
    for cut in IN_PLACE:
        targets = targets - jnp.where(stays(cut), 1, 0)
    targets = targets + jnp.where(time_pos == RELAY, len(IN_TIME), 0)
    targets = targets - jnp.where(time_pos == 0, len(IN_TIME) - 2, 0)
    pl.semaphore_wait(barrier, targets)
    clip.pass_on()
    clip.start(CUTS)
    spread_bias(operand("table"), slab_ref, spread_ref)
    fill_bias((0, 1), spread_ref, skew_ref, bias_ref)
    clip.wait_sent()
    goal.start(CUTS)
    fill_bias((2, 3), spread_ref, skew_ref, bias_ref)
    goal.pass_on()

    lane = iota((1, CHAN), 1)
    spot = lane % HEAD
    head_masks = [lane // HEAD == h for h in range(HEADS)]
    head_lanes = [mask.astype(F32).astype(BF16) for mask in head_masks]
    token = iota((TOK, 1), 0)
    query_class = region_classes(token // (WW * WT), token % (WW * WT) // WT, token % WT)
    classes_ref[...] = jnp.where(query_class == spot, 1.0, 0.0).astype(BF16)
    key = iota((KEYS, 1), 0)
    key_row, key_col = key // 64, key % 64 // WT
    key_class = region_classes(key_row, key_col, key % WT)
    key_class = jnp.where((key_row < WH) & (key_col < WW), key_class, 8)
    barred_ref[...] = jnp.where((key_class != spot) & (spot < 8), MASKED, 0.0).astype(BF16)

    gain1 = operand("gain1")
    shift1 = operand("shift1")
    qkv_weight = operand("qkv_weight")
    qkv_bias = operand("qkv_bias")
    query_weight_across = qkv_weight[:, :CHAN].T
    query_bias_across = jnp.broadcast_to(qkv_bias[0:1], (CHAN, CHAN)).T[:, 0:1]
    proj_weight = operand("proj_weight")
    proj_bias = operand("proj_bias")
    gain2 = operand("gain2")
    shift2 = operand("shift2")
    fc1_weight = operand("fc1_weight")
    fc1_bias = operand("fc1_bias")
    fc2_weight = operand("fc2_weight")
    fc2_bias = operand("fc2_bias")
    clip.wait_received()
    frames = joined(clip_in[...])
    normal1, inv_std1 = norm_stats(frames)
    normed1 = (normal1 * gain1 + shift1).astype(BF16)
    projected = jnp.concatenate([dot(normed1[part], qkv_weight) for part in HALVES], axis=0)
    queries_ref[...] = ((projected[:, :CHAN] + qkv_bias[0:1]) * (SCALE * LOG2E)).astype(BF16)
    keys_ref[...] = pad_keys(projected[:, CHAN : 2 * CHAN] + qkv_bias[1:2]).astype(BF16)
    values_ref[...] = pad_keys(projected[:, 2 * CHAN :] + qkv_bias[2:3]).astype(BF16)

    def score(h):
        mine, spare = head_lanes[h], head_lanes[(h + 1) % HEADS]
        head_queries = queries_ref[...] * mine + classes_ref[...] * spare
        head_keys = keys_ref[...] * mine + barred_ref[...] * spare
        scores_ref[h, 0:TOK, :] = dot(head_queries, head_keys, NT)

    def weigh(h):
        for chunk in range(ROWS // CHUNK):
            span = pl.ds(chunk * CHUNK, CHUNK)
            bias = [
                bias_ref[h, pl.ds(chunk * TILES + 42 - 14 * m, TILES)].reshape(CHUNK, 128)
                for m in range(4)
            ]
            scores = scores_ref[h, span, :] + jnp.concatenate(bias, axis=1)
            exponent = jnp.exp2(scores - jnp.max(scores, -1, keepdims=True))
            probs_ref[h, span, :] = exponent.astype(BF16)

    def mix(h):
        ones = jnp.broadcast_to(head_lanes[h], (KEYS, CHAN))
        sides = jnp.concatenate([values_ref[...] * head_lanes[h], ones], axis=1)
        part = dot(probs_ref[h, 0:TOK, :], sides)
        mixed_ref[...] = part if h == 0 else mixed_ref[...] + part

    score(0)
    for h in range(HEADS):
        if h + 1 < HEADS:
            score(h + 1)
        if h > 0:
            mix(h - 1)
        weigh(h)
    queries_across = dot(query_weight_across, normed1, NT) + query_bias_across
    queries_across = (queries_across * SCALE).astype(BF16)
    mix(HEADS - 1)

    inv_total = 1.0 / mixed_ref[:, CHAN:]
    mixed = mixed_ref[:, :CHAN] * inv_total
    mixed_low = mixed.astype(BF16)
    branch = [(dot(mixed_low[part], proj_weight) + proj_bias).astype(BF16) for part in QUARTERS]
    ys = [frames[part] + branch[i].astype(F32) for i, part in enumerate(QUARTERS)]
    stats2 = [norm_stats(y) for y in ys]
    for i, part in enumerate(QUARTERS):
        normed2 = (stats2[i][0] * gain2 + shift2).astype(BF16)
        scores_ref[0, part, :] = dot(normed2, fc1_weight) + fc1_bias
    inv_total_across = inv_total.T
    outputs = []
    for i, part in enumerate(QUARTERS):
        active, slope = gelu_parts(scores_ref[0, part, :])
        scores_ref[1, part, :] = slope
        outputs.append(ys[i] + dot(active.astype(BF16), fc2_weight) + fc2_bias)
    goal.wait_received()
    wanted = joined(goal_in[...])
    grad_out = [outputs[i] - wanted[part] for i, part in enumerate(QUARTERS)]
    grad_pre = [
        (dot(grad_out[i].astype(BF16), fc2_weight, NT) * scores_ref[1, part, :]).astype(BF16)
        for i, part in enumerate(QUARTERS)
    ]
    grad_norm2 = [dot(grad, fc1_weight, NT) for grad in grad_pre]
    grad_ys = jnp.concatenate(
        [grad_out[i] + norm_backward(grad_norm2[i], *stats2[i], gain2) for i in range(4)], axis=0
    )

    grad_low = grad_ys.astype(BF16)
    grad_mixed = (dot(grad_low, proj_weight, NT) * inv_total).astype(BF16)
    grad_mixed_across = (dot(proj_weight, grad_low, NT) * inv_total_across).astype(BF16)
    mixed_grad_ref[...] = grad_mixed
    toward_ref[0:TOK, :] = grad_mixed.astype(F32) * mixed

    def score_grad(h):
        scores_ref[h, 0:TOK, :] = dot(mixed_grad_ref[...] * head_lanes[h], values_ref[...], NT)

    def weigh_grad(h):
        for chunk in range(ROWS // CHUNK):
            span = pl.ds(chunk * CHUNK, CHUNK)
            own = jnp.where(head_masks[h], toward_ref[span, :], 0.0)
            delta = jnp.sum(own, -1, keepdims=True)
            excess = (scores_ref[h, span, :] - delta).astype(BF16)
            grads_ref[h, span, :] = probs_ref[h, span, :] * excess

    def value_grad(h):
        rows = slice(h * HEAD, (h + 1) * HEAD)
        return dot(grad_mixed_across[rows], probs_ref[h, 0:TOK, :]).astype(BF16)

    def key_grad(h):
        rows = slice(h * HEAD, (h + 1) * HEAD)
        return dot(queries_across[rows], grads_ref[h, 0:TOK, :]).astype(BF16)

    def query_grad(h):
        part = dot(grads_ref[h, 0:TOK, :], keys_ref[...] * head_lanes[h])
        grad_queries_ref[...] = part if h == 0 else grad_queries_ref[...] + part

    grad_values = [None] * HEADS
    grad_keys = [None] * HEADS
    score_grad(0)
    for h in range(HEADS):
        if h + 1 < HEADS:
            score_grad(h + 1)
        grad_values[h] = value_grad(h)
        if h > 0:
            query_grad(h - 1)
            grad_keys[h - 1] = key_grad(h - 1)
        weigh_grad(h)
    grad_keys[HEADS - 1] = key_grad(HEADS - 1)
    query_grad(HEADS - 1)

    across = jnp.concatenate(grad_keys + grad_values, axis=0)
    grad_normed = unpad_keys(dot(qkv_weight[:, CHAN:], across).T)
    grad_queries = (grad_queries_ref[...] * SCALE).astype(BF16)
    for group, rows in enumerate((range(0, WH - SH), range(WH - SH, WH))):
        part = slice(rows.start * WW * WT, rows.stop * WW * WT)
        total = grad_normed[part] + dot(grad_queries[part], qkv_weight[:, :CHAN], NT)
        total = total.astype(BF16).astype(F32)
        result = grad_ys[part] + norm_backward(total, normal1[part], inv_std1[part], gain1)
        result = result.reshape(len(rows), WW, WT, CHAN)
        back_out[rows.start : rows.stop, :, 0] = result[:, :, :ST].astype(BF16)
        back_out[rows.start : rows.stop, :, 1] = result[:, :, ST:].astype(BF16)
        back.start([cut for cut in CUTS if cut[1] == group])
    back.wait_received()
    goal.wait_sent()
    clip.wait_passed_on()
    goal.wait_passed_on()
    back.wait_sent()


def shards(
    clip_tokens,
    target,
    norm1_gain,
    norm1_bias,
    qkv_weight,
    qkv_bias,
    bias_table,
    proj_weight,
    proj_bias,
    norm2_gain,
    norm2_bias,
    fc1_weight,
    fc1_bias,
    fc2_weight,
    fc2_bias,
):
    def by_place(tokens):
        return jnp.transpose(tokens, (1, 2, 3, 0, 4)).reshape(WH, WW, 2, ST, CHAN)

    named = {
        "table": bias_table.T,
        "gain1": norm1_gain.reshape(1, -1),
        "shift1": norm1_bias.reshape(1, -1),
        "qkv_weight": qkv_weight,
        "qkv_bias": qkv_bias.reshape(3, -1),
        "proj_weight": proj_weight,
        "proj_bias": proj_bias.reshape(1, -1),
        "gain2": norm2_gain.reshape(1, -1),
        "shift2": norm2_bias.reshape(1, -1),
        "fc1_weight": fc1_weight,
        "fc1_bias": fc1_bias.reshape(1, -1),
        "fc2_weight": fc2_weight,
        "fc2_bias": fc2_bias.reshape(1, -1),
    }
    operands = [named[name] for name in OPERANDS]
    inputs = [by_place(clip_tokens), by_place(target)] + operands
    plane = (2 * WH - 1) * (2 * WW - 1)
    out = pl.pallas_call(
        kernel,
        out_shape=pltpu.VMEM((WH, WW, 2, ST, CHAN), BF16),
        in_specs=[pl.BlockSpec(memory_space=pltpu.HBM)] * len(inputs),
        out_specs=pl.BlockSpec(memory_space=pltpu.VMEM),
        scratch_shapes=[pltpu.VMEM(x.shape, x.dtype) for x in operands]
        + [pltpu.SemaphoreType.DMA((len(operands),))]
        + [pltpu.VMEM((WH, WW, 2, ST, CHAN), BF16)] * 3
        + [pltpu.VMEM((WH, WW, ST, CHAN), BF16)] * 2
        + [
            pltpu.VMEM((HEADS * 2 * WT, plane), F32),
            pltpu.VMEM((2 * WH - 1, HEADS * 2 * WT, 128), F32),
            pltpu.VMEM((HEADS, 2 * WH - 1, WT, 128), F32),
            pltpu.VMEM((HEADS, (2 * WH - 1) * WW + 1, WT, 128), F32),
            pltpu.VMEM((HEADS, ROWS, KEYS), F32),
            pltpu.VMEM((HEADS, ROWS, KEYS), BF16),
            pltpu.VMEM((HEADS, ROWS, KEYS), BF16),
            pltpu.VMEM((TOK, CHAN), BF16),
            pltpu.VMEM((TOK, CHAN), BF16),
            pltpu.VMEM((KEYS, CHAN), BF16),
            pltpu.VMEM((KEYS, CHAN), BF16),
            pltpu.VMEM((KEYS, CHAN), BF16),
            pltpu.VMEM((TOK, 2 * CHAN), F32),
            pltpu.VMEM((TOK, CHAN), BF16),
            pltpu.VMEM((ROWS, CHAN), F32),
            pltpu.VMEM((TOK, CHAN), F32),
            pltpu.SemaphoreType.DMA((3, len(CUTS))),
            pltpu.SemaphoreType.DMA((3, len(CUTS))),
            pltpu.SemaphoreType.DMA((3, len(CUTS))),
            pltpu.SemaphoreType.DMA((2, 2, 2)),
            pltpu.SemaphoreType.DMA((2, len(IN_TIME))),
        ],
        compiler_params=pltpu.CompilerParams(
            collective_id=0, has_side_effects=True, vmem_limit_bytes=40 * 1024 * 1024
        ),
        name="window_block",
    )(*[pltpu.with_memory_space_constraint(x, pltpu.HBM) for x in inputs])
    return jnp.transpose(out.reshape(1, WH, WW, WT, CHAN), (3, 0, 1, 2, 4))


def solution(mesh):
    return jax.shard_map(
        shards,
        mesh=mesh,
        in_specs=(P("tm", "tile", None, None, None),) * 2 + (P(),) * 13,
        out_specs=P("tm", "tile", None, None, None),
        check_vma=False,
    )
```

```python
import itertools

import jax
import jax.numpy as jnp
import numpy as np
from jax import lax
from jax.experimental import pallas as pl
from jax.experimental.pallas import tpu as pltpu
from jax.sharding import PartitionSpec as P

HEADS = 4
HEAD = 32
CHAN = 128
FF = 512
WT = 8
WH = 7
WW = 7
ST = 4
SH = 3
SW = 3
TCOLS = 4
TROWS = 4
TM = 16
TOK = WT * WH * WW
KEYS = 512
ROWS = 400
CHUNK = 80
TILES = CHUNK // WT

EPSILON = 1e-05
MASKED = -1000000000.0
INV_ROOT_TAU = 0.3989422804014327
ERF_STEP = 0.3275911 * 0.7071067811865476
ERF_TERMS = (0.254829592, -0.284496736, 1.421413741, -1.453152027, 1.061405429)
SCALE = HEAD ** (-0.5)
LOG2E = 1.4426950408889634

F32 = jnp.float32
BF16 = jnp.bfloat16
MESH = pl.DeviceIdType.MESH


CUTS = sorted(itertools.product(range(2), range(2), range(2)), reverse=True)
IN_TIME = [cut for cut in CUTS if cut[0]]
IN_PLACE = [cut for cut in CUTS if not cut[0]]
RELAY = TM // 2 - 1
HALVES = (slice(0, 192), slice(192, TOK))
QUARTERS = (slice(0, 96), slice(96, 192), slice(192, 288), slice(288, TOK))


def box(cut, rolled):
    et, er, ec = cut
    if rolled:
        rows, cols, half = (WH - SH if er else 0), (WW - SW if ec else 0), et
    else:
        rows, cols, half = (0 if er else SH), (0 if ec else SW), 1 - et
    return (pl.ds(rows, SH if er else WH - SH), pl.ds(cols, SW if ec else WW - SW), half)


def dot(a, b, dims=((1,), (0,))):
    return lax.dot_general(a, b, (dims, ((), ())), preferred_element_type=F32)


NT = ((1,), (1,))


def row_mean(values):
    return jnp.sum(values, -1, keepdims=True) * (1.0 / CHAN)


def norm_stats(values):
    center = values - row_mean(values)
    inv_std = lax.rsqrt(row_mean(center * center) + EPSILON)
    return center * inv_std, inv_std


def norm_backward(grad_out, normal, inv_std, gain):
    scaled = grad_out * gain
    return inv_std * (scaled - row_mean(scaled) - normal * row_mean(scaled * normal))


def iota(shape, dim):
    return lax.broadcasted_iota(jnp.int32, shape, dim)


def position():
    tile_pos = lax.axis_index("tile")
    return lax.axis_index("tm"), tile_pos // TCOLS, tile_pos % TCOLS


def crosses(time):
    return time % (TM // 2) == TM // 2 - 1


def spread_out(window):
    return jnp.where(window == 0, 0, jnp.where(window == 3, 1, window + 1))


def gathered(place):
    return jnp.where(place == 0, 0, jnp.where(place == 1, 3, place - 1))


def row_place(time, window):
    return jnp.where(crosses(time), (window + TROWS // 2) % TROWS, spread_out(window))


def window_position():
    time, row, col = position()
    window_row = jnp.where(crosses(time), (row + TROWS // 2) % TROWS, gathered(row))
    return time, window_row, gathered(col)


def device(time, row, col):
    return {"tm": time, "tile": row * TCOLS + col}


def target(cut):
    time, row, col = position()
    time = (time + TM - cut[0]) % TM
    row = row_place(time, (row + TROWS - cut[1]) % TROWS)
    return device(time, row, spread_out((col + TCOLS - cut[2]) % TCOLS))


def source(cut):
    time, row, col = window_position()
    return device((time + cut[0]) % TM, (row + cut[1]) % TROWS, (col + cut[2]) % TCOLS)


def stays(cut):
    return source(cut)["tile"] == lax.axis_index("tile")


def where_it_lies(cut, local, remote):
    if cut[0]:
        remote()
    else:
        pl.when(stays(cut))(local)
        pl.when(jnp.logical_not(stays(cut)))(remote)


def nothing():
    pass


def sender(cut):
    where = source(cut)
    if cut[0]:
        time, _, col = position()
        relay = device(RELAY, where["tile"] // TCOLS, col)
        where = {axis: jnp.where(time == TM - 1, relay[axis], where[axis]) for axis in where}
    return where


class Exchange:
    def __init__(self, src, dst, sems, to_window, relay=None):
        send_sems, recv_sems, local_sems = sems[:3]
        self.time, row, col = position()
        self.remote = {
            cut: pltpu.make_async_remote_copy(
                src_ref=src.at[box(cut, not to_window)],
                dst_ref=dst.at[box(cut, to_window)],
                send_sem=send_sems.at[i],
                recv_sem=recv_sems.at[i],
                device_id=target(cut) if to_window else source(cut),
                device_id_type=MESH,
            )
            for i, cut in enumerate(CUTS)
        }
        self.local = {
            cut: pltpu.make_async_copy(
                src.at[box(cut, not to_window)], dst.at[box(cut, to_window)], local_sems.at[i]
            )
            for i, cut in enumerate(CUTS)
            if not cut[0]
        }
        self.relayed = to_window
        if not to_window:
            return
        relay_sems, onward_sems = sems[3:]
        self.hand_over = [
            pltpu.make_async_remote_copy(
                src_ref=src.at[:, box((1, 0, ec), False)[1], 0],
                dst_ref=relay.at[:, box((1, 0, ec), True)[1]],
                send_sem=relay_sems.at[0, ec],
                recv_sem=relay_sems.at[1, ec],
                device_id=device(RELAY, row, spread_out((col + TCOLS - ec) % TCOLS)),
                device_id_type=MESH,
            )
            for ec in range(2)
        ]
        self.onward = [
            pltpu.make_async_remote_copy(
                src_ref=relay.at[box(cut, False)[0], box(cut, True)[1]],
                dst_ref=dst.at[box(cut, True)],
                send_sem=onward_sems.at[i],
                recv_sem=recv_sems.at[CUTS.index(cut)],
                device_id=device(TM - 1, row_place(TM - 1, (row + TROWS - cut[1]) % TROWS), col),
                device_id_type=MESH,
            )
            for i, cut in enumerate(IN_TIME)
        ]

    def over_time(self, act):
        if not self.relayed:
            for cut in IN_TIME:
                act(self.remote[cut])
            return

        @pl.when(self.time == 0)
        def _():
            for copy in self.hand_over:
                act(copy)

        @pl.when(self.time != 0)
        def _():
            for cut in IN_TIME:
                act(self.remote[cut])

    def start(self, cuts):
        if self.relayed:
            self.over_time(lambda copy: copy.start())
            cuts = [cut for cut in cuts if not cut[0]]
        for cut in cuts:
            if cut[0]:
                self.remote[cut].start()
            else:
                where_it_lies(cut, self.local[cut].start, self.remote[cut].start)

    def pass_on(self):
        @pl.when(self.time == RELAY)
        def _():
            for copy in self.hand_over:
                copy.wait_recv()
            for copy in self.onward:
                copy.start()

    def wait_passed_on(self):
        @pl.when(self.time == RELAY)
        def _():
            for copy in self.onward:
                copy.wait_send()

    def wait_sent(self):
        self.over_time(lambda copy: copy.wait_send())
        for cut in IN_PLACE:
            where_it_lies(cut, nothing, self.remote[cut].wait_send)

    def wait_received(self):
        for cut in IN_TIME:
            self.remote[cut].wait_recv()
        for cut in IN_PLACE:
            where_it_lies(cut, self.local[cut].wait, self.remote[cut].wait_recv)


def joined(halves):
    halves = halves.astype(F32).reshape(WH * WW, 2, ST, CHAN)
    return jnp.concatenate([halves[:, 0], halves[:, 1]], axis=1).reshape(TOK, CHAN)


def spread_bias(table, slab_ref, spread_ref):
    time_span, row_span, col_span = 2 * WT - 1, 2 * WH - 1, 2 * WW - 1
    plane = row_span * col_span
    slab_ref[HEADS * time_span :, :] = jnp.zeros((HEADS, plane), F32)
    for d in range(time_span):
        slab_ref[HEADS * d : HEADS * (d + 1), :] = table[:, d * plane : (d + 1) * plane]
    slabs = slab_ref[...] * LOG2E
    high = slabs.astype(BF16)
    rest = slabs - high.astype(F32)
    middle = rest.astype(BF16)
    low = (rest - middle.astype(F32)).astype(BF16)
    lanes = iota((1, row_span * 128), 1)
    slot = lanes % 128 // WT
    wanted = jnp.where(slot < col_span, lanes // 128 * col_span + (col_span - 1) - slot, -1)
    pick = (iota((plane, row_span * 128), 0) == wanted).astype(F32).astype(BF16)
    spread = dot(jnp.concatenate([low, middle, high], axis=0), pick)
    count = slabs.shape[0]
    spread = (spread[:count] + spread[count : 2 * count]) + spread[2 * count :]
    for p in range(row_span):
        spread_ref[p] = spread[:, p * 128 : (p + 1) * 128]


def fill_bias(heads, spread_ref, skew_ref, bias_ref):
    row_span = 2 * WH - 1
    lane_time = iota((WT, 128), 1) % WT
    first = iota((WT, 128), 1) < 64

    for h in heads:
        for p in range(row_span):
            skewed = None
            for a in range(WT):
                rows = spread_ref[p, pl.ds((WT - 1 - a) * HEADS + h, WT, stride=HEADS), :]
                skewed = rows if skewed is None else jnp.where(lane_time == a, rows, skewed)
            skew_ref[h, p] = skewed
    for h in heads:
        for d in range(row_span):
            one, two = skew_ref[h, d], skew_ref[h, max(d - 1, 0)]
            for c in range(WW):
                shift = WT * (WW - 1 - c)
                bias_ref[h, d * WW + c] = jnp.where(
                    first,
                    one if shift == 0 else pltpu.roll(one, 128 - shift, 1),
                    pltpu.roll(two, 64 - shift, 1),
                )


def gelu_parts(pre_act):
    bell = jnp.exp2((-0.5 * LOG2E) * pre_act * pre_act)
    step = 1.0 / (1.0 + ERF_STEP * jnp.abs(pre_act))
    tail = ERF_TERMS[4]
    for term in ERF_TERMS[3::-1]:
        tail = tail * step + term
    tail = tail * step * (0.5 * bell)
    share = jnp.where(pre_act < 0.0, tail, 1.0 - tail)
    return pre_act * share, share + pre_act * (INV_ROOT_TAU * bell)


def region_classes(row, col, time):
    window_time, window_row, window_col = window_position()
    last_time = window_time == TM - 1
    last_row = window_row == TROWS - 1
    last_col = window_col == TCOLS - 1
    return (
        jnp.where(time >= ST, jnp.where(last_time, 4, 0), 0)
        + jnp.where(row >= WH - SH, jnp.where(last_row, 2, 0), 0)
        + jnp.where(col >= WW - SW, jnp.where(last_col, 1, 0), 0)
    )


def pad_keys(values):
    blocks = values.reshape(WH, WW, WT, CHAN)
    blocks = jnp.concatenate([blocks, jnp.zeros((WH, 1, WT, CHAN), values.dtype)], axis=1)
    blocks = jnp.concatenate([blocks, jnp.zeros((1, 8, WT, CHAN), values.dtype)], axis=0)
    return blocks.reshape(KEYS, CHAN)


def unpad_keys(values):
    return values.reshape(8, 8, WT, CHAN)[:WH, :WW].reshape(TOK, CHAN)


OPERANDS = (
    "table",
    "gain1",
    "shift1",
    "qkv_weight",
    "qkv_bias",
    "proj_weight",
    "proj_bias",
    "gain2",
    "shift2",
    "fc1_weight",
    "fc1_bias",
    "fc2_weight",
    "fc2_bias",
)


def kernel(*refs):
    count = len(OPERANDS)
    clip_ref, goal_ref, *sources = refs[: count + 2]
    out_ref = refs[count + 2]
    held = refs[count + 3 : 2 * count + 3]
    (
        load_sems,
        clip_in,
        goal_in,
        back_out,
        clip_relay,
        goal_relay,
        slab_ref,
        spread_ref,
        skew_ref,
        bias_ref,
        scores_ref,
        probs_ref,
        grads_ref,
        queries_ref,
        classes_ref,
        keys_ref,
        barred_ref,
        values_ref,
        mixed_ref,
        mixed_grad_ref,
        toward_ref,
        grad_queries_ref,
        send_sems,
        recv_sems,
        local_sems,
        relay_sems,
        onward_sems,
    ) = refs[2 * count + 3 :]

    loads = {}

    def load(i):
        name = OPERANDS[i]
        loads[name] = (pltpu.make_async_copy(sources[i], held[i], load_sems.at[i]), held[i])
        loads[name][0].start()

    time_pos, row_pos, col_pos = position()
    barrier = pltpu.get_barrier_semaphore()

    def greet(cut):
        pl.semaphore_signal(barrier, inc=1, device_id=sender(cut), device_id_type=MESH)

    for cut in CUTS:
        where_it_lies(cut, nothing, lambda cut=cut: greet(cut))

    @pl.when(time_pos == RELAY)
    def _():
        for ec in range(2):
            first_block = device(0, row_pos, (gathered(col_pos) + ec) % TCOLS)
            pl.semaphore_signal(barrier, inc=1, device_id=first_block, device_id_type=MESH)

    sems = [
        (send_sems.at[k], recv_sems.at[k], local_sems.at[k], relay_sems.at[k], onward_sems.at[k])
        for k in range(2)
    ]
    clip = Exchange(clip_ref, clip_in, sems[0], True, clip_relay)
    goal = Exchange(goal_ref, goal_in, sems[1], True, goal_relay)
    back_sems = (send_sems.at[2], recv_sems.at[2], local_sems.at[2])
    back = Exchange(back_out, out_ref, back_sems, False)
    for i in range(count):
        load(i)

    def operand(name):
        copy, ref = loads[name]
        copy.wait()
        return ref[...]

    targets = len(CUTS)
    for cut in IN_PLACE:
        targets = targets - jnp.where(stays(cut), 1, 0)
    targets = targets + jnp.where(time_pos == RELAY, len(IN_TIME), 0)
    targets = targets - jnp.where(time_pos == 0, len(IN_TIME) - 2, 0)
    pl.semaphore_wait(barrier, targets)
    clip.start(CUTS)
    clip.pass_on()
    spread_bias(operand("table"), slab_ref, spread_ref)
    fill_bias((0, 1), spread_ref, skew_ref, bias_ref)
    clip.wait_sent()
    goal.start(CUTS)
    fill_bias((2, 3), spread_ref, skew_ref, bias_ref)
    goal.pass_on()

    lane = iota((1, CHAN), 1)
    spot = lane % HEAD
    head_masks = [lane // HEAD == h for h in range(HEADS)]
    head_lanes = [mask.astype(F32).astype(BF16) for mask in head_masks]
    token = iota((TOK, 1), 0)
    query_class = region_classes(token // (WW * WT), token % (WW * WT) // WT, token % WT)
    classes_ref[...] = jnp.where(query_class == spot, 1.0, 0.0).astype(BF16)
    key = iota((KEYS, 1), 0)
    key_row, key_col = key // 64, key % 64 // WT
    key_class = region_classes(key_row, key_col, key % WT)
    key_class = jnp.where((key_row < WH) & (key_col < WW), key_class, 8)
    barred_ref[...] = jnp.where((key_class != spot) & (spot < 8), MASKED, 0.0).astype(BF16)

    gain1 = operand("gain1")
    shift1 = operand("shift1")
    qkv_weight = operand("qkv_weight")
    qkv_bias = operand("qkv_bias")
    query_weight_across = qkv_weight[:, :CHAN].T
    query_bias_across = jnp.broadcast_to(qkv_bias[0:1], (CHAN, CHAN)).T[:, 0:1]
    proj_weight = operand("proj_weight")
    proj_bias = operand("proj_bias")
    gain2 = operand("gain2")
    shift2 = operand("shift2")
    fc1_weight = operand("fc1_weight")
    fc1_bias = operand("fc1_bias")
    fc2_weight = operand("fc2_weight")
    fc2_bias = operand("fc2_bias")
    clip.wait_received()
    frames = joined(clip_in[...])
    normal1, inv_std1 = norm_stats(frames)
    normed1 = (normal1 * gain1 + shift1).astype(BF16)
    projected = jnp.concatenate([dot(normed1[part], qkv_weight) for part in HALVES], axis=0)
    queries_ref[...] = ((projected[:, :CHAN] + qkv_bias[0:1]) * (SCALE * LOG2E)).astype(BF16)
    keys_ref[...] = pad_keys(projected[:, CHAN : 2 * CHAN] + qkv_bias[1:2]).astype(BF16)
    values_ref[...] = pad_keys(projected[:, 2 * CHAN :] + qkv_bias[2:3]).astype(BF16)

    def score(h):
        mine, spare = head_lanes[h], head_lanes[(h + 1) % HEADS]
        head_queries = queries_ref[...] * mine + classes_ref[...] * spare
        head_keys = keys_ref[...] * mine + barred_ref[...] * spare
        scores_ref[h, 0:TOK, :] = dot(head_queries, head_keys, NT)

    def weigh(h):
        for chunk in range(ROWS // CHUNK):
            span = pl.ds(chunk * CHUNK, CHUNK)
            bias = [
                bias_ref[h, pl.ds(chunk * TILES + 42 - 14 * m, TILES)].reshape(CHUNK, 128)
                for m in range(4)
            ]
            scores = scores_ref[h, span, :] + jnp.concatenate(bias, axis=1)
            exponent = jnp.exp2(scores - jnp.max(scores, -1, keepdims=True))
            probs_ref[h, span, :] = exponent.astype(BF16)

    def mix(h):
        ones = jnp.broadcast_to(head_lanes[h], (KEYS, CHAN))
        sides = jnp.concatenate([values_ref[...] * head_lanes[h], ones], axis=1)
        part = dot(probs_ref[h, 0:TOK, :], sides)
        mixed_ref[...] = part if h == 0 else mixed_ref[...] + part

    score(0)
    for h in range(HEADS):
        if h + 1 < HEADS:
            score(h + 1)
        if h > 0:
            mix(h - 1)
        weigh(h)
    queries_across = dot(query_weight_across, normed1, NT) + query_bias_across
    queries_across = (queries_across * SCALE).astype(BF16)
    mix(HEADS - 1)

    inv_total = 1.0 / mixed_ref[:, CHAN:]
    mixed = mixed_ref[:, :CHAN] * inv_total
    mixed_low = mixed.astype(BF16)
    branch = [(dot(mixed_low[part], proj_weight) + proj_bias).astype(BF16) for part in QUARTERS]
    ys = [frames[part] + branch[i].astype(F32) for i, part in enumerate(QUARTERS)]
    stats2 = [norm_stats(y) for y in ys]
    for i, part in enumerate(QUARTERS):
        normed2 = (stats2[i][0] * gain2 + shift2).astype(BF16)
        scores_ref[0, part, :] = dot(normed2, fc1_weight) + fc1_bias
    inv_total_across = inv_total.T
    outputs = []
    for i, part in enumerate(QUARTERS):
        active, slope = gelu_parts(scores_ref[0, part, :])
        scores_ref[1, part, :] = slope
        outputs.append(ys[i] + dot(active.astype(BF16), fc2_weight) + fc2_bias)
    goal.wait_received()
    wanted = joined(goal_in[...])
    grad_out = [outputs[i] - wanted[part] for i, part in enumerate(QUARTERS)]
    grad_pre = [
        (dot(grad_out[i].astype(BF16), fc2_weight, NT) * scores_ref[1, part, :]).astype(BF16)
        for i, part in enumerate(QUARTERS)
    ]
    grad_norm2 = [dot(grad, fc1_weight, NT) for grad in grad_pre]
    grad_ys = jnp.concatenate(
        [grad_out[i] + norm_backward(grad_norm2[i], *stats2[i], gain2) for i in range(4)], axis=0
    )

    grad_low = grad_ys.astype(BF16)
    grad_mixed = (dot(grad_low, proj_weight, NT) * inv_total).astype(BF16)
    grad_mixed_across = (dot(proj_weight, grad_low, NT) * inv_total_across).astype(BF16)
    mixed_grad_ref[...] = grad_mixed
    toward_ref[0:TOK, :] = grad_mixed.astype(F32) * mixed

    def score_grad(h):
        scores_ref[h, 0:TOK, :] = dot(mixed_grad_ref[...] * head_lanes[h], values_ref[...], NT)

    def weigh_grad(h):
        for chunk in range(ROWS // CHUNK):
            span = pl.ds(chunk * CHUNK, CHUNK)
            own = jnp.where(head_masks[h], toward_ref[span, :], 0.0)
            delta = jnp.sum(own, -1, keepdims=True)
            excess = (scores_ref[h, span, :] - delta).astype(BF16)
            grads_ref[h, span, :] = probs_ref[h, span, :] * excess

    def value_grad(h):
        rows = slice(h * HEAD, (h + 1) * HEAD)
        return dot(grad_mixed_across[rows], probs_ref[h, 0:TOK, :]).astype(BF16)

    def key_grad(h):
        rows = slice(h * HEAD, (h + 1) * HEAD)
        return dot(queries_across[rows], grads_ref[h, 0:TOK, :]).astype(BF16)

    def query_grad(h):
        part = dot(grads_ref[h, 0:TOK, :], keys_ref[...] * head_lanes[h])
        grad_queries_ref[...] = part if h == 0 else grad_queries_ref[...] + part

    grad_values = [None] * HEADS
    grad_keys = [None] * HEADS
    score_grad(0)
    for h in range(HEADS):
        if h + 1 < HEADS:
            score_grad(h + 1)
        grad_values[h] = value_grad(h)
        if h > 0:
            query_grad(h - 1)
            grad_keys[h - 1] = key_grad(h - 1)
        weigh_grad(h)
    grad_keys[HEADS - 1] = key_grad(HEADS - 1)
    query_grad(HEADS - 1)

    across = jnp.concatenate(grad_keys + grad_values, axis=0)
    grad_normed = unpad_keys(dot(qkv_weight[:, CHAN:], across).T)
    grad_queries = (grad_queries_ref[...] * SCALE).astype(BF16)
    for group, rows in enumerate((range(0, WH - SH), range(WH - SH, WH))):
        part = slice(rows.start * WW * WT, rows.stop * WW * WT)
        total = grad_normed[part] + dot(grad_queries[part], qkv_weight[:, :CHAN], NT)
        total = total.astype(BF16).astype(F32)
        result = grad_ys[part] + norm_backward(total, normal1[part], inv_std1[part], gain1)
        result = result.reshape(len(rows), WW, WT, CHAN)
        back_out[rows.start : rows.stop, :, 0] = result[:, :, :ST].astype(BF16)
        back_out[rows.start : rows.stop, :, 1] = result[:, :, ST:].astype(BF16)
        back.start([cut for cut in CUTS if cut[1] == group])
    back.wait_received()
    goal.wait_sent()
    clip.wait_passed_on()
    goal.wait_passed_on()
    back.wait_sent()


def shards(
    clip_tokens,
    target,
    norm1_gain,
    norm1_bias,
    qkv_weight,
    qkv_bias,
    bias_table,
    proj_weight,
    proj_bias,
    norm2_gain,
    norm2_bias,
    fc1_weight,
    fc1_bias,
    fc2_weight,
    fc2_bias,
):
    def by_place(tokens):
        return jnp.transpose(tokens, (1, 2, 3, 0, 4)).reshape(WH, WW, 2, ST, CHAN)

    named = {
        "table": bias_table.T,
        "gain1": norm1_gain.reshape(1, -1),
        "shift1": norm1_bias.reshape(1, -1),
        "qkv_weight": qkv_weight,
        "qkv_bias": qkv_bias.reshape(3, -1),
        "proj_weight": proj_weight,
        "proj_bias": proj_bias.reshape(1, -1),
        "gain2": norm2_gain.reshape(1, -1),
        "shift2": norm2_bias.reshape(1, -1),
        "fc1_weight": fc1_weight,
        "fc1_bias": fc1_bias.reshape(1, -1),
        "fc2_weight": fc2_weight,
        "fc2_bias": fc2_bias.reshape(1, -1),
    }
    operands = [named[name] for name in OPERANDS]
    inputs = [by_place(clip_tokens), by_place(target)] + operands
    plane = (2 * WH - 1) * (2 * WW - 1)
    out = pl.pallas_call(
        kernel,
        out_shape=pltpu.VMEM((WH, WW, 2, ST, CHAN), BF16),
        in_specs=[pl.BlockSpec(memory_space=pltpu.HBM)] * len(inputs),
        out_specs=pl.BlockSpec(memory_space=pltpu.VMEM),
        scratch_shapes=[pltpu.VMEM(x.shape, x.dtype) for x in operands]
        + [pltpu.SemaphoreType.DMA((len(operands),))]
        + [pltpu.VMEM((WH, WW, 2, ST, CHAN), BF16)] * 3
        + [pltpu.VMEM((WH, WW, ST, CHAN), BF16)] * 2
        + [
            pltpu.VMEM((HEADS * 2 * WT, plane), F32),
            pltpu.VMEM((2 * WH - 1, HEADS * 2 * WT, 128), F32),
            pltpu.VMEM((HEADS, 2 * WH - 1, WT, 128), F32),
            pltpu.VMEM((HEADS, (2 * WH - 1) * WW + 1, WT, 128), F32),
            pltpu.VMEM((HEADS, ROWS, KEYS), F32),
            pltpu.VMEM((HEADS, ROWS, KEYS), BF16),
            pltpu.VMEM((HEADS, ROWS, KEYS), BF16),
            pltpu.VMEM((TOK, CHAN), BF16),
            pltpu.VMEM((TOK, CHAN), BF16),
            pltpu.VMEM((KEYS, CHAN), BF16),
            pltpu.VMEM((KEYS, CHAN), BF16),
            pltpu.VMEM((KEYS, CHAN), BF16),
            pltpu.VMEM((TOK, 2 * CHAN), F32),
            pltpu.VMEM((TOK, CHAN), BF16),
            pltpu.VMEM((ROWS, CHAN), F32),
            pltpu.VMEM((TOK, CHAN), F32),
            pltpu.SemaphoreType.DMA((3, len(CUTS))),
            pltpu.SemaphoreType.DMA((3, len(CUTS))),
            pltpu.SemaphoreType.DMA((3, len(CUTS))),
            pltpu.SemaphoreType.DMA((2, 2, 2)),
            pltpu.SemaphoreType.DMA((2, len(IN_TIME))),
        ],
        compiler_params=pltpu.CompilerParams(
            collective_id=0, has_side_effects=True, vmem_limit_bytes=40 * 1024 * 1024
        ),
        name="window_block",
    )(*[pltpu.with_memory_space_constraint(x, pltpu.HBM) for x in inputs])
    return jnp.transpose(out.reshape(1, WH, WW, WT, CHAN), (3, 0, 1, 2, 4))


def solution(mesh):
    return jax.shard_map(
        shards,
        mesh=mesh,
        in_specs=(P("tm", "tile", None, None, None),) * 2 + (P(),) * 13,
        out_specs=P("tm", "tile", None, None, None),
        check_vma=False,
    )
```
